32 devices in a mesh: comp: 8 (over z, y), lat: 4 (over x, core).
Axes of the slice: x: 2, y: 2, z: 4, core: 2. Of those that a mesh axis runs over, the one named last changes fastest.
Arguments:
- spectrum: float32 [32, 36, 384, 512], P('comp', None, 'lat'), may hold values from 0.1 to 3
- sea_mask: int32 [384, 512], P('lat'), may hold values from 0 to 1, as said below
- point_index: int32 [4, 32768], P('lat'), may hold values from 0 to 49151, as said below
- band_counts: int32 [4], P('lat'), may hold values from 16384 to 32768, as said below
- sub_counts: int32 [32], P('comp'), may hold values from 2 to 4, as said below
- mix_in: bfloat16 [1152, 1152], replicated, may hold values from -0.1875 to 0.1875
- mix_out: bfloat16 [1152, 1152], replicated, may hold values from -0.1875 to 0.1875
- growth: float32 [32, 36], replicated, may hold values from 0.05 to 1
- damping: float32 [32, 36], replicated, may hold values from 0.1 to 2
Outputs:
- new_spectrum: float32 [32, 36, 384, 512], P('comp', None, 'lat')
The draws below stay inside these ranges and needn't reach their ends.
Inputs may be any that keep to these rules, and one draw needn't show every extreme that they name: `sea_mask`: exactly band_counts[b] of the 49152 cells of band b are sea. `point_index`: row b lists the sea cells of band b in increasing order in its first band_counts[b] slots, zeros after them. `band_counts`: some band has exactly 32768 sea cells. `sub_counts`: some frequency has exactly 4 substeps.
All inputs are finite; a program needn't handle non-finite values.
Results may differ from the reference program's by a relative error of at most 0.0015.
Values may be sent and summed in bfloat16 or wider, within the bound.
No kernel may reach another device: no remote copies, remote signals or barrier semaphores. Data moves between devices by JAX's collectives and lax.ppermute only.
A program may use at most 192 MiB of HBM per device.

```python
import math
import jax
import jax.numpy as jnp
from jax import lax

NDIR = 36
NFREQ = 32
ROWS = 96
LON = 512
NSUB = 4
K = 1152
BANDS = 4
NY = 384
PCAP = 32768


def sea_layout(key):
    base_key = jax.random.fold_in(key, 7)
    subkeys = jax.random.split(base_key, 4)
    counts = jax.random.randint(subkeys[0], (BANDS,), PCAP // 2, PCAP + 1)
    top_band = jax.random.randint(subkeys[1], (), 0, BANDS)
    counts = jnp.where(jnp.arange(BANDS) == top_band, PCAP, counts)
    coarse = jax.random.randint(subkeys[2], (BANDS, (ROWS + 7) // 8, (LON + 7) // 8), 0, 16)
    coarse = jnp.repeat(jnp.repeat(coarse, 8, axis=1), 8, axis=2)[:, :ROWS, :LON]
    fine_level = jax.random.randint(subkeys[3], (BANDS, ROWS, LON), 0, 64)
    cell_count = ROWS * LON
    cell_ids = jnp.arange(cell_count, dtype=jnp.int32)
    scores = ((coarse * 64 + fine_level) * cell_count).reshape(BANDS, cell_count) + cell_ids[None, :]
    cell_rank = jnp.argsort(jnp.argsort(scores, axis=1), axis=1)
    sea_cells = cell_rank < counts[:, None]
    order_key = jnp.where(sea_cells, cell_ids[None, :], cell_count + cell_ids[None, :])
    listed = jnp.argsort(order_key, axis=1)[:, :PCAP]
    listed = jnp.where(jnp.arange(PCAP)[None, :] < counts[:, None], listed, 0)
    return (sea_cells.astype(jnp.int32), listed.astype(jnp.int32), counts.astype(jnp.int32))


def draw_sea_mask(key, part):
    return sea_layout(key)[0].reshape(BANDS * ROWS, LON)


def draw_point_index(key, part):
    return sea_layout(key)[1]


def draw_band_counts(key, part):
    return sea_layout(key)[2]


def draw_sub_counts(key, part):
    base_key = jax.random.fold_in(key, 13)
    subkeys = jax.random.split(base_key, 2)
    steps_drawn = jax.random.randint(subkeys[0], (NFREQ,), 2, NSUB + 1)
    top_freq = jax.random.randint(subkeys[1], (), 0, NFREQ)
    return jnp.where(jnp.arange(NFREQ) == top_freq, NSUB, steps_drawn).astype(jnp.int32)


def levels(stream_key, shape, shards, least, high):
    gain = 1.0
    for axis_at, parts in shards:
        draws = jax.random.uniform(jax.random.fold_in(jax.random.fold_in(stream_key, 6), axis_at), (parts,), jnp.float32, least / len(shards), high / len(shards))
        gain = gain * jnp.repeat(jnp.exp(draws), shape[axis_at] // parts).reshape((-1,) + (1,) * (len(shape) - 1 - axis_at))
    return gain


def noise(rng, extent, deviation, bound, kind=jnp.bfloat16):
    array = jax.random.normal(rng, extent, jnp.float32) * deviation
    return jnp.minimum(jnp.maximum(array, -bound), bound).astype(kind)


def setup_inputs(seed: int = 0) -> dict:
    key_of = jax.random.split(jax.random.key(seed), 10)
    return {
        "spectrum": jnp.clip(jnp.exp(math.log(3.0) - 3.4011974 * jax.random.uniform(key_of[0], (NFREQ, NDIR, NY, LON), jnp.float32) ** levels(key_of[0], (NFREQ, NDIR, NY, LON), ((0, 8), (2, 4)), -0.2, 0.2)), 0.1, 3.0),
        "sea_mask": draw_sea_mask(jax.random.fold_in(key_of[9], 71), 0),
        "point_index": draw_point_index(jax.random.fold_in(key_of[9], 71), 0),
        "band_counts": draw_band_counts(jax.random.fold_in(key_of[9], 71), 0),
        "sub_counts": draw_sub_counts(jax.random.fold_in(key_of[9], 71), 0),
        "mix_in": noise(key_of[5], (K, K), K ** -0.5, 0.1875),
        "mix_out": noise(key_of[6], (K, K), K ** -0.5, 0.1875),
        "growth": jnp.clip(jnp.exp(jax.random.uniform(key_of[7], (NFREQ, NDIR), jnp.float32, math.log(0.05), math.log(1.0))), 0.05, 1.0),
        "damping": jnp.clip(jnp.exp(jax.random.uniform(key_of[8], (NFREQ, NDIR), jnp.float32, math.log(0.1), math.log(2.0))), 0.1, 2.0),
    }


def next_column(values_in):
    return jnp.concatenate([values_in[..., 1:], jnp.zeros_like(values_in[..., :1])], axis=-1)


def prev_column(values_in):
    return jnp.concatenate([jnp.zeros_like(values_in[..., :1]), values_in[..., :-1]], axis=-1)


def openings(mask_rows):
    inner_mask = mask_rows[1:-1]
    open_lon = inner_mask * next_column(inner_mask)
    open_lat = mask_rows[:-1] * mask_rows[1:]
    return open_lon, open_lat


def advance(padded, open_lon, open_lat, courant_x, courant_y):
    inner_rows = padded[..., 1:-1, :]
    flux_lon = (jnp.maximum(courant_x, 0.0) * inner_rows + jnp.minimum(courant_x, 0.0) * next_column(inner_rows)) * open_lon
    flux_lat = (jnp.maximum(courant_y, 0.0) * padded[..., :-1, :] + jnp.minimum(courant_y, 0.0) * padded[..., 1:, :]) * open_lat
    return inner_rows - flux_lon + prev_column(flux_lon) - flux_lat[..., 1:, :] + flux_lat[..., :-1, :]


def courant(freq_index, sub_steps, substep, dir_count):
    group_speed = 1.4 * jnp.power(0.93, freq_index.astype(jnp.float32))
    active = (sub_steps > substep).astype(jnp.float32)
    per_step = group_speed * active / sub_steps.astype(jnp.float32)
    angles = (jnp.arange(dir_count, dtype=jnp.float32) + 0.5) * (2.0 * jnp.pi / dir_count)
    return per_step[..., None] * jnp.cos(angles), per_step[..., None] * jnp.sin(angles)


def freq_weights(freq_count, dir_count):
    raw_weight = jnp.power(1.1, jnp.arange(freq_count, dtype=jnp.float32))
    raw_weight = raw_weight / (dir_count * jnp.sum(raw_weight))
    return jnp.repeat(raw_weight, dir_count)


def source_increment(points, growth_col, damping_col, mix_in, mix_out, freq_weight):
    energy = points.astype(jnp.float32)
    hidden = jnp.dot(mix_in, points, preferred_element_type=jnp.float32)
    square = (hidden * hidden).astype(jnp.bfloat16)
    transfer = jnp.dot(mix_out, square, preferred_element_type=jnp.float32)
    mean_energy = jnp.sum(freq_weight[:, None] * energy, axis=0)
    increment = 0.5 * (growth_col * energy + 0.25 * transfer - damping_col * energy * (mean_energy / (1.0 + mean_energy)))
    return increment.astype(jnp.bfloat16)


def reference(spectrum, sea_mask, point_index, band_counts, sub_counts, mix_in, mix_out, growth, damping):
    mask_float = sea_mask.astype(jnp.float32)
    mask_ext = jnp.pad(mask_float, ((1, 1), (0, 0)))
    open_lon, open_lat = openings(mask_ext)

    def propagate_freq(packed):
        wave_field, freq_index, sub_steps = packed
        wave_field = wave_field * mask_float
        for substep in range(NSUB):
            courant_x, courant_y = courant(freq_index, sub_steps, substep, NDIR)
            padded = jnp.pad(wave_field, ((0, 0), (1, 1), (0, 0)))
            wave_field = advance(padded, open_lon, open_lat, courant_x[:, None, None], courant_y[:, None, None])
        return wave_field

    propagated = lax.map(propagate_freq, (spectrum, jnp.arange(NFREQ, dtype=jnp.int32), sub_counts))
    freq_weight = freq_weights(NFREQ, NDIR)
    growth_col = growth.reshape(K, 1)
    damping_col = damping.reshape(K, 1)
    band_fields = []
    for band_index in range(BANDS):
        flat_field = propagated[:, :, band_index * ROWS:(band_index + 1) * ROWS, :].reshape(K, ROWS * LON)
        listed = point_index[band_index]
        points = jnp.take(flat_field.astype(jnp.bfloat16), listed, axis=1)
        increment = source_increment(points, growth_col, damping_col, mix_in, mix_out, freq_weight)
        in_range = (jnp.arange(PCAP) < band_counts[band_index]).astype(jnp.float32)
        flat_field = flat_field.at[:, listed].add(increment.astype(jnp.float32) * in_range[None, :])
        band_fields.append(flat_field.reshape(NFREQ, NDIR, ROWS, LON))
    return jnp.concatenate(band_fields, axis=2)
```

```python
import functools

import jax
import jax.numpy as jnp
from jax import lax
from jax.experimental import pallas as pl
from jax.experimental.pallas import tpu as pltpu
from jax.sharding import PartitionSpec as P

NSUB = 4
SUBLANES = 8
LANES = 128
HALVES = 2
VMEM_BYTES = 56 * 1024 * 1024


def chunk_sizes(comp_count):
    if comp_count % 16:
        return [comp_count]
    units = comp_count // 16
    sizes = [1]
    units -= 1
    while units > 0:
        sizes.append(min(3, units))
        units -= sizes[-1]
    return [16 * size for size in sizes]


def block_size(start, size):
    for block in range(min(16, size), 0, -1):
        if size % block == 0 and start % block == 0:
            return block
    return 1


def courant(freq_index, sub_steps, dir_count):
    group_speed = 1.4 * jnp.power(0.93, freq_index.astype(jnp.float32))
    per_step = group_speed / sub_steps.astype(jnp.float32)
    angles = (jnp.arange(dir_count, dtype=jnp.float32) + 0.5) * (2.0 * jnp.pi / dir_count)
    return (per_step[..., None] * jnp.cos(angles), per_step[..., None] * jnp.sin(angles))


def freq_weights(freq_count, dir_count):
    raw_weight = jnp.power(1.1, jnp.arange(freq_count, dtype=jnp.float32))
    raw_weight = raw_weight / (dir_count * jnp.sum(raw_weight))
    return jnp.repeat(raw_weight, dir_count)


def propagate_kernel(
    ax_ref, ay_ref, quad_ref, steps_ref,
    spec_ref, low_ref, high_ref, mask_ref,
    out_ref,
    keep, from_x, from_y, top, bottom,
):
    block = spec_ref.shape[0]
    rows, cols = spec_ref.shape[1], spec_ref.shape[2]
    halo = low_ref.shape[1]
    strips = rows // SUBLANES + 2
    row_id = lax.broadcasted_iota(jnp.int32, (SUBLANES, cols), 0)

    def run(i, ax, ay, x_up, y_up):
        def strip_rows(s):
            return pl.ds(s * SUBLANES, SUBLANES)

        def load(s):
            if s == 0:
                return top[...]
            if s == strips - 1:
                return bottom[...]
            return out_ref[i, pl.ds((s - 1) * SUBLANES, SUBLANES), :]

        def store(s, value):
            if s == 0:
                top[...] = value
            elif s == strips - 1:
                bottom[...] = value
            else:
                out_ref[i, pl.ds((s - 1) * SUBLANES, SUBLANES), :] = value

        blank = jnp.zeros((SUBLANES - halo, cols), jnp.float32)
        for s in range(strips):
            mask = mask_ref[0, strip_rows(s), :]
            keep[strip_rows(s), :] = (
                1.0
                - ax * mask_ref[2 if x_up else 1, strip_rows(s), :]
                - ay * mask_ref[4 if y_up else 3, strip_rows(s), :]
            )
            from_x[strip_rows(s), :] = ax * mask_ref[5 if x_up else 6, strip_rows(s), :]
            from_y[strip_rows(s), :] = ay * mask
            if s == 0:
                value = jnp.concatenate([blank, low_ref[i]], axis=0)
            elif s == strips - 1:
                value = jnp.concatenate([high_ref[i], blank], axis=0)
            else:
                value = spec_ref[i, pl.ds((s - 1) * SUBLANES, SUBLANES), :]
            store(s, value * mask)

        def substep(_, carry):
            order = range(strips) if y_up else range(strips - 1, -1, -1)
            before = jnp.zeros((SUBLANES, cols), jnp.float32)
            for s in order:
                value = load(s)
                turned = pltpu.roll(value, 1 if y_up else SUBLANES - 1, 0)
                upwind_y = jnp.where(row_id == (0 if y_up else SUBLANES - 1), before, turned)
                before = turned
                upwind_x = pltpu.roll(value, 1 if x_up else cols - 1, 1)
                store(
                    s,
                    value * keep[strip_rows(s), :]
                    + from_x[strip_rows(s), :] * upwind_x
                    + from_y[strip_rows(s), :] * upwind_y,
                )
            return carry

        lax.fori_loop(0, steps_ref[pl.program_id(0) * block + i], substep, 0)

    def component(i, carry):
        at = pl.program_id(0) * block + i
        for quad in range(4):

            @pl.when(quad_ref[at] == quad)
            def _():
                run(i, ax_ref[at], ay_ref[at], quad % 2 == 0, quad // 2 == 0)

        return carry

    lax.fori_loop(0, block, component, 0)


def propagate(scalars, spectrum, low, high, masks, start, size, low_start):
    comp_count, rows, cols = spectrum.shape
    halo = low.shape[1]
    block = block_size(start, size)
    while low_start % block:
        block -= 1
        while size % block or start % block:
            block -= 1
    ext = masks.shape[1]
    cells = size * rows * cols
    return pl.pallas_call(
        propagate_kernel,
        grid_spec=pltpu.PrefetchScalarGridSpec(
            num_scalar_prefetch=4,
            grid=(size // block,),
            in_specs=[
                pl.BlockSpec((block, rows, cols), lambda g, *_: (start // block + g, 0, 0)),
                pl.BlockSpec((block, halo, cols), lambda g, *_: (low_start // block + g, 0, 0)),
                pl.BlockSpec((block, halo, cols), lambda g, *_: (low_start // block + g, 0, 0)),
                pl.BlockSpec(masks.shape, lambda g, *_: (0, 0, 0)),
            ],
            out_specs=pl.BlockSpec((block, rows, cols), lambda g, *_: (g, 0, 0)),
            scratch_shapes=[
                pltpu.VMEM((ext, cols), jnp.float32),
                pltpu.VMEM((ext, cols), jnp.float32),
                pltpu.VMEM((ext, cols), jnp.float32),
                pltpu.VMEM((SUBLANES, cols), jnp.float32),
                pltpu.VMEM((SUBLANES, cols), jnp.float32),
            ],
        ),
        out_shape=jax.ShapeDtypeStruct((size, rows, cols), jnp.float32),
        compiler_params=pltpu.CompilerParams(vmem_limit_bytes=VMEM_BYTES),
        cost_estimate=pl.CostEstimate(
            flops=cells * 30, bytes_accessed=cells * 8, transcendentals=0
        ),
        name="propagate",
    )(*[scalar[start:start + size] for scalar in scalars], spectrum, low, high, masks)


def selection(dest_row, width):
    slot = lax.broadcasted_iota(jnp.int32, (2 * width, width), 0)
    return jnp.where(slot == dest_row, 1.0, 0.0).astype(jnp.bfloat16)


def gather_kernel(tile_ref, field_ref, dest_ref, *refs):
    outs, (packed, rows_of) = refs[:-2], refs[-2:]
    size, rows, cols = field_ref.shape
    parts = cols // LANES
    per_group = packed.shape[2] // LANES
    last = packed.shape[0] * per_group - 1
    step = pl.program_id(0)

    @pl.when(step == 0)
    def _():
        packed[...] = jnp.zeros_like(packed)

    for t in range(parts):
        rows_of[t] = field_ref[:, :, t * LANES:(t + 1) * LANES].reshape(size * rows, LANES)
    for r in range(rows):
        results = []
        for t in range(parts):
            values = rows_of[t, pl.ds(r, size, stride=rows), :].astype(jnp.bfloat16)
            pick = selection(dest_ref[pl.ds(r * parts + t, 1), :], LANES)
            results.append(
                lax.dot_general(
                    values, pick, (((1,), (1,)), ((), ())), preferred_element_type=jnp.float32
                ).astype(jnp.bfloat16)
            )
        for t in range(parts):
            first = tile_ref[(step * rows + r) * parts + t]
            for side in range(2):
                tile = jnp.minimum(first + side, last)
                at = (
                    tile // per_group,
                    slice(None),
                    pl.ds(pl.multiple_of(lax.rem(tile, per_group) * LANES, LANES), LANES),
                )
                packed[at] = packed[at] + results[t][:, side * LANES:(side + 1) * LANES]

    @pl.when(step == pl.num_programs(0) - 1)
    def _():
        groups = packed.shape[0] // len(outs)
        for h, out in enumerate(outs):
            out[...] = packed[h * groups:(h + 1) * groups]


def gather_points(tiles, dest, field, groups, per_group):
    size, rows, cols = field.shape
    parts = cols // LANES
    return pl.pallas_call(
        gather_kernel,
        grid_spec=pltpu.PrefetchScalarGridSpec(
            num_scalar_prefetch=1,
            grid=(rows // SUBLANES,),
            in_specs=[
                pl.BlockSpec((size, SUBLANES, cols), lambda g, *_: (0, g, 0)),
                pl.BlockSpec((SUBLANES * parts, LANES), lambda g, *_: (g, 0)),
            ],
            out_specs=[
                pl.BlockSpec((groups, size, per_group), lambda g, *_: (0, 0, 0))
                for _ in range(HALVES)
            ],
            scratch_shapes=[
                pltpu.VMEM((HALVES * groups, size, per_group), jnp.bfloat16),
                pltpu.VMEM((parts, size * SUBLANES, LANES), jnp.float32),
            ],
        ),
        out_shape=[
            jax.ShapeDtypeStruct((groups, size, per_group), jnp.bfloat16) for _ in range(HALVES)
        ],
        compiler_params=pltpu.CompilerParams(vmem_limit_bytes=VMEM_BYTES),
        cost_estimate=pl.CostEstimate(
            flops=size * rows * cols * 4 * LANES,
            bytes_accessed=size * rows * cols * 6,
            transcendentals=0,
        ),
        name="gather_points",
    )(tiles, field, dest)


def scatter_kernel(tile_ref, field_ref, dest_ref, *refs):
    returned, (out_ref, rows_of) = refs[:HALVES], refs[-2:]
    size, rows, cols = field_ref.shape
    parts = cols // LANES
    groups, _, width = returned[0].shape
    packed = refs[-3]
    per_group = width // LANES
    last = HALVES * groups * per_group - 1
    step = pl.program_id(0)

    @pl.when(step == 0)
    def _():
        for h in range(HALVES):
            packed[h * groups:(h + 1) * groups] = returned[h][...]

    for r in range(rows):
        for t in range(parts):
            first = tile_ref[(step * rows + r) * parts + t]
            sides = []
            for side in range(2):
                tile = jnp.minimum(first + side, last)
                sides.append(
                    packed[
                        tile // per_group,
                        :,
                        pl.ds(pl.multiple_of(lax.rem(tile, per_group) * LANES, LANES), LANES),
                    ]
                )
            pick = selection(dest_ref[pl.ds(r * parts + t, 1), :], LANES)
            rows_of[t, pl.ds(r, size, stride=rows), :] = jnp.dot(
                jnp.concatenate(sides, axis=1), pick, preferred_element_type=jnp.float32
            )
    for t in range(parts):
        at = (slice(None), slice(None), slice(t * LANES, (t + 1) * LANES))
        out_ref[at] = field_ref[at] + rows_of[t].reshape(size, rows, LANES)


def scatter_points(tiles, dest, field, returned, whole, comp_count, start):
    size, rows, cols = field.shape
    parts = cols // LANES
    groups, _, width = returned[0].shape
    aliased = [] if whole is None else [whole]

    def kernel(tile_ref, field_ref, dest_ref, *refs):
        out_ref, packed, rows_of = refs[-3:]
        scatter_kernel(
            tile_ref, field_ref, dest_ref, *refs[:HALVES], packed, out_ref, rows_of
        )

    return pl.pallas_call(
        kernel,
        grid_spec=pltpu.PrefetchScalarGridSpec(
            num_scalar_prefetch=1,
            grid=(rows // SUBLANES,),
            in_specs=[
                pl.BlockSpec((size, SUBLANES, cols), lambda g, *_: (0, g, 0)),
                pl.BlockSpec((SUBLANES * parts, LANES), lambda g, *_: (g, 0)),
            ]
            + [
                pl.BlockSpec((groups, size, width), lambda g, *_: (0, 0, 0))
                for _ in range(HALVES)
            ]
            + [pl.BlockSpec(memory_space=pl.ANY) for _ in aliased],
            out_specs=pl.BlockSpec((pl.Element(size), pl.Element(SUBLANES), pl.Element(cols)),
                                   lambda g, *_: (start, g * SUBLANES, 0)),
            scratch_shapes=[
                pltpu.VMEM((HALVES * groups, size, width), jnp.bfloat16),
                pltpu.VMEM((parts, size * SUBLANES, LANES), jnp.float32),
            ],
        ),
        out_shape=jax.ShapeDtypeStruct((comp_count, rows, cols), jnp.float32),
        input_output_aliases={3 + HALVES: 0} if aliased else {},
        compiler_params=pltpu.CompilerParams(vmem_limit_bytes=VMEM_BYTES),
        cost_estimate=pl.CostEstimate(
            flops=size * rows * cols * 4 * LANES,
            bytes_accessed=size * rows * cols * 10,
            transcendentals=0,
        ),
        name="scatter_points",
    )(tiles, field, dest, *returned, *aliased)


def source_kernel(counts, groups, mix_in, mix_out, growth, damping, weight, *refs):
    ins, outs, points = refs[:len(counts)], refs[len(counts):-1], refs[-1]
    total = sum(counts)
    for g in range(groups):
        at = g * total
        for ref, count in zip(ins, counts):
            points[at:at + count, :] = ref[g * count:(g + 1) * count, :]
            at += count
    rounded = points[...]
    hidden = jnp.dot(mix_in[...], rounded, preferred_element_type=jnp.float32)
    square = (hidden * hidden).astype(jnp.bfloat16)
    transfer = jnp.dot(mix_out[...], square, preferred_element_type=jnp.float32)
    energy = rounded.astype(jnp.float32)
    mean_energy = jnp.sum(weight[...] * energy, axis=0, keepdims=True)
    increment = 0.5 * (
        growth[...] * energy
        + 0.25 * transfer
        - damping[...] * energy * (mean_energy / (1.0 + mean_energy))
    )
    increment = increment.astype(jnp.bfloat16)
    for g in range(groups):
        at = g * total
        for ref, count in zip(outs, counts):
            ref[g * count:(g + 1) * count, :] = increment[at:at + count, :]
            at += count


def source_terms(pieces, counts, groups, mix_in, mix_out, growth, damping, weight):
    comp_count = mix_in.shape[0]
    slots = pieces[0].shape[1]
    width = min(512, slots)
    fixed = lambda g: (0, 0)
    moving = lambda g: (0, g)
    if len(counts) == 1:
        counts, groups = [comp_count], 1
    return pl.pallas_call(
        functools.partial(source_kernel, counts, groups),
        grid=(slots // width,),
        in_specs=[pl.BlockSpec(mix_in.shape, fixed)] * 2
        + [pl.BlockSpec((comp_count, 1), fixed)] * 3
        + [pl.BlockSpec((groups * count, width), moving) for count in counts],
        out_specs=[pl.BlockSpec((groups * count, width), moving) for count in counts],
        out_shape=[
            jax.ShapeDtypeStruct((groups * count, slots), jnp.bfloat16) for count in counts
        ],
        scratch_shapes=[pltpu.VMEM((comp_count, width), jnp.bfloat16)],
        compiler_params=pltpu.CompilerParams(vmem_limit_bytes=VMEM_BYTES),
        cost_estimate=pl.CostEstimate(
            flops=4 * comp_count * comp_count * slots,
            bytes_accessed=4 * comp_count * (comp_count + slots),
            transcendentals=0,
        ),
        name="source_terms",
    )(mix_in, mix_out, growth, damping, weight, *pieces)


def edge_rows(block, dim, width, axis):
    count = lax.axis_size(axis)
    forward = [(i, i + 1) for i in range(count - 1)]
    backward = [(target, source) for source, target in forward]
    size = block.shape[dim]
    low = lax.ppermute(lax.slice_in_dim(block, size - width, size, axis=dim), axis, forward)
    high = lax.ppermute(lax.slice_in_dim(block, 0, width, axis=dim), axis, backward)
    return low, high


def mask_planes(sea_mask, low, high, strip):
    blank = jnp.zeros((strip - low.shape[0], sea_mask.shape[1]), sea_mask.dtype)
    mask = jnp.concatenate([blank, low, sea_mask, high, blank], axis=0).astype(jnp.float32)
    row = jnp.zeros_like(mask[:1])
    col = jnp.zeros_like(mask[:, :1])
    left = jnp.concatenate([col, mask[:, :-1]], axis=1)
    right = jnp.concatenate([mask[:, 1:], col], axis=1)
    above = jnp.concatenate([row, mask[:-1]], axis=0)
    below = jnp.concatenate([mask[1:], row], axis=0)
    return jnp.stack([mask, left, right, above, below, mask * left, mask * right])


def slot_table(sea_mask):
    cells = sea_mask.reshape(-1, LANES).astype(jnp.float32)
    upto = jnp.triu(jnp.ones((LANES, LANES), jnp.float32))
    rank = jnp.dot(cells, upto, precision=lax.Precision.HIGHEST)
    count = rank[:, -1]
    blocks = cells.shape[0]
    before = jnp.tril(jnp.ones((blocks, blocks), jnp.float32), -1)
    offset = jnp.dot(before, count, precision=lax.Precision.HIGHEST).astype(jnp.int32)
    tiles = offset // LANES
    rank = rank.astype(jnp.int32) - 1 + (offset - tiles * LANES)[:, None]
    return tiles, jnp.where(cells > 0.0, rank, -1)


def local(
    spectrum, sea_mask, point_index, band_counts, sub_counts, mix_in, mix_out, growth, damping
):
    freq_count, dir_count, row_count, lon_count = spectrum.shape
    comp_count = freq_count * dir_count
    all_count = growth.shape[0] * growth.shape[1]
    groups = lax.axis_size("comp")
    per_group = point_index.shape[1] // (groups * HALVES)
    sizes = chunk_sizes(comp_count)
    starts = [sum(sizes[:j]) for j in range(len(sizes))]

    field = spectrum.reshape(comp_count, row_count, lon_count)
    mask_low, mask_high = edge_rows(sea_mask, 0, NSUB, "lat")
    edges = [edge_rows(field[:sizes[0]], 1, NSUB, "lat")]
    if len(sizes) > 1:
        edges.append(edge_rows(field[sizes[0]:], 1, NSUB, "lat"))

    freq_index = lax.axis_index("comp") * freq_count + jnp.arange(freq_count, dtype=jnp.int32)
    courant_x, courant_y = courant(freq_index, sub_counts, dir_count)
    courant_x, courant_y = courant_x.reshape(-1), courant_y.reshape(-1)
    scalars = (
        jnp.abs(courant_x),
        jnp.abs(courant_y),
        (courant_x < 0.0).astype(jnp.int32) + 2 * (courant_y < 0.0).astype(jnp.int32),
        jnp.repeat(sub_counts, dir_count),
    )
    tiles, dest = slot_table(sea_mask)
    masks = mask_planes(sea_mask, mask_low, mask_high, SUBLANES)

    fields, arrived = [], [[] for _ in range(HALVES)]
    for j, (start, size) in enumerate(zip(starts, sizes)):
        low, high = edges[min(j, 1)]
        moved = propagate(
            scalars, field, low, high, masks, start, size, 0 if j == 0 else start - sizes[0]
        )
        fields.append(moved)
        packed = gather_points(tiles, dest, moved, groups, per_group)
        for h in range(HALVES):
            piece = lax.all_to_all(packed[h], "comp", split_axis=0, concat_axis=0, tiled=True)
            arrived[h].append(piece.reshape(groups * size, per_group))

    weight = freq_weights(*growth.shape).reshape(all_count, 1)
    growth_col = growth.reshape(all_count, 1)
    damping_col = damping.reshape(all_count, 1)
    back = [[None] * HALVES for _ in sizes]
    for h in range(HALVES):
        increments = source_terms(
            arrived[h], sizes, groups, mix_in, mix_out, growth_col, damping_col, weight
        )
        for j in reversed(range(len(sizes))):
            piece = increments[j].reshape(groups, sizes[j], per_group)
            back[j][h] = lax.all_to_all(piece, "comp", split_axis=0, concat_axis=0, tiled=True)

    whole = None
    for j in reversed(range(len(sizes))):
        whole = scatter_points(tiles, dest, fields[j], back[j], whole, comp_count, starts[j])
    return whole.reshape(spectrum.shape)


def solution(mesh):
    return jax.shard_map(
        local,
        mesh=mesh,
        in_specs=(
            P("comp", None, "lat", None),
            P("lat", None),
            P("lat", None),
            P("lat"),
            P("comp"),
            P(),
            P(),
            P(),
            P(),
        ),
        out_specs=P("comp", None, "lat", None),
        check_vma=False,
    )
```

```python
import functools

import jax
import jax.numpy as jnp
from jax import lax
from jax.experimental import pallas as pl
from jax.experimental.pallas import tpu as pltpu
from jax.sharding import PartitionSpec as P

NSUB = 4
SUBLANES = 8
LANES = 128
VMEM_BYTES = 56 * 1024 * 1024


def chunk_sizes(comp_count, shares):
    if comp_count % 16:
        return [comp_count]
    units, total = comp_count // 16, sum(shares)
    bounds = [units * sum(shares[:j]) // total for j in range(len(shares) + 1)]
    return [16 * (high - low) for low, high in zip(bounds, bounds[1:]) if high > low]


def courant(freq_index, sub_steps, dir_count):
    group_speed = 1.4 * jnp.power(0.93, freq_index.astype(jnp.float32))
    per_step = group_speed / sub_steps.astype(jnp.float32)
    angles = (jnp.arange(dir_count, dtype=jnp.float32) + 0.5) * (2.0 * jnp.pi / dir_count)
    return (per_step[..., None] * jnp.cos(angles), per_step[..., None] * jnp.sin(angles))


def freq_weights(freq_count, dir_count):
    raw_weight = jnp.power(1.1, jnp.arange(freq_count, dtype=jnp.float32))
    raw_weight = raw_weight / (dir_count * jnp.sum(raw_weight))
    return jnp.repeat(raw_weight, dir_count)


def propagate_kernel(
    start,
    ax_ref, ay_ref, quad_ref, steps_ref,
    spec_ref, low_ref, high_ref, mask_ref,
    out_ref,
    keep, from_x, from_y, even, odd,
):
    block, rows, cols = spec_ref.shape
    halo = low_ref.shape[1]
    strips = rows // SUBLANES + 2
    row_id = lax.broadcasted_iota(jnp.int32, (SUBLANES, cols), 0)

    def strip_rows(s):
        return pl.ds(s * SUBLANES, SUBLANES)

    def run(i, at, x_up, y_up):
        ax, ay = ax_ref[at], ay_ref[at]
        blank = jnp.zeros((SUBLANES - halo, cols), jnp.float32)
        for s in range(strips):
            mask = mask_ref[0, strip_rows(s), :]
            keep[strip_rows(s), :] = (
                1.0
                - ax * mask_ref[2 if x_up else 1, strip_rows(s), :]
                - ay * mask_ref[4 if y_up else 3, strip_rows(s), :]
            )
            from_x[strip_rows(s), :] = ax * mask_ref[5 if x_up else 6, strip_rows(s), :]
            from_y[strip_rows(s), :] = ay * mask
            if s == 0:
                value = jnp.concatenate([blank, low_ref[i]], axis=0)
            elif s == strips - 1:
                value = jnp.concatenate([high_ref[i], blank], axis=0)
            else:
                value = spec_ref[i, strip_rows(s - 1), :]
            even[strip_rows(s), :] = value * mask

        def substep(source, target):
            edge = 0 if y_up else SUBLANES - 1
            before = jnp.zeros((SUBLANES, cols), jnp.float32)
            for s in range(strips) if y_up else range(strips - 1, -1, -1):
                value = source[strip_rows(s), :]
                turned = pltpu.roll(value, 1 if y_up else SUBLANES - 1, 0)
                upwind_y = jnp.where(row_id == edge, before, turned)
                before = turned
                upwind_x = pltpu.roll(value, 1 if x_up else cols - 1, 1)
                target[strip_rows(s), :] = (
                    value * keep[strip_rows(s), :]
                    + from_x[strip_rows(s), :] * upwind_x
                    + from_y[strip_rows(s), :] * upwind_y
                )

        def pair(_, carry):
            substep(even, odd)
            substep(odd, even)
            return carry

        steps = steps_ref[at]
        lax.fori_loop(0, steps // 2, pair, 0)

        @pl.when(lax.rem(steps, 2) == 1)
        def _():
            substep(even, odd)
            out_ref[i] = odd[pl.ds(SUBLANES, rows), :]

        @pl.when(lax.rem(steps, 2) == 0)
        def _():
            out_ref[i] = even[pl.ds(SUBLANES, rows), :]

    def component(i, carry):
        at = start + pl.program_id(0) * block + i
        for quad in range(4):

            @pl.when(quad_ref[at] == quad)
            def _():
                run(i, at, quad % 2 == 0, quad // 2 == 0)

        return carry

    lax.fori_loop(0, block, component, 0)


def propagate(scalars, spectrum, low, high, masks, start, size, low_start):
    comp_count, rows, cols = spectrum.shape
    halo = low.shape[1]
    block = next(
        n for n in range(min(16, size), 0, -1)
        if size % n == 0 and start % n == 0 and low_start % n == 0
    )
    ext = masks.shape[1]
    cells = size * rows * cols
    return pl.pallas_call(
        functools.partial(propagate_kernel, start),
        grid_spec=pltpu.PrefetchScalarGridSpec(
            num_scalar_prefetch=4,
            grid=(size // block,),
            in_specs=[
                pl.BlockSpec((block, rows, cols), lambda g, *_: (start // block + g, 0, 0)),
                pl.BlockSpec((block, halo, cols), lambda g, *_: (low_start // block + g, 0, 0)),
                pl.BlockSpec((block, halo, cols), lambda g, *_: (low_start // block + g, 0, 0)),
                pl.BlockSpec(masks.shape, lambda g, *_: (0, 0, 0)),
            ],
            out_specs=pl.BlockSpec((block, rows, cols), lambda g, *_: (g, 0, 0)),
            scratch_shapes=[pltpu.VMEM((ext, cols), jnp.float32) for _ in range(5)],
        ),
        out_shape=jax.ShapeDtypeStruct((size, rows, cols), jnp.float32),
        compiler_params=pltpu.CompilerParams(vmem_limit_bytes=VMEM_BYTES),
        cost_estimate=pl.CostEstimate(
            flops=cells * 30, bytes_accessed=cells * 8, transcendentals=0
        ),
        name="propagate",
    )(*scalars, spectrum, low, high, masks)


def selection(dest_row, width):
    slot = lax.broadcasted_iota(jnp.int32, (2 * width, width), 0)
    return jnp.where(slot == dest_row, 1.0, 0.0).astype(jnp.bfloat16)


def tile_place(tile, per_group):
    lane = lax.rem(tile, per_group) * LANES
    return tile // per_group, slice(None), pl.ds(pl.multiple_of(lane, LANES), LANES)


def gather_kernel(tile_ref, field_ref, dest_ref, *refs):
    outs, (packed, rows_of, open_tile) = refs[:-3], refs[-3:]
    size, rows, cols = field_ref.shape
    parts = cols // LANES
    per_group = packed.shape[2] // LANES
    last_tile = packed.shape[0] * per_group - 1
    step = pl.program_id(0)
    first_block = step * rows * parts

    @pl.when(step == 0)
    def _():
        packed[...] = jnp.zeros_like(packed)
        open_tile[...] = jnp.zeros_like(open_tile)

    for t in range(parts):
        rows_of[t] = field_ref[:, :, t * LANES:(t + 1) * LANES].reshape(size * rows, LANES)

    begun = open_tile[...]
    for b in range(rows * parts):
        r, t = b // parts, b % parts
        values = rows_of[t, pl.ds(r, size, stride=rows), :].astype(jnp.bfloat16)
        pick = selection(dest_ref[pl.ds(b, 1), :], LANES)
        result = lax.dot_general(
            values, pick, (((1,), (1,)), ((), ())), preferred_element_type=jnp.float32
        ).astype(jnp.bfloat16)
        tile, following = tile_ref[first_block + b], tile_ref[first_block + b + 1]
        full = begun + result[:, :LANES]
        packed[tile_place(tile, per_group)] = full
        begun = jnp.where(following > tile, result[:, LANES:], full)
    open_tile[...] = begun

    @pl.when(step == pl.num_programs(0) - 1)
    def _():
        tile = tile_ref[first_block + rows * parts]

        @pl.when(tile <= last_tile)
        def _():
            packed[tile_place(tile, per_group)] = begun

        width = outs[0].shape[2]
        for h, out in enumerate(outs):
            out[...] = packed[:, :, h * width:(h + 1) * width]


def gather_points(tiles, dest, field, groups, per_group, pieces):
    size, rows, cols = field.shape
    parts = cols // LANES
    width = per_group // pieces
    return pl.pallas_call(
        gather_kernel,
        grid_spec=pltpu.PrefetchScalarGridSpec(
            num_scalar_prefetch=1,
            grid=(rows // SUBLANES,),
            in_specs=[
                pl.BlockSpec((size, SUBLANES, cols), lambda g, *_: (0, g, 0)),
                pl.BlockSpec((SUBLANES * parts, LANES), lambda g, *_: (g, 0)),
            ],
            out_specs=[
                pl.BlockSpec((groups, size, width), lambda g, *_: (0, 0, 0))
                for _ in range(pieces)
            ],
            scratch_shapes=[
                pltpu.VMEM((groups, size, per_group), jnp.bfloat16),
                pltpu.VMEM((parts, size * SUBLANES, LANES), jnp.float32),
                pltpu.VMEM((size, LANES), jnp.bfloat16),
            ],
        ),
        out_shape=[
            jax.ShapeDtypeStruct((groups, size, width), jnp.bfloat16) for _ in range(pieces)
        ],
        compiler_params=pltpu.CompilerParams(vmem_limit_bytes=VMEM_BYTES),
        cost_estimate=pl.CostEstimate(
            flops=size * rows * cols * 4 * LANES,
            bytes_accessed=size * rows * cols * 6,
            transcendentals=0,
        ),
        name="gather_points",
    )(tiles, field, dest)


def scatter_kernel(tile_ref, field_ref, dest_ref, first_ref, second_ref, *refs):
    out_ref, packed, rows_of = refs[-3:]
    size, rows, cols = field_ref.shape
    parts = cols // LANES
    width = first_ref.shape[2]
    per_group = packed.shape[2] // LANES
    last_tile = packed.shape[0] * per_group - 1
    first_block = pl.program_id(0) * rows * parts

    @pl.when(pl.program_id(0) == 0)
    def _():
        packed[:, :, :width] = first_ref[...]
        packed[:, :, width:] = second_ref[...]

    for b in range(rows * parts):
        r, t = b // parts, b % parts
        tile = jnp.minimum(tile_ref[first_block + b], last_tile)
        following = jnp.minimum(tile + 1, last_tile)
        values = jnp.concatenate(
            [packed[tile_place(tile, per_group)], packed[tile_place(following, per_group)]],
            axis=1,
        )
        pick = selection(dest_ref[pl.ds(b, 1), :], LANES)
        rows_of[t, pl.ds(r, size, stride=rows), :] = jnp.dot(
            values, pick, preferred_element_type=jnp.float32
        )
    for t in range(parts):
        at = (slice(None), slice(None), slice(t * LANES, (t + 1) * LANES))
        out_ref[at] = field_ref[at] + rows_of[t].reshape(size, rows, LANES)


def scatter_points(tiles, dest, field, first, second, whole, start):
    comp_count, (size, rows, cols) = first.shape[1], field.shape
    parts = cols // LANES
    groups, _, width = first.shape
    aliased = [] if whole is None else [whole]
    block = (pl.Element(size), pl.Element(SUBLANES), pl.Element(cols))
    return pl.pallas_call(
        scatter_kernel,
        grid_spec=pltpu.PrefetchScalarGridSpec(
            num_scalar_prefetch=1,
            grid=(rows // SUBLANES,),
            in_specs=[
                pl.BlockSpec((size, SUBLANES, cols), lambda g, *_: (0, g, 0)),
                pl.BlockSpec((SUBLANES * parts, LANES), lambda g, *_: (g, 0)),
                pl.BlockSpec(
                    (pl.Element(groups), pl.Element(size), pl.Element(width)),
                    lambda g, *_: (0, start, 0),
                ),
                pl.BlockSpec((groups, size, width), lambda g, *_: (0, 0, 0)),
            ]
            + [pl.BlockSpec(memory_space=pl.ANY) for _ in aliased],
            out_specs=pl.BlockSpec(block, lambda g, *_: (start, g * SUBLANES, 0)),
            scratch_shapes=[
                pltpu.VMEM((groups, size, 2 * width), jnp.bfloat16),
                pltpu.VMEM((parts, size * SUBLANES, LANES), jnp.float32),
            ],
        ),
        out_shape=jax.ShapeDtypeStruct((comp_count, rows, cols), jnp.float32),
        input_output_aliases={5: 0} if aliased else {},
        compiler_params=pltpu.CompilerParams(vmem_limit_bytes=VMEM_BYTES),
        cost_estimate=pl.CostEstimate(
            flops=size * rows * cols * 4 * LANES,
            bytes_accessed=size * rows * cols * 10,
            transcendentals=0,
        ),
        name="scatter_points",
    )(tiles, field, dest, first, second, *aliased)


def source_kernel(counts, out_counts, groups, mix_in, mix_out, growth, damping, weight, *refs):
    ins, outs, points = refs[:len(counts)], refs[len(counts):-1], refs[-1]
    total = sum(counts)
    for g in range(groups):
        at = g * total
        for ref, count in zip(ins, counts):
            points[at:at + count, :] = ref[g * count:(g + 1) * count, :]
            at += count
    rounded = points[...]
    hidden = jnp.dot(mix_in[...], rounded, preferred_element_type=jnp.float32)
    square = (hidden * hidden).astype(jnp.bfloat16)
    transfer = jnp.dot(mix_out[...], square, preferred_element_type=jnp.float32)
    energy = rounded.astype(jnp.float32)
    mean_energy = jnp.sum(weight[...] * energy, axis=0, keepdims=True)
    increment = 0.5 * (
        growth[...] * energy
        + 0.25 * transfer
        - damping[...] * energy * (mean_energy / (1.0 + mean_energy))
    )
    increment = increment.astype(jnp.bfloat16)
    for g in range(groups):
        at = g * total
        for ref, count in zip(outs, out_counts):
            ref[g * count:(g + 1) * count, :] = increment[at:at + count, :]
            at += count


def source_terms(pieces, counts, out_counts, slots, starts, groups, mix_in, mix_out, columns):
    comp_count = mix_in.shape[0]
    width = min(512, slots)
    fixed = lambda g: (0, 0)
    if len(counts) == 1:
        counts, out_counts, groups = [comp_count], [comp_count], 1

    def moving(start):
        return lambda g: (0, start // width + g)

    return pl.pallas_call(
        functools.partial(source_kernel, counts, out_counts, groups),
        grid=(slots // width,),
        in_specs=[pl.BlockSpec(mix_in.shape, fixed)] * 2
        + [pl.BlockSpec((comp_count, 1), fixed)] * 3
        + [
            pl.BlockSpec((groups * count, width), moving(start))
            for count, start in zip(counts, starts)
        ],
        out_specs=[pl.BlockSpec((groups * count, width), moving(0)) for count in out_counts],
        out_shape=[
            jax.ShapeDtypeStruct((groups * count, slots), jnp.bfloat16) for count in out_counts
        ],
        scratch_shapes=[pltpu.VMEM((comp_count, width), jnp.bfloat16)],
        compiler_params=pltpu.CompilerParams(vmem_limit_bytes=VMEM_BYTES),
        cost_estimate=pl.CostEstimate(
            flops=4 * comp_count * comp_count * slots,
            bytes_accessed=4 * comp_count * (comp_count + slots),
            transcendentals=0,
        ),
        name="source_terms",
    )(mix_in, mix_out, *columns, *pieces)


def edge_rows(block, dim, width, axis):
    count = lax.axis_size(axis)
    forward = [(i, i + 1) for i in range(count - 1)]
    backward = [(target, source) for source, target in forward]
    size = block.shape[dim]
    low = lax.ppermute(lax.slice_in_dim(block, size - width, size, axis=dim), axis, forward)
    high = lax.ppermute(lax.slice_in_dim(block, 0, width, axis=dim), axis, backward)
    return low, high


def mask_planes(sea_mask, low, high, strip):
    blank = jnp.zeros((strip - low.shape[0], sea_mask.shape[1]), sea_mask.dtype)
    mask = jnp.concatenate([blank, low, sea_mask, high, blank], axis=0).astype(jnp.float32)
    row = jnp.zeros_like(mask[:1])
    col = jnp.zeros_like(mask[:, :1])
    left = jnp.concatenate([col, mask[:, :-1]], axis=1)
    right = jnp.concatenate([mask[:, 1:], col], axis=1)
    above = jnp.concatenate([row, mask[:-1]], axis=0)
    below = jnp.concatenate([mask[1:], row], axis=0)
    return jnp.stack([mask, left, right, above, below, mask * left, mask * right])


def slot_table(sea_mask):
    cells = sea_mask.reshape(-1, LANES).astype(jnp.float32)
    upto = jnp.triu(jnp.ones((LANES, LANES), jnp.float32))
    rank = jnp.dot(cells, upto, precision=lax.Precision.HIGHEST)
    count = rank[:, -1]
    blocks = cells.shape[0]
    before = jnp.tril(jnp.ones((blocks, blocks), jnp.float32), -1)
    offset = jnp.dot(before, count, precision=lax.Precision.HIGHEST)
    offset = jnp.append(offset, offset[-1] + count[-1]).astype(jnp.int32)
    tiles = offset // LANES
    offset = (offset - tiles * LANES)[:-1]
    rank = rank.astype(jnp.int32) - 1 + offset[:, None]
    return tiles, jnp.where(cells > 0.0, rank, -1)


def local(
    spectrum, sea_mask, point_index, band_counts, sub_counts, mix_in, mix_out, growth, damping
):
    freq_count, dir_count, row_count, lon_count = spectrum.shape
    comp_count = freq_count * dir_count
    all_count = growth.shape[0] * growth.shape[1]
    groups = lax.axis_size("comp")
    per_group = point_index.shape[1] // groups
    half = per_group // 2
    sizes = chunk_sizes(comp_count, (1, 2, 3, 3))
    starts = [sum(sizes[:j]) for j in range(len(sizes))]

    field = spectrum.reshape(comp_count, row_count, lon_count)
    mask_low, mask_high = edge_rows(sea_mask, 0, NSUB, "lat")
    edges = [edge_rows(field[:sizes[0]], 1, NSUB, "lat")]
    if len(sizes) > 1:
        edges.append(edge_rows(field[sizes[0]:], 1, NSUB, "lat"))

    freq_index = lax.axis_index("comp") * freq_count + jnp.arange(freq_count, dtype=jnp.int32)
    courant_x, courant_y = courant(freq_index, sub_counts, dir_count)
    courant_x, courant_y = courant_x.reshape(-1), courant_y.reshape(-1)
    scalars = (
        jnp.abs(courant_x),
        jnp.abs(courant_y),
        (courant_x < 0.0).astype(jnp.int32) + 2 * (courant_y < 0.0).astype(jnp.int32),
        jnp.repeat(sub_counts, dir_count),
    )
    tiles, dest = slot_table(sea_mask)
    masks = mask_planes(sea_mask, mask_low, mask_high, SUBLANES)

    def exchange(piece):
        return lax.all_to_all(piece, "comp", split_axis=0, concat_axis=0, tiled=True)

    def as_rows(piece):
        return piece.reshape(groups * piece.shape[1], piece.shape[2])

    fields, arrived = [], [[], []]
    for j, (start, size) in enumerate(zip(starts, sizes)):
        low, high = edges[min(j, 1)]
        moved = propagate(
            scalars, field, low, high, masks, start, size, 0 if j == 0 else start - sizes[0]
        )
        fields.append(moved)
        pieces = 2 if j == len(sizes) - 1 else 1
        packed = gather_points(tiles, dest, moved, groups, per_group, pieces)
        packed = [as_rows(exchange(piece)) for piece in packed]
        for h in range(2):
            arrived[h].append((packed[h % pieces], h * half if pieces == 1 else 0))

    columns = [
        column.reshape(all_count, 1)
        for column in (growth, damping, freq_weights(*growth.shape))
    ]
    for h in range(2):
        parts_out = [comp_count] if h == 0 else sizes
        increments = source_terms(
            [piece for piece, _ in arrived[h]], sizes, parts_out, half,
            [at for _, at in arrived[h]], groups, mix_in, mix_out, columns,
        )
        if h == 0:
            first = exchange(increments[0].reshape(groups, comp_count, half))

    whole = None
    for j in reversed(range(len(sizes))):
        second = exchange(increments[j].reshape(groups, sizes[j], half))
        whole = scatter_points(tiles, dest, fields[j], first, second, whole, starts[j])
    return whole.reshape(spectrum.shape)


def solution(mesh):
    return jax.shard_map(
        local,
        mesh=mesh,
        in_specs=(
            P("comp", None, "lat", None),
            P("lat", None),
            P("lat", None),
            P("lat"),
            P("comp"),
            P(),
            P(),
            P(),
            P(),
        ),
        out_specs=P("comp", None, "lat", None),
        check_vma=False,
    )
```

```python
import functools

import jax
import jax.numpy as jnp
from jax import lax
from jax.experimental import pallas as pl
from jax.experimental.pallas import tpu as pltpu
from jax.sharding import PartitionSpec as P

NSUB = 4
SUBLANES = 8
LANES = 128
VMEM_BYTES = 56 * 1024 * 1024


def chunk_sizes(comp_count, shares):
    if comp_count % 16:
        return [comp_count]
    units, total = comp_count // 16, sum(shares)
    bounds = [units * sum(shares[:j]) // total for j in range(len(shares) + 1)]
    return [16 * (high - low) for low, high in zip(bounds, bounds[1:]) if high > low]


def courant(freq_index, sub_steps, dir_count):
    group_speed = 1.4 * jnp.power(0.93, freq_index.astype(jnp.float32))
    per_step = group_speed / sub_steps.astype(jnp.float32)
    angles = (jnp.arange(dir_count, dtype=jnp.float32) + 0.5) * (2.0 * jnp.pi / dir_count)
    return (per_step[..., None] * jnp.cos(angles), per_step[..., None] * jnp.sin(angles))


def freq_weights(freq_count, dir_count):
    raw_weight = jnp.power(1.1, jnp.arange(freq_count, dtype=jnp.float32))
    raw_weight = raw_weight / (dir_count * jnp.sum(raw_weight))
    return jnp.repeat(raw_weight, dir_count)


def propagate_kernel(
    start,
    ax_ref, ay_ref, quad_ref, steps_ref,
    spec_ref, low_ref, high_ref, mask_ref,
    *refs,
):
    out_ref, keep, from_x, from_y, even, odd = refs[-6:]
    block, rows, cols = spec_ref.shape
    halo = low_ref.shape[1]
    strips = rows // SUBLANES + 2
    row_id = lax.broadcasted_iota(jnp.int32, (SUBLANES, cols), 0)

    def strip_rows(s):
        return pl.ds(s * SUBLANES, SUBLANES)

    def run(i, at, x_up, y_up):
        ax, ay = ax_ref[at], ay_ref[at]
        blank = jnp.zeros((SUBLANES - halo, cols), jnp.float32)
        for s in range(strips):
            mask = mask_ref[0, strip_rows(s), :]
            keep[strip_rows(s), :] = (
                1.0
                - ax * mask_ref[2 if x_up else 1, strip_rows(s), :]
                - ay * mask_ref[4 if y_up else 3, strip_rows(s), :]
            )
            from_x[strip_rows(s), :] = ax * mask_ref[5 if x_up else 6, strip_rows(s), :]
            from_y[strip_rows(s), :] = ay * mask
            if s == 0:
                value = jnp.concatenate([blank, low_ref[i]], axis=0)
            elif s == strips - 1:
                value = jnp.concatenate([high_ref[i], blank], axis=0)
            else:
                value = spec_ref[i, strip_rows(s - 1), :]
            even[strip_rows(s), :] = value * mask

        def substep(source, target):
            edge = 0 if y_up else SUBLANES - 1
            before = jnp.zeros((SUBLANES, cols), jnp.float32)
            for s in range(strips) if y_up else range(strips - 1, -1, -1):
                value = source[strip_rows(s), :]
                turned = pltpu.roll(value, 1 if y_up else SUBLANES - 1, 0)
                upwind_y = jnp.where(row_id == edge, before, turned)
                before = turned
                upwind_x = pltpu.roll(value, 1 if x_up else cols - 1, 1)
                target[strip_rows(s), :] = (
                    value * keep[strip_rows(s), :]
                    + from_x[strip_rows(s), :] * upwind_x
                    + from_y[strip_rows(s), :] * upwind_y
                )

        def pair(_, carry):
            substep(even, odd)
            substep(odd, even)
            return carry

        steps = steps_ref[at]
        lax.fori_loop(0, steps // 2, pair, 0)

        @pl.when(lax.rem(steps, 2) == 1)
        def _():
            substep(even, odd)
            out_ref[i] = odd[pl.ds(SUBLANES, rows), :]

        @pl.when(lax.rem(steps, 2) == 0)
        def _():
            out_ref[i] = even[pl.ds(SUBLANES, rows), :]

    def component(i, carry):
        at = start + pl.program_id(0) * block + i
        for quad in range(4):

            @pl.when(quad_ref[at] == quad)
            def _():
                run(i, at, quad % 2 == 0, quad // 2 == 0)

        return carry

    lax.fori_loop(0, block, component, 0)


def propagate(scalars, spectrum, low, high, masks, start, size, low_start, chain):
    comp_count, rows, cols = spectrum.shape
    halo = low.shape[1]
    block = next(
        n for n in range(min(16, size), 0, -1)
        if size % n == 0 and start % n == 0 and low_start % n == 0
    )
    ext = masks.shape[1]
    cells = size * rows * cols
    return pl.pallas_call(
        functools.partial(propagate_kernel, start),
        grid_spec=pltpu.PrefetchScalarGridSpec(
            num_scalar_prefetch=4,
            grid=(size // block,),
            in_specs=[
                pl.BlockSpec((block, rows, cols), lambda g, *_: (start // block + g, 0, 0)),
                pl.BlockSpec((block, halo, cols), lambda g, *_: (low_start // block + g, 0, 0)),
                pl.BlockSpec((block, halo, cols), lambda g, *_: (low_start // block + g, 0, 0)),
                pl.BlockSpec(masks.shape, lambda g, *_: (0, 0, 0)),
            ]
            + [pl.BlockSpec(memory_space=pl.ANY) for _ in chain],
            out_specs=pl.BlockSpec((block, rows, cols), lambda g, *_: (start // block + g, 0, 0)),
            scratch_shapes=[pltpu.VMEM((ext, cols), jnp.float32) for _ in range(5)],
        ),
        out_shape=jax.ShapeDtypeStruct((comp_count, rows, cols), jnp.float32),
        input_output_aliases={8: 0} if chain else {},
        compiler_params=pltpu.CompilerParams(vmem_limit_bytes=VMEM_BYTES),
        cost_estimate=pl.CostEstimate(
            flops=cells * 30, bytes_accessed=cells * 8, transcendentals=0
        ),
        name="propagate",
    )(*scalars, spectrum, low, high, masks, *chain)


def selection(dest_row, width):
    slot = lax.broadcasted_iota(jnp.int32, (2 * width, width), 0)
    slot = slot.astype(jnp.float32).astype(jnp.bfloat16)
    one, zero = jnp.ones((), jnp.bfloat16), jnp.zeros((), jnp.bfloat16)
    return jnp.where(slot == dest_row.astype(jnp.float32).astype(jnp.bfloat16), one, zero)


def tile_place(tile, per_group):
    lane = lax.rem(tile, per_group) * LANES
    return tile // per_group, slice(None), pl.ds(pl.multiple_of(lane, LANES), LANES)


def gather_kernel(tile_ref, field_ref, dest_ref, *refs):
    outs, (packed, rows_of, open_tile) = refs[:-3], refs[-3:]
    size, rows, cols = field_ref.shape
    parts = cols // LANES
    per_group = packed.shape[2] // LANES
    step = pl.program_id(0)
    first_block = step * rows * parts

    @pl.when(step == 0)
    def _():
        packed[...] = jnp.zeros_like(packed)
        open_tile[...] = jnp.zeros_like(open_tile)

    for t in range(parts):
        rows_of[t] = field_ref[:, :, t * LANES:(t + 1) * LANES].reshape(size * rows, LANES)

    begun = open_tile[...]
    for b in range(rows * parts):
        r, t = b // parts, b % parts
        values = rows_of[t, pl.ds(r, size, stride=rows), :].astype(jnp.bfloat16)
        pick = selection(dest_ref[pl.ds(b, 1), :], LANES)
        result = lax.dot_general(
            values, pick, (((1,), (1,)), ((), ())), preferred_element_type=jnp.float32
        ).astype(jnp.bfloat16)
        tile, following = tile_ref[first_block + b], tile_ref[first_block + b + 1]
        full = begun + result[:, :LANES]
        packed[tile_place(tile, per_group)] = full
        begun = jnp.where(following > tile, result[:, LANES:], full)
    open_tile[...] = begun

    @pl.when(step == pl.num_programs(0) - 1)
    def _():
        packed[tile_place(tile_ref[first_block + rows * parts], per_group)] = begun
        groups, _, width = outs[0].shape
        for h, out in enumerate(outs):
            out[...] = packed[:groups, :, h * width:(h + 1) * width]


def gather_points(tiles, dest, field, start, size, groups, per_group, pieces):
    rows, cols = field.shape[1:]
    parts = cols // LANES
    width = per_group // pieces
    return pl.pallas_call(
        gather_kernel,
        grid_spec=pltpu.PrefetchScalarGridSpec(
            num_scalar_prefetch=1,
            grid=(rows // SUBLANES,),
            in_specs=[
                pl.BlockSpec(
                    (pl.Element(size), pl.Element(SUBLANES), pl.Element(cols)),
                    lambda g, *_: (start, g * SUBLANES, 0),
                ),
                pl.BlockSpec((SUBLANES * parts, LANES), lambda g, *_: (g, 0)),
            ],
            out_specs=[
                pl.BlockSpec((groups, size, width), lambda g, *_: (0, 0, 0))
                for _ in range(pieces)
            ],
            scratch_shapes=[
                pltpu.VMEM((groups + 1, size, per_group), jnp.bfloat16),
                pltpu.VMEM((parts, size * SUBLANES, LANES), jnp.float32),
                pltpu.VMEM((size, LANES), jnp.bfloat16),
            ],
        ),
        out_shape=[
            jax.ShapeDtypeStruct((groups, size, width), jnp.bfloat16) for _ in range(pieces)
        ],
        compiler_params=pltpu.CompilerParams(vmem_limit_bytes=VMEM_BYTES),
        cost_estimate=pl.CostEstimate(
            flops=size * rows * cols * 4 * LANES,
            bytes_accessed=size * rows * cols * 6,
            transcendentals=0,
        ),
        name="gather_points",
    )(tiles, field, dest)


def scatter_kernel(tile_ref, field_ref, dest_ref, first_ref, second_ref, *refs):
    out_ref, packed, rows_of = refs[-3:]
    size, rows, cols = field_ref.shape
    parts = cols // LANES
    width = first_ref.shape[2]
    per_group = packed.shape[2] // LANES
    last_tile = packed.shape[0] * per_group - 1
    first_block = pl.program_id(0) * rows * parts

    @pl.when(pl.program_id(0) == 0)
    def _():
        packed[:, :, :width] = first_ref[...]
        packed[:, :, width:] = second_ref[...]

    for b in range(rows * parts):
        r, t = b // parts, b % parts
        tile = jnp.minimum(tile_ref[first_block + b], last_tile)
        following = jnp.minimum(tile + 1, last_tile)
        values = jnp.concatenate(
            [packed[tile_place(tile, per_group)], packed[tile_place(following, per_group)]],
            axis=1,
        )
        pick = selection(dest_ref[pl.ds(b, 1), :], LANES)
        rows_of[t, pl.ds(r, size, stride=rows), :] = jnp.dot(
            values, pick, preferred_element_type=jnp.float32
        )
    for t in range(parts):
        at = (slice(None), slice(None), slice(t * LANES, (t + 1) * LANES))
        out_ref[at] = field_ref[at] + rows_of[t].reshape(size, rows, LANES)


def scatter_points(tiles, dest, field, first, second, start):
    groups, size, width = second.shape
    rows, cols = field.shape[1:]
    parts = cols // LANES
    field_spec = pl.BlockSpec(
        (pl.Element(size), pl.Element(SUBLANES), pl.Element(cols)),
        lambda g, *_: (start, g * SUBLANES, 0),
    )
    return pl.pallas_call(
        scatter_kernel,
        grid_spec=pltpu.PrefetchScalarGridSpec(
            num_scalar_prefetch=1,
            grid=(rows // SUBLANES,),
            in_specs=[
                field_spec,
                pl.BlockSpec((SUBLANES * parts, LANES), lambda g, *_: (g, 0)),
                pl.BlockSpec(
                    (pl.Element(groups), pl.Element(size), pl.Element(width)),
                    lambda g, *_: (0, start, 0),
                ),
                pl.BlockSpec((groups, size, width), lambda g, *_: (0, 0, 0)),
            ],
            out_specs=field_spec,
            scratch_shapes=[
                pltpu.VMEM((groups, size, 2 * width), jnp.bfloat16),
                pltpu.VMEM((parts, size * SUBLANES, LANES), jnp.float32),
            ],
        ),
        out_shape=jax.ShapeDtypeStruct(field.shape, jnp.float32),
        input_output_aliases={1: 0},
        compiler_params=pltpu.CompilerParams(vmem_limit_bytes=VMEM_BYTES),
        cost_estimate=pl.CostEstimate(
            flops=size * rows * cols * 4 * LANES,
            bytes_accessed=size * rows * cols * 10,
            transcendentals=0,
        ),
        name="scatter_points",
    )(tiles, field, dest, first, second)


def source_kernel(counts, out_counts, groups, mix_in, mix_out, growth, damping, weight, *refs):
    ins, outs, points = refs[:len(counts)], refs[len(counts):-1], refs[-1]
    total = sum(counts)
    for g in range(groups):
        at = g * total
        for ref, count in zip(ins, counts):
            points[at:at + count, :] = ref[g * count:(g + 1) * count, :]
            at += count
    rounded = points[...]
    hidden = jnp.dot(mix_in[...], rounded, preferred_element_type=jnp.float32)
    square = (hidden * hidden).astype(jnp.bfloat16)
    transfer = jnp.dot(mix_out[...], square, preferred_element_type=jnp.float32)
    energy = rounded.astype(jnp.float32)
    mean_energy = jnp.sum(weight[...] * energy, axis=0, keepdims=True)
    increment = 0.5 * (
        growth[...] * energy
        + 0.25 * transfer
        - damping[...] * energy * (mean_energy / (1.0 + mean_energy))
    )
    increment = increment.astype(jnp.bfloat16)
    for g in range(groups):
        at = g * total
        for ref, count in zip(outs, out_counts):
            ref[g * count:(g + 1) * count, :] = increment[at:at + count, :]
            at += count


def source_terms(pieces, counts, out_counts, slots, starts, groups, mix_in, mix_out, columns):
    comp_count = mix_in.shape[0]
    width = min(512, slots)
    fixed = lambda g: (0, 0)
    if len(counts) == 1:
        counts, out_counts, groups = [comp_count], [comp_count], 1

    def moving(start):
        return lambda g: (0, start // width + g)

    return pl.pallas_call(
        functools.partial(source_kernel, counts, out_counts, groups),
        grid=(slots // width,),
        in_specs=[pl.BlockSpec(mix_in.shape, fixed)] * 2
        + [pl.BlockSpec((comp_count, 1), fixed)] * 3
        + [
            pl.BlockSpec((groups * count, width), moving(start))
            for count, start in zip(counts, starts)
        ],
        out_specs=[pl.BlockSpec((groups * count, width), moving(0)) for count in out_counts],
        out_shape=[
            jax.ShapeDtypeStruct((groups * count, slots), jnp.bfloat16) for count in out_counts
        ],
        scratch_shapes=[pltpu.VMEM((comp_count, width), jnp.bfloat16)],
        compiler_params=pltpu.CompilerParams(vmem_limit_bytes=VMEM_BYTES),
        cost_estimate=pl.CostEstimate(
            flops=4 * comp_count * comp_count * slots,
            bytes_accessed=4 * comp_count * (comp_count + slots),
            transcendentals=0,
        ),
        name="source_terms",
    )(mix_in, mix_out, *columns, *pieces)


def edge_rows(make, axis):
    count = lax.axis_size(axis)
    forward = [(i, i + 1) for i in range(count - 1)]
    backward = [(target, source) for source, target in forward]
    return lax.ppermute(make(True), axis, forward), lax.ppermute(make(False), axis, backward)


def mask_planes(sea_mask, low, high, strip):
    blank = jnp.zeros((strip - low.shape[0], sea_mask.shape[1]), jnp.float32)
    inner = sea_mask.astype(jnp.float32)
    mask = jnp.concatenate([blank, low, inner, high, blank], axis=0)
    row = jnp.zeros_like(mask[:1])
    col = jnp.zeros_like(mask[:, :1])
    left = jnp.concatenate([col, mask[:, :-1]], axis=1)
    right = jnp.concatenate([mask[:, 1:], col], axis=1)
    above = jnp.concatenate([row, mask[:-1]], axis=0)
    below = jnp.concatenate([mask[1:], row], axis=0)
    return jnp.stack([mask, left, right, above, below, mask * left, mask * right])


def slot_table(sea_mask):
    cells = sea_mask.reshape(-1, LANES).astype(jnp.float32)
    upto = jnp.triu(jnp.ones((LANES, LANES), jnp.float32))
    rank = jnp.dot(cells, upto, precision=lax.Precision.HIGHEST)
    count = rank[:, -1]
    blocks = cells.shape[0]
    before = jnp.tril(jnp.ones((blocks, blocks), jnp.float32), -1)
    offset = jnp.dot(before, count, precision=lax.Precision.HIGHEST)
    offset = jnp.append(offset, offset[-1] + count[-1]).astype(jnp.int32)
    tiles = offset // LANES
    offset = (offset - tiles * LANES)[:-1]
    rank = rank.astype(jnp.int32) - 1 + offset[:, None]
    return tiles, jnp.where(cells > 0.0, rank, -1)


def local(
    spectrum, sea_mask, point_index, band_counts, sub_counts, mix_in, mix_out, growth, damping
):
    freq_count, dir_count, row_count, lon_count = spectrum.shape
    comp_count = freq_count * dir_count
    all_count = growth.shape[0] * growth.shape[1]
    groups = lax.axis_size("comp")
    per_group = point_index.shape[1] // groups
    half = per_group // 2
    sizes = chunk_sizes(comp_count, (2, 3, 4))
    starts = [sum(sizes[:j]) for j in range(len(sizes))]
    out_sizes = chunk_sizes(comp_count, (7, 2))
    out_starts = [sum(out_sizes[:j]) for j in range(len(out_sizes))]

    field = spectrum.reshape(comp_count, row_count, lon_count)

    def first_edge(last):
        at = slice(row_count - NSUB, row_count) if last else slice(0, NSUB)
        mask_rows = sea_mask[at].astype(jnp.float32)
        return jnp.concatenate([field[:sizes[0], at], mask_rows[None]], axis=0)

    def later_edge(last):
        at = slice(row_count - NSUB, row_count) if last else slice(0, NSUB)
        return field[sizes[0]:, at]

    edges = [edge_rows(first_edge, "lat")]
    if len(sizes) > 1:
        edges.append(edge_rows(later_edge, "lat"))
    mask_low, mask_high = edges[0][0][sizes[0]], edges[0][1][sizes[0]]

    freq_index = lax.axis_index("comp") * freq_count + jnp.arange(freq_count, dtype=jnp.int32)
    courant_x, courant_y = courant(freq_index, sub_counts, dir_count)
    courant_x, courant_y = courant_x.reshape(-1), courant_y.reshape(-1)
    scalars = (
        jnp.abs(courant_x),
        jnp.abs(courant_y),
        (courant_x < 0.0).astype(jnp.int32) + 2 * (courant_y < 0.0).astype(jnp.int32),
        jnp.repeat(sub_counts, dir_count),
    )
    tiles, dest = slot_table(sea_mask)
    masks = mask_planes(sea_mask, mask_low, mask_high, SUBLANES)

    done = []

    def exchange(piece):
        if done:
            piece, done[-1] = lax.optimization_barrier((piece, done[-1]))
        done.append(lax.all_to_all(piece, "comp", split_axis=0, concat_axis=0, tiled=True))
        return len(done) - 1

    def as_rows(piece):
        return piece.reshape(groups * piece.shape[1], piece.shape[2])

    chain, arrived = [], [[], []]
    for j, (start, size) in enumerate(zip(starts, sizes)):
        low, high = edges[min(j, 1)]
        low_start = 0 if j == 0 else start - sizes[0]
        moved = propagate(scalars, field, low, high, masks, start, size, low_start, chain)
        pieces = 2 if j == len(sizes) - 1 else 1
        packed = gather_points(tiles, dest, moved, start, size, groups, per_group, pieces)
        chain = [moved, packed[0]]
        packed = [exchange(piece) for piece in packed]
        for h in range(2):
            arrived[h].append((packed[h % pieces], h * half if pieces == 1 else 0))

    columns = [
        column.reshape(all_count, 1)
        for column in (growth, damping, freq_weights(*growth.shape))
    ]
    back = []
    for h in range(2):
        parts_out = [comp_count] if h == 0 else out_sizes
        increments = source_terms(
            [as_rows(done[at]) for at, _ in arrived[h]], sizes, parts_out, half,
            [lane for _, lane in arrived[h]], groups, mix_in, mix_out, columns,
        )
        for rows, size in zip(increments, parts_out):
            back.append(exchange(rows.reshape(groups, size, half)))

    for start, at in zip(out_starts, back[1:]):
        moved = scatter_points(tiles, dest, moved, done[back[0]], done[at], start)
    return moved.reshape(spectrum.shape)


def solution(mesh):
    return jax.shard_map(
        local,
        mesh=mesh,
        in_specs=(
            P("comp", None, "lat", None),
            P("lat", None),
            P("lat", None),
            P("lat"),
            P("comp"),
            P(),
            P(),
            P(),
            P(),
        ),
        out_specs=P("comp", None, "lat", None),
        check_vma=False,
    )
```

```python
import functools

import jax
import jax.numpy as jnp
import numpy as np
from jax import lax
from jax.experimental import pallas as pl
from jax.experimental.pallas import tpu as pltpu
from jax.sharding import PartitionSpec as P

NSUB = 4
SUBLANES = 8
LANES = 128
VMEM_BYTES = 56 * 1024 * 1024


def chunk_sizes(comp_count, shares):
    if comp_count % 16:
        return [comp_count]
    units, total = comp_count // 16, sum(shares)
    bounds = [units * sum(shares[:j]) // total for j in range(len(shares) + 1)]
    return [16 * (high - low) for low, high in zip(bounds, bounds[1:]) if high > low]


def wave_speeds(freq_index, sub_steps):
    group_speed = 1.4 * jnp.power(0.93, freq_index.astype(jnp.float32))
    return group_speed / sub_steps.astype(jnp.float32)


def direction_table(dir_count):
    angles = (np.arange(dir_count, dtype=np.float32) + np.float32(0.5)) * np.float32(
        2.0 * np.pi / dir_count
    )
    return [part(angles.astype(np.float64)).astype(np.float32) for part in (np.cos, np.sin)]


def freq_weights(freq_count, dir_count):
    raw_weight = jnp.power(1.1, jnp.arange(freq_count, dtype=jnp.float32))
    raw_weight = raw_weight / (dir_count * jnp.sum(raw_weight))
    return jnp.repeat(raw_weight, dir_count)


def propagate_kernel(
    start,
    speed_ref, steps_ref, cos_ref, sin_ref,
    spec_ref, low_ref, high_ref, mask_ref,
    *refs,
):
    out_ref, keep, even, odd = refs[-4:]
    block, rows, cols = spec_ref.shape
    halo = low_ref.shape[1]
    strips = rows // SUBLANES + 2
    parts = cols // LANES
    row_id = lax.broadcasted_iota(jnp.int32, (SUBLANES, LANES), 0)
    col_id = lax.broadcasted_iota(jnp.int32, (SUBLANES, LANES), 1)

    def strip_rows(s):
        return pl.ds(s * SUBLANES, SUBLANES)

    def run(i, ax, ay, steps, x_up, y_up):
        blank = jnp.zeros((SUBLANES - halo, cols), jnp.float32)
        for s in range(strips):
            keep[strip_rows(s), :] = (
                1.0
                - ax * mask_ref[2 if x_up else 1, strip_rows(s), :]
                - ay * mask_ref[4 if y_up else 3, strip_rows(s), :]
            )
            if s == 0:
                value = jnp.concatenate([blank, low_ref[i]], axis=0)
            elif s == strips - 1:
                value = jnp.concatenate([high_ref[i], blank], axis=0)
            else:
                value = spec_ref[i, strip_rows(s - 1), :]
            even[strip_rows(s), :] = value * mask_ref[0, strip_rows(s), :]

        edge_row = row_id == (0 if y_up else SUBLANES - 1)
        edge_col = col_id == (0 if x_up else LANES - 1)
        nothing = jnp.zeros((SUBLANES, LANES), jnp.float32)

        def substep(source, target):
            before_y = [nothing] * parts
            for s in range(strips) if y_up else range(strips - 1, -1, -1):
                before_x = nothing
                for t in range(parts) if x_up else range(parts - 1, -1, -1):
                    at = (strip_rows(s), slice(t * LANES, (t + 1) * LANES))
                    value = source[at]
                    turned = pltpu.roll(value, 1 if y_up else SUBLANES - 1, 0)
                    upwind_y = jnp.where(edge_row, before_y[t], turned)
                    before_y[t] = turned
                    turned = pltpu.roll(value, 1 if x_up else LANES - 1, 1)
                    upwind_x = jnp.where(edge_col, before_x, turned)
                    before_x = turned
                    target[at] = value * keep[at] + mask_ref[(0, *at)] * (
                        ax * upwind_x + ay * upwind_y
                    )

        def pair(_, carry):
            substep(even, odd)
            substep(odd, even)
            return carry

        lax.fori_loop(0, steps // 2, pair, 0)

        @pl.when(lax.rem(steps, 2) == 1)
        def _():
            substep(even, odd)
            out_ref[i] = odd[pl.ds(SUBLANES, rows), :]

        @pl.when(lax.rem(steps, 2) == 0)
        def _():
            out_ref[i] = even[pl.ds(SUBLANES, rows), :]

    def component(i, carry):
        at = start + pl.program_id(0) * block + i
        freq = at // cos_ref.shape[0]
        toward = at - freq * cos_ref.shape[0]
        cx, cy = speed_ref[freq] * cos_ref[toward], speed_ref[freq] * sin_ref[toward]
        steps = steps_ref[freq]
        for x_up in (True, False):
            for y_up in (True, False):

                @pl.when(((cx >= 0.0) == x_up) & ((cy >= 0.0) == y_up))
                def _():
                    run(i, cx if x_up else -cx, cy if y_up else -cy, steps, x_up, y_up)

        return carry

    lax.fori_loop(0, block, component, 0)


def propagate(scalars, spectrum, low, high, masks, start, size, low_start, chain):
    comp_count, rows, cols = spectrum.shape
    halo = low.shape[1]
    block = next(
        n for n in range(min(16, size), 0, -1)
        if size % n == 0 and start % n == 0 and low_start % n == 0
    )
    ext = masks.shape[1]
    cells = size * rows * cols
    return pl.pallas_call(
        functools.partial(propagate_kernel, start),
        grid_spec=pltpu.PrefetchScalarGridSpec(
            num_scalar_prefetch=4,
            grid=(size // block,),
            in_specs=[
                pl.BlockSpec((block, rows, cols), lambda g, *_: (start // block + g, 0, 0)),
                pl.BlockSpec((block, halo, cols), lambda g, *_: (low_start // block + g, 0, 0)),
                pl.BlockSpec((block, halo, cols), lambda g, *_: (low_start // block + g, 0, 0)),
                pl.BlockSpec(masks.shape, lambda g, *_: (0, 0, 0)),
            ]
            + [pl.BlockSpec(memory_space=pl.ANY) for _ in chain],
            out_specs=pl.BlockSpec((block, rows, cols), lambda g, *_: (start // block + g, 0, 0)),
            scratch_shapes=[pltpu.VMEM((ext, cols), jnp.float32) for _ in range(3)],
        ),
        out_shape=jax.ShapeDtypeStruct((comp_count, rows, cols), jnp.float32),
        input_output_aliases={8: 0} if chain else {},
        compiler_params=pltpu.CompilerParams(vmem_limit_bytes=VMEM_BYTES),
        cost_estimate=pl.CostEstimate(
            flops=cells * 30, bytes_accessed=cells * 8, transcendentals=0
        ),
        name="propagate",
    )(*scalars, spectrum, low, high, masks, *chain)


def selection(dest_row):
    slot = lax.broadcasted_iota(jnp.int32, (LANES, LANES), 0)
    slot = slot.astype(jnp.float32).astype(jnp.bfloat16)
    one, zero = jnp.ones((), jnp.bfloat16), jnp.zeros((), jnp.bfloat16)
    return jnp.where(slot == dest_row.astype(jnp.float32).astype(jnp.bfloat16), one, zero)


def tile_of(offset):
    return lax.shift_right_logical(offset, LANES.bit_length() - 1)


def lane_of(offset):
    return jnp.bitwise_and(offset, LANES - 1)


def tile_place(tile, per_group):
    lane = lax.rem(tile, per_group) * LANES
    return tile // per_group, slice(None), pl.ds(pl.multiple_of(lane, LANES), LANES)


def gather_kernel(offset_ref, field_ref, dest_ref, *refs):
    outs, (packed, rows_of, open_tile) = refs[:-3], refs[-3:]
    size, rows, cols = field_ref.shape
    parts = cols // LANES
    per_group = packed.shape[2] // LANES
    step = pl.program_id(0)
    first_block = step * rows * parts

    @pl.when(step == 0)
    def _():
        packed[...] = jnp.zeros_like(packed)
        open_tile[...] = jnp.zeros_like(open_tile)

    for t in range(parts):
        rows_of[t] = field_ref[:, :, t * LANES:(t + 1) * LANES].reshape(size * rows, LANES)

    lane_id = lax.broadcasted_iota(jnp.int32, (size, LANES), 1)
    begun = open_tile[...]
    for b in range(rows * parts):
        r, t = b // parts, b % parts
        values = rows_of[t, pl.ds(r, size, stride=rows), :].astype(jnp.bfloat16)
        placed = lax.dot_general(
            values, selection(dest_ref[pl.ds(b, 1), :]), (((1,), (1,)), ((), ())),
            preferred_element_type=jnp.float32,
        )
        offset, following = offset_ref[first_block + b], offset_ref[first_block + b + 1]
        full = jnp.where(lane_id >= lane_of(offset), placed, begun)
        packed[tile_place(tile_of(offset), per_group)] = full.astype(jnp.bfloat16)
        begun = jnp.where(tile_of(following) > tile_of(offset), placed, full)
    open_tile[...] = begun

    @pl.when(step == pl.num_programs(0) - 1)
    def _():
        tile = tile_of(offset_ref[first_block + rows * parts])
        packed[tile_place(tile, per_group)] = begun.astype(jnp.bfloat16)
        groups, _, width = outs[0].shape
        for h, out in enumerate(outs):
            out[...] = packed[:groups, :, h * width:(h + 1) * width]


def gather_points(offsets, dest, field, start, size, groups, per_group, pieces):
    rows, cols = field.shape[1:]
    parts = cols // LANES
    width = per_group // pieces
    return pl.pallas_call(
        gather_kernel,
        grid_spec=pltpu.PrefetchScalarGridSpec(
            num_scalar_prefetch=1,
            grid=(rows // SUBLANES,),
            in_specs=[
                pl.BlockSpec(
                    (pl.Element(size), pl.Element(SUBLANES), pl.Element(cols)),
                    lambda g, *_: (start, g * SUBLANES, 0),
                ),
                pl.BlockSpec((SUBLANES * parts, LANES), lambda g, *_: (g, 0)),
            ],
            out_specs=[
                pl.BlockSpec((groups, size, width), lambda g, *_: (0, 0, 0))
                for _ in range(pieces)
            ],
            scratch_shapes=[
                pltpu.VMEM((groups + 1, size, per_group), jnp.bfloat16),
                pltpu.VMEM((parts, size * SUBLANES, LANES), jnp.float32),
                pltpu.VMEM((size, LANES), jnp.float32),
            ],
        ),
        out_shape=[
            jax.ShapeDtypeStruct((groups, size, width), jnp.bfloat16) for _ in range(pieces)
        ],
        compiler_params=pltpu.CompilerParams(vmem_limit_bytes=VMEM_BYTES),
        cost_estimate=pl.CostEstimate(
            flops=size * rows * cols * 2 * LANES,
            bytes_accessed=size * rows * cols * 6,
            transcendentals=0,
        ),
        name="gather_points",
    )(offsets, field, dest)


def scatter_kernel(offset_ref, field_ref, dest_ref, first_ref, second_ref, *refs):
    out_ref, packed, rows_of = refs[-3:]
    size, rows, cols = field_ref.shape
    parts = cols // LANES
    width = first_ref.shape[2]
    per_group = packed.shape[2] // LANES
    last_tile = packed.shape[0] * per_group - 1
    first_block = pl.program_id(0) * rows * parts

    @pl.when(pl.program_id(0) == 0)
    def _():
        packed[:, :, :width] = first_ref[...]
        packed[:, :, width:] = second_ref[...]

    lane_id = lax.broadcasted_iota(jnp.int32, (size, LANES), 1)
    lane_id = lane_id.astype(jnp.float32).astype(jnp.bfloat16)
    for b in range(rows * parts):
        r, t = b // parts, b % parts
        offset = offset_ref[first_block + b]
        tile = jnp.minimum(tile_of(offset), last_tile)
        following = jnp.minimum(tile + 1, last_tile)
        values = jnp.where(
            lane_id >= lane_of(offset).astype(jnp.float32).astype(jnp.bfloat16),
            packed[tile_place(tile, per_group)],
            packed[tile_place(following, per_group)],
        )
        rows_of[t, pl.ds(r, size, stride=rows), :] = jnp.dot(
            values, selection(dest_ref[pl.ds(b, 1), :]), preferred_element_type=jnp.float32
        )
    for t in range(parts):
        at = (slice(None), slice(None), slice(t * LANES, (t + 1) * LANES))
        out_ref[at] = field_ref[at] + rows_of[t].reshape(size, rows, LANES)


def scatter_points(offsets, dest, field, first, second, start):
    groups, size, width = second.shape
    rows, cols = field.shape[1:]
    parts = cols // LANES
    field_spec = pl.BlockSpec(
        (pl.Element(size), pl.Element(SUBLANES), pl.Element(cols)),
        lambda g, *_: (start, g * SUBLANES, 0),
    )
    return pl.pallas_call(
        scatter_kernel,
        grid_spec=pltpu.PrefetchScalarGridSpec(
            num_scalar_prefetch=1,
            grid=(rows // SUBLANES,),
            in_specs=[
                field_spec,
                pl.BlockSpec((SUBLANES * parts, LANES), lambda g, *_: (g, 0)),
                pl.BlockSpec(
                    (pl.Element(groups), pl.Element(size), pl.Element(width)),
                    lambda g, *_: (0, start, 0),
                ),
                pl.BlockSpec((groups, size, width), lambda g, *_: (0, 0, 0)),
            ],
            out_specs=field_spec,
            scratch_shapes=[
                pltpu.VMEM((groups, size, 2 * width), jnp.bfloat16),
                pltpu.VMEM((parts, size * SUBLANES, LANES), jnp.float32),
            ],
        ),
        out_shape=jax.ShapeDtypeStruct(field.shape, jnp.float32),
        input_output_aliases={1: 0},
        compiler_params=pltpu.CompilerParams(vmem_limit_bytes=VMEM_BYTES),
        cost_estimate=pl.CostEstimate(
            flops=size * rows * cols * 2 * LANES,
            bytes_accessed=size * rows * cols * 10,
            transcendentals=0,
        ),
        name="scatter_points",
    )(offsets, field, dest, first, second)


def source_kernel(counts, out_counts, groups, mix_in, mix_out, growth, damping, weight, *refs):
    ins, outs, points = refs[:len(counts)], refs[len(counts):-1], refs[-1]
    total = sum(counts)
    for g in range(groups):
        at = g * total
        for ref, count in zip(ins, counts):
            points[at:at + count, :] = ref[g * count:(g + 1) * count, :]
            at += count
    rounded = points[...]
    hidden = jnp.dot(mix_in[...], rounded, preferred_element_type=jnp.float32)
    square = (hidden * hidden).astype(jnp.bfloat16)
    transfer = jnp.dot(mix_out[...], square, preferred_element_type=jnp.float32)
    energy = rounded.astype(jnp.float32)
    mean_energy = jnp.sum(weight[...] * energy, axis=0, keepdims=True)
    increment = 0.5 * (
        growth[...] * energy
        + 0.25 * transfer
        - damping[...] * energy * (mean_energy / (1.0 + mean_energy))
    )
    increment = increment.astype(jnp.bfloat16)
    for g in range(groups):
        at = g * total
        for ref, count in zip(outs, out_counts):
            ref[g * count:(g + 1) * count, :] = increment[at:at + count, :]
            at += count


def source_terms(pieces, counts, out_counts, slots, starts, groups, mix_in, mix_out, columns):
    comp_count = mix_in.shape[0]
    width = min(512, slots)
    fixed = lambda g: (0, 0)
    if len(counts) == 1:
        counts, out_counts, groups = [comp_count], [comp_count], 1

    def moving(start):
        return lambda g: (0, start // width + g)

    return pl.pallas_call(
        functools.partial(source_kernel, counts, out_counts, groups),
        grid=(slots // width,),
        in_specs=[pl.BlockSpec(mix_in.shape, fixed)] * 2
        + [pl.BlockSpec((comp_count, 1), fixed)] * 3
        + [
            pl.BlockSpec((groups * count, width), moving(start))
            for count, start in zip(counts, starts)
        ],
        out_specs=[pl.BlockSpec((groups * count, width), moving(0)) for count in out_counts],
        out_shape=[
            jax.ShapeDtypeStruct((groups * count, slots), jnp.bfloat16) for count in out_counts
        ],
        scratch_shapes=[pltpu.VMEM((comp_count, width), jnp.bfloat16)],
        compiler_params=pltpu.CompilerParams(vmem_limit_bytes=VMEM_BYTES),
        cost_estimate=pl.CostEstimate(
            flops=4 * comp_count * comp_count * slots,
            bytes_accessed=4 * comp_count * (comp_count + slots),
            transcendentals=0,
        ),
        name="source_terms",
    )(mix_in, mix_out, *columns, *pieces)


def edge_rows(make, axis):
    count = lax.axis_size(axis)
    forward = [(i, i + 1) for i in range(count - 1)]
    backward = [(target, source) for source, target in forward]
    return lax.ppermute(make(True), axis, forward), lax.ppermute(make(False), axis, backward)


def mask_planes(sea_mask, low, high, strip):
    blank = jnp.zeros((strip - low.shape[0], sea_mask.shape[1]), jnp.float32)
    inner = sea_mask.astype(jnp.float32)
    mask = jnp.concatenate([blank, low, inner, high, blank], axis=0)
    row = jnp.zeros_like(mask[:1])
    col = jnp.zeros_like(mask[:, :1])
    left = jnp.concatenate([col, mask[:, :-1]], axis=1)
    right = jnp.concatenate([mask[:, 1:], col], axis=1)
    above = jnp.concatenate([row, mask[:-1]], axis=0)
    below = jnp.concatenate([mask[1:], row], axis=0)
    return jnp.stack([mask, left, right, above, below])


def slot_table(sea_mask):
    cells = sea_mask.reshape(-1, LANES).astype(jnp.float32)
    upto = jnp.triu(jnp.ones((LANES, LANES), jnp.float32))
    rank = jnp.dot(cells, upto, precision=lax.Precision.HIGHEST)
    count = rank[:, -1]
    blocks = cells.shape[0]
    before = jnp.tril(jnp.ones((blocks, blocks), jnp.float32), -1)
    offset = jnp.dot(before, count, precision=lax.Precision.HIGHEST)
    offset = jnp.append(offset, offset[-1] + count[-1]).astype(jnp.int32)
    place = lane_of(rank.astype(jnp.int32) - 1 + offset[:-1, None])
    return offset, jnp.where(cells > 0.0, place, -1)


def local(
    spectrum, sea_mask, point_index, band_counts, sub_counts, mix_in, mix_out, growth, damping
):
    freq_count, dir_count, row_count, lon_count = spectrum.shape
    comp_count = freq_count * dir_count
    all_count = growth.shape[0] * growth.shape[1]
    groups = lax.axis_size("comp")
    per_group = point_index.shape[1] // groups
    half = per_group // 2
    sizes = chunk_sizes(comp_count, (1, 1, 1))
    starts = [sum(sizes[:j]) for j in range(len(sizes))]
    out_sizes = chunk_sizes(comp_count, (7, 2))
    out_starts = [sum(out_sizes[:j]) for j in range(len(out_sizes))]

    field = spectrum.reshape(comp_count, row_count, lon_count)

    def first_edge(last):
        at = slice(row_count - NSUB, row_count) if last else slice(0, NSUB)
        mask_rows = sea_mask[at].astype(jnp.float32)
        return jnp.concatenate([field[:sizes[0], at], mask_rows[None]], axis=0)

    def later_edge(last):
        at = slice(row_count - NSUB, row_count) if last else slice(0, NSUB)
        return field[sizes[0]:, at]

    edges = [edge_rows(first_edge, "lat")]
    if len(sizes) > 1:
        edges.append(edge_rows(later_edge, "lat"))
    mask_low, mask_high = edges[0][0][sizes[0]], edges[0][1][sizes[0]]

    freq_index = lax.axis_index("comp") * freq_count + jnp.arange(freq_count, dtype=jnp.int32)
    scalars = (wave_speeds(freq_index, sub_counts), sub_counts, *direction_table(dir_count))
    offsets, dest = slot_table(sea_mask)
    masks = mask_planes(sea_mask, mask_low, mask_high, SUBLANES)

    done = []

    def exchange(piece):
        if done:
            piece, done[-1] = lax.optimization_barrier((piece, done[-1]))
        done.append(lax.all_to_all(piece, "comp", split_axis=0, concat_axis=0, tiled=True))
        return len(done) - 1

    def as_rows(piece):
        return piece.reshape(groups * piece.shape[1], piece.shape[2])

    chain, arrived = [], [[], []]
    for j, (start, size) in enumerate(zip(starts, sizes)):
        low, high = edges[min(j, 1)]
        low_start = 0 if j == 0 else start - sizes[0]
        moved = propagate(scalars, field, low, high, masks, start, size, low_start, chain)
        pieces = 2 if j == len(sizes) - 1 else 1
        packed = gather_points(offsets, dest, moved, start, size, groups, per_group, pieces)
        chain = [moved, packed[0]]
        packed = [exchange(piece) for piece in packed]
        for h in range(2):
            arrived[h].append((packed[h % pieces], h * half if pieces == 1 else 0))

    columns = [
        column.reshape(all_count, 1)
        for column in (growth, damping, freq_weights(*growth.shape))
    ]
    back = []
    for h in range(2):
        parts_out = [comp_count] if h == 0 else out_sizes
        increments = source_terms(
            [as_rows(done[at]) for at, _ in arrived[h]], sizes, parts_out, half,
            [lane for _, lane in arrived[h]], groups, mix_in, mix_out, columns,
        )
        for rows, size in zip(increments, parts_out):
            back.append(exchange(rows.reshape(groups, size, half)))

    for start, at in zip(out_starts, back[1:]):
        moved = scatter_points(offsets, dest, moved, done[back[0]], done[at], start)
    return moved.reshape(spectrum.shape)


def solution(mesh):
    return jax.shard_map(
        local,
        mesh=mesh,
        in_specs=(
            P("comp", None, "lat", None),
            P("lat", None),
            P("lat", None),
            P("lat"),
            P("comp"),
            P(),
            P(),
            P(),
            P(),
        ),
        out_specs=P("comp", None, "lat", None),
        check_vma=False,
    )
```

```python
import functools

import jax
import jax.numpy as jnp
import numpy as np
from jax import lax
from jax.experimental import pallas as pl
from jax.experimental.pallas import tpu as pltpu
from jax.sharding import PartitionSpec as P

NSUB = 4
SUBLANES = 8
LANES = 128
BLOCK = 256
VMEM_BYTES = 56 * 1024 * 1024


def chunk_sizes(comp_count, shares):
    if comp_count % 16:
        return [comp_count]
    units, total = comp_count // 16, sum(shares)
    bounds = [units * sum(shares[:j]) // total for j in range(len(shares) + 1)]
    return [16 * (high - low) for low, high in zip(bounds, bounds[1:]) if high > low]


def wave_speeds(freq_index, sub_steps):
    group_speed = 1.4 * jnp.power(0.93, freq_index.astype(jnp.float32))
    return group_speed / sub_steps.astype(jnp.float32)


def direction_table(dir_count):
    angles = (np.arange(dir_count, dtype=np.float32) + np.float32(0.5)) * np.float32(
        2.0 * np.pi / dir_count
    )
    return [part(angles.astype(np.float64)).astype(np.float32) for part in (np.cos, np.sin)]


def freq_weights(freq_count, dir_count):
    raw_weight = jnp.power(1.1, jnp.arange(freq_count, dtype=jnp.float32))
    raw_weight = raw_weight / (dir_count * jnp.sum(raw_weight))
    return jnp.repeat(raw_weight, dir_count)


def propagate_kernel(
    start,
    speed_ref, steps_ref, cos_ref, sin_ref,
    spec_ref, low_ref, high_ref, mask_ref,
    *refs,
):
    out_ref, keep, even, odd = refs[-4:]
    block, rows, cols = spec_ref.shape
    halo = low_ref.shape[1]
    strips = rows // SUBLANES + 2
    parts = cols // LANES
    row_id = lax.broadcasted_iota(jnp.int32, (SUBLANES, LANES), 0)
    col_id = lax.broadcasted_iota(jnp.int32, (SUBLANES, LANES), 1)

    def strip_rows(s):
        return pl.ds(s * SUBLANES, SUBLANES)

    def run(i, ax, ay, steps, x_up, y_up):
        blank = jnp.zeros((SUBLANES - halo, cols), jnp.float32)
        for s in range(strips):
            keep[strip_rows(s), :] = (
                1.0
                - ax * mask_ref[2 if x_up else 1, strip_rows(s), :]
                - ay * mask_ref[4 if y_up else 3, strip_rows(s), :]
            )
            if s == 0:
                value = jnp.concatenate([blank, low_ref[i]], axis=0)
            elif s == strips - 1:
                value = jnp.concatenate([high_ref[i], blank], axis=0)
            else:
                value = spec_ref[i, strip_rows(s - 1), :]
            even[strip_rows(s), :] = value * mask_ref[0, strip_rows(s), :]

        edge_row = row_id == (0 if y_up else SUBLANES - 1)
        edge_col = col_id == (0 if x_up else LANES - 1)
        nothing = jnp.zeros((SUBLANES, LANES), jnp.float32)

        def substep(source, target):
            before_y = [nothing] * parts
            for s in range(strips) if y_up else range(strips - 1, -1, -1):
                before_x = nothing
                for t in range(parts) if x_up else range(parts - 1, -1, -1):
                    at = (strip_rows(s), slice(t * LANES, (t + 1) * LANES))
                    value = source[at]
                    turned = pltpu.roll(value, 1 if y_up else SUBLANES - 1, 0)
                    upwind_y = jnp.where(edge_row, before_y[t], turned)
                    before_y[t] = turned
                    turned = pltpu.roll(value, 1 if x_up else LANES - 1, 1)
                    upwind_x = jnp.where(edge_col, before_x, turned)
                    before_x = turned
                    target[at] = value * keep[at] + mask_ref[(0, *at)] * (
                        ax * upwind_x + ay * upwind_y
                    )

        def pair(_, carry):
            substep(even, odd)
            substep(odd, even)
            return carry

        lax.fori_loop(0, steps // 2, pair, 0)

        @pl.when(lax.rem(steps, 2) == 1)
        def _():
            substep(even, odd)
            out_ref[i] = odd[pl.ds(SUBLANES, rows), :]

        @pl.when(lax.rem(steps, 2) == 0)
        def _():
            out_ref[i] = even[pl.ds(SUBLANES, rows), :]

    def component(i, carry):
        at = start + pl.program_id(0) * block + i
        freq = at // cos_ref.shape[0]
        toward = at - freq * cos_ref.shape[0]
        cx, cy = speed_ref[freq] * cos_ref[toward], speed_ref[freq] * sin_ref[toward]
        steps = steps_ref[freq]
        for x_up in (True, False):
            for y_up in (True, False):

                @pl.when(((cx >= 0.0) == x_up) & ((cy >= 0.0) == y_up))
                def _():
                    run(i, cx if x_up else -cx, cy if y_up else -cy, steps, x_up, y_up)

        return carry

    lax.fori_loop(0, block, component, 0)


def propagate(scalars, spectrum, low, high, masks, start, size, low_start, chain):
    comp_count, rows, cols = spectrum.shape
    halo = low.shape[1]
    block = next(
        n for n in range(min(16, size), 0, -1)
        if size % n == 0 and start % n == 0 and low_start % n == 0
    )
    ext = masks.shape[1]
    cells = size * rows * cols
    return pl.pallas_call(
        functools.partial(propagate_kernel, start),
        grid_spec=pltpu.PrefetchScalarGridSpec(
            num_scalar_prefetch=4,
            grid=(size // block,),
            in_specs=[
                pl.BlockSpec((block, rows, cols), lambda g, *_: (start // block + g, 0, 0)),
                pl.BlockSpec((block, halo, cols), lambda g, *_: (low_start // block + g, 0, 0)),
                pl.BlockSpec((block, halo, cols), lambda g, *_: (low_start // block + g, 0, 0)),
                pl.BlockSpec(masks.shape, lambda g, *_: (0, 0, 0)),
            ]
            + [pl.BlockSpec(memory_space=pl.ANY) for _ in chain],
            out_specs=pl.BlockSpec((block, rows, cols), lambda g, *_: (start // block + g, 0, 0)),
            scratch_shapes=[pltpu.VMEM((ext, cols), jnp.float32) for _ in range(3)],
        ),
        out_shape=jax.ShapeDtypeStruct((comp_count, rows, cols), jnp.float32),
        input_output_aliases={8: 0} if chain else {},
        compiler_params=pltpu.CompilerParams(vmem_limit_bytes=VMEM_BYTES),
        cost_estimate=pl.CostEstimate(
            flops=cells * 30, bytes_accessed=cells * 8, transcendentals=0
        ),
        name="propagate",
    )(*scalars, spectrum, low, high, masks, *chain)


def selection(dest_row):
    slot = lax.broadcasted_iota(jnp.int32, (BLOCK, BLOCK), 0)
    slot = slot.astype(jnp.float32).astype(jnp.bfloat16)
    one, zero = jnp.ones((), jnp.bfloat16), jnp.zeros((), jnp.bfloat16)
    return jnp.where(slot == dest_row.astype(jnp.float32).astype(jnp.bfloat16), one, zero)


def tile_of(offset):
    return lax.shift_right_logical(offset, BLOCK.bit_length() - 1)


def lane_of(offset):
    return jnp.bitwise_and(offset, BLOCK - 1)


def tile_place(tile, per_group):
    lane = lax.rem(tile, per_group) * BLOCK
    return tile // per_group, slice(None), pl.ds(pl.multiple_of(lane, BLOCK), BLOCK)


def gather_kernel(offset_ref, field_ref, dest_ref, *refs):
    outs, (packed, rows_of, open_tile) = refs[:-3], refs[-3:]
    size, rows, cols = field_ref.shape
    blocks = cols // BLOCK
    per_group = packed.shape[2] // BLOCK
    step = pl.program_id(0)
    first_block = step * rows * blocks

    @pl.when(step == 0)
    def _():
        packed[...] = jnp.zeros_like(packed)
        open_tile[...] = jnp.zeros_like(open_tile)

    for t in range(cols // LANES):
        rows_of[t] = field_ref[:, :, t * LANES:(t + 1) * LANES].reshape(size * rows, LANES)

    lane_id = lax.broadcasted_iota(jnp.int32, (size, BLOCK), 1)
    begun = open_tile[...]
    for b in range(rows * blocks):
        r, t = b // blocks, b % blocks * (BLOCK // LANES)
        values = jnp.concatenate(
            [rows_of[t + i, pl.ds(r, size, stride=rows), :] for i in range(BLOCK // LANES)], axis=1
        ).astype(jnp.bfloat16)
        placed = lax.dot_general(
            values, selection(dest_ref[pl.ds(b, 1), :]), (((1,), (1,)), ((), ())),
            preferred_element_type=jnp.float32,
        )
        offset, following = offset_ref[first_block + b], offset_ref[first_block + b + 1]
        full = jnp.where(lane_id >= lane_of(offset), placed, begun)
        packed[tile_place(tile_of(offset), per_group)] = full.astype(jnp.bfloat16)
        begun = jnp.where(tile_of(following) > tile_of(offset), placed, full)
    open_tile[...] = begun

    @pl.when(step == pl.num_programs(0) - 1)
    def _():
        tile = tile_of(offset_ref[first_block + rows * blocks])
        packed[tile_place(tile, per_group)] = begun.astype(jnp.bfloat16)
        groups, _, width = outs[0].shape
        for h, out in enumerate(outs):
            out[...] = packed[:groups, :, h * width:(h + 1) * width]


def gather_points(offsets, dest, field, start, size, groups, per_group, pieces):
    rows, cols = field.shape[1:]
    parts = cols // LANES
    width = per_group // pieces
    return pl.pallas_call(
        gather_kernel,
        grid_spec=pltpu.PrefetchScalarGridSpec(
            num_scalar_prefetch=1,
            grid=(rows // SUBLANES,),
            in_specs=[
                pl.BlockSpec(
                    (pl.Element(size), pl.Element(SUBLANES), pl.Element(cols)),
                    lambda g, *_: (start, g * SUBLANES, 0),
                ),
                pl.BlockSpec((SUBLANES * cols // BLOCK, BLOCK), lambda g, *_: (g, 0)),
            ],
            out_specs=[
                pl.BlockSpec((groups, size, width), lambda g, *_: (0, 0, 0))
                for _ in range(pieces)
            ],
            scratch_shapes=[
                pltpu.VMEM((groups + 1, size, per_group), jnp.bfloat16),
                pltpu.VMEM((parts, size * SUBLANES, LANES), jnp.float32),
                pltpu.VMEM((size, BLOCK), jnp.float32),
            ],
        ),
        out_shape=[
            jax.ShapeDtypeStruct((groups, size, width), jnp.bfloat16) for _ in range(pieces)
        ],
        compiler_params=pltpu.CompilerParams(vmem_limit_bytes=VMEM_BYTES),
        cost_estimate=pl.CostEstimate(
            flops=size * rows * cols * 2 * BLOCK,
            bytes_accessed=size * rows * cols * 6,
            transcendentals=0,
        ),
        name="gather_points",
    )(offsets, field, dest)


def scatter_kernel(offset_ref, field_ref, dest_ref, first_ref, second_ref, *refs):
    out_ref, packed, rows_of = refs[-3:]
    size, rows, cols = field_ref.shape
    blocks = cols // BLOCK
    width = first_ref.shape[2]
    per_group = packed.shape[2] // BLOCK
    last_tile = packed.shape[0] * per_group - 1
    first_block = pl.program_id(0) * rows * blocks

    @pl.when(pl.program_id(0) == 0)
    def _():
        packed[:, :, :width] = first_ref[...]
        packed[:, :, width:] = second_ref[...]

    lane_id = lax.broadcasted_iota(jnp.int32, (size, BLOCK), 1)
    lane_id = lane_id.astype(jnp.float32).astype(jnp.bfloat16)
    for b in range(rows * blocks):
        r, t = b // blocks, b % blocks * (BLOCK // LANES)
        offset = offset_ref[first_block + b]
        tile = jnp.minimum(tile_of(offset), last_tile)
        following = jnp.minimum(tile + 1, last_tile)
        values = jnp.where(
            lane_id >= lane_of(offset).astype(jnp.float32).astype(jnp.bfloat16),
            packed[tile_place(tile, per_group)],
            packed[tile_place(following, per_group)],
        )
        found = jnp.dot(
            values, selection(dest_ref[pl.ds(b, 1), :]), preferred_element_type=jnp.float32
        )
        for i in range(BLOCK // LANES):
            rows_of[t + i, pl.ds(r, size, stride=rows), :] = found[:, i * LANES:(i + 1) * LANES]
    for t in range(cols // LANES):
        at = (slice(None), slice(None), slice(t * LANES, (t + 1) * LANES))
        out_ref[at] = field_ref[at] + rows_of[t].reshape(size, rows, LANES)


def scatter_points(offsets, dest, field, first, second, start):
    groups, size, width = second.shape
    rows, cols = field.shape[1:]
    parts = cols // LANES
    field_spec = pl.BlockSpec(
        (pl.Element(size), pl.Element(SUBLANES), pl.Element(cols)),
        lambda g, *_: (start, g * SUBLANES, 0),
    )
    return pl.pallas_call(
        scatter_kernel,
        grid_spec=pltpu.PrefetchScalarGridSpec(
            num_scalar_prefetch=1,
            grid=(rows // SUBLANES,),
            in_specs=[
                field_spec,
                pl.BlockSpec((SUBLANES * cols // BLOCK, BLOCK), lambda g, *_: (g, 0)),
                pl.BlockSpec(
                    (pl.Element(groups), pl.Element(size), pl.Element(width)),
                    lambda g, *_: (0, start, 0),
                ),
                pl.BlockSpec((groups, size, width), lambda g, *_: (0, 0, 0)),
            ],
            out_specs=field_spec,
            scratch_shapes=[
                pltpu.VMEM((groups, size, 2 * width), jnp.bfloat16),
                pltpu.VMEM((parts, size * SUBLANES, LANES), jnp.float32),
            ],
        ),
        out_shape=jax.ShapeDtypeStruct(field.shape, jnp.float32),
        input_output_aliases={1: 0},
        compiler_params=pltpu.CompilerParams(vmem_limit_bytes=VMEM_BYTES),
        cost_estimate=pl.CostEstimate(
            flops=size * rows * cols * 2 * BLOCK,
            bytes_accessed=size * rows * cols * 10,
            transcendentals=0,
        ),
        name="scatter_points",
    )(offsets, field, dest, first, second)


def source_kernel(counts, out_counts, groups, mix_in, mix_out, growth, damping, weight, *refs):
    ins, outs, points = refs[:len(counts)], refs[len(counts):-1], refs[-1]
    total = sum(counts)
    for g in range(groups):
        at = g * total
        for ref, count in zip(ins, counts):
            points[at:at + count, :] = ref[g * count:(g + 1) * count, :]
            at += count
    rounded = points[...]
    hidden = jnp.dot(mix_in[...], rounded, preferred_element_type=jnp.float32)
    square = (hidden * hidden).astype(jnp.bfloat16)
    transfer = jnp.dot(mix_out[...], square, preferred_element_type=jnp.float32)
    energy = rounded.astype(jnp.float32)
    mean_energy = jnp.sum(weight[...] * energy, axis=0, keepdims=True)
    increment = 0.5 * (
        growth[...] * energy
        + 0.25 * transfer
        - damping[...] * energy * (mean_energy / (1.0 + mean_energy))
    )
    increment = increment.astype(jnp.bfloat16)
    for g in range(groups):
        at = g * total
        for ref, count in zip(outs, out_counts):
            ref[g * count:(g + 1) * count, :] = increment[at:at + count, :]
            at += count


def source_terms(pieces, counts, out_counts, slots, starts, groups, mix_in, mix_out, columns):
    comp_count = mix_in.shape[0]
    width = min(512, slots)
    fixed = lambda g: (0, 0)
    if len(counts) == 1:
        counts, out_counts, groups = [comp_count], [comp_count], 1

    def moving(start):
        return lambda g: (0, start // width + g)

    return pl.pallas_call(
        functools.partial(source_kernel, counts, out_counts, groups),
        grid=(slots // width,),
        in_specs=[pl.BlockSpec(mix_in.shape, fixed)] * 2
        + [pl.BlockSpec((comp_count, 1), fixed)] * 3
        + [
            pl.BlockSpec((groups * count, width), moving(start))
            for count, start in zip(counts, starts)
        ],
        out_specs=[pl.BlockSpec((groups * count, width), moving(0)) for count in out_counts],
        out_shape=[
            jax.ShapeDtypeStruct((groups * count, slots), jnp.bfloat16) for count in out_counts
        ],
        scratch_shapes=[pltpu.VMEM((comp_count, width), jnp.bfloat16)],
        compiler_params=pltpu.CompilerParams(vmem_limit_bytes=VMEM_BYTES),
        cost_estimate=pl.CostEstimate(
            flops=4 * comp_count * comp_count * slots,
            bytes_accessed=4 * comp_count * (comp_count + slots),
            transcendentals=0,
        ),
        name="source_terms",
    )(mix_in, mix_out, *columns, *pieces)


def edge_rows(make, axis):
    count = lax.axis_size(axis)
    forward = [(i, i + 1) for i in range(count - 1)]
    backward = [(target, source) for source, target in forward]
    return lax.ppermute(make(True), axis, forward), lax.ppermute(make(False), axis, backward)


def mask_planes(sea_mask, low, high, strip):
    blank = jnp.zeros((strip - low.shape[0], sea_mask.shape[1]), jnp.float32)
    inner = sea_mask.astype(jnp.float32)
    mask = jnp.concatenate([blank, low, inner, high, blank], axis=0)
    row = jnp.zeros_like(mask[:1])
    col = jnp.zeros_like(mask[:, :1])
    left = jnp.concatenate([col, mask[:, :-1]], axis=1)
    right = jnp.concatenate([mask[:, 1:], col], axis=1)
    above = jnp.concatenate([row, mask[:-1]], axis=0)
    below = jnp.concatenate([mask[1:], row], axis=0)
    return jnp.stack([mask, left, right, above, below])


def slot_table(sea_mask):
    cells = sea_mask.reshape(-1, BLOCK).astype(jnp.float32)
    upto = jnp.triu(jnp.ones((BLOCK, BLOCK), jnp.float32))
    rank = jnp.dot(cells, upto, precision=lax.Precision.HIGHEST)
    count = rank[:, -1]
    blocks = cells.shape[0]
    before = jnp.tril(jnp.ones((blocks, blocks), jnp.float32), -1)
    offset = jnp.dot(before, count, precision=lax.Precision.HIGHEST)
    offset = jnp.append(offset, offset[-1] + count[-1]).astype(jnp.int32)
    place = lane_of(rank.astype(jnp.int32) - 1 + offset[:-1, None])
    return offset, jnp.where(cells > 0.0, place, -1)


def local(
    spectrum, sea_mask, point_index, band_counts, sub_counts, mix_in, mix_out, growth, damping
):
    freq_count, dir_count, row_count, lon_count = spectrum.shape
    comp_count = freq_count * dir_count
    all_count = growth.shape[0] * growth.shape[1]
    groups = lax.axis_size("comp")
    per_group = point_index.shape[1] // groups
    half = per_group // 2
    sizes = chunk_sizes(comp_count, (2, 3, 4))
    starts = [sum(sizes[:j]) for j in range(len(sizes))]
    out_sizes = chunk_sizes(comp_count, (7, 2))
    out_starts = [sum(out_sizes[:j]) for j in range(len(out_sizes))]

    field = spectrum.reshape(comp_count, row_count, lon_count)

    def first_edge(last):
        at = slice(row_count - NSUB, row_count) if last else slice(0, NSUB)
        mask_rows = sea_mask[at].astype(jnp.float32)
        return jnp.concatenate([field[:sizes[0], at], mask_rows[None]], axis=0)

    def later_edge(last):
        at = slice(row_count - NSUB, row_count) if last else slice(0, NSUB)
        return field[sizes[0]:, at]

    edges = [edge_rows(first_edge, "lat")]
    if len(sizes) > 1:
        edges.append(edge_rows(later_edge, "lat"))
    mask_low, mask_high = edges[0][0][sizes[0]], edges[0][1][sizes[0]]

    freq_index = lax.axis_index("comp") * freq_count + jnp.arange(freq_count, dtype=jnp.int32)
    scalars = (wave_speeds(freq_index, sub_counts), sub_counts, *direction_table(dir_count))
    offsets, dest = slot_table(sea_mask)
    masks = mask_planes(sea_mask, mask_low, mask_high, SUBLANES)

    done = []

    def exchange(piece):
        if done:
            piece, done[-1] = lax.optimization_barrier((piece, done[-1]))
        done.append(lax.all_to_all(piece, "comp", split_axis=0, concat_axis=0, tiled=True))
        return len(done) - 1

    def as_rows(piece):
        return piece.reshape(groups * piece.shape[1], piece.shape[2])

    chain, arrived = [], [[], []]
    for j, (start, size) in enumerate(zip(starts, sizes)):
        low, high = edges[min(j, 1)]
        low_start = 0 if j == 0 else start - sizes[0]
        moved = propagate(scalars, field, low, high, masks, start, size, low_start, chain)
        pieces = 2 if j == len(sizes) - 1 else 1
        packed = gather_points(offsets, dest, moved, start, size, groups, per_group, pieces)
        chain = [moved, packed[0]]
        packed = [exchange(piece) for piece in packed]
        for h in range(2):
            arrived[h].append((packed[h % pieces], h * half if pieces == 1 else 0))

    columns = [
        column.reshape(all_count, 1)
        for column in (growth, damping, freq_weights(*growth.shape))
    ]
    back = []
    for h in range(2):
        parts_out = [comp_count] if h == 0 else out_sizes
        increments = source_terms(
            [as_rows(done[at]) for at, _ in arrived[h]], sizes, parts_out, half,
            [lane for _, lane in arrived[h]], groups, mix_in, mix_out, columns,
        )
        for rows, size in zip(increments, parts_out):
            back.append(exchange(rows.reshape(groups, size, half)))

    for start, at in zip(out_starts, back[1:]):
        moved = scatter_points(offsets, dest, moved, done[back[0]], done[at], start)
    return moved.reshape(spectrum.shape)


def solution(mesh):
    return jax.shard_map(
        local,
        mesh=mesh,
        in_specs=(
            P("comp", None, "lat", None),
            P("lat", None),
            P("lat", None),
            P("lat"),
            P("comp"),
            P(),
            P(),
            P(),
            P(),
        ),
        out_specs=P("comp", None, "lat", None),
        check_vma=False,
    )
```

```python
import functools

import jax
import jax.numpy as jnp
import numpy as np
from jax import lax
from jax.experimental import pallas as pl
from jax.experimental.pallas import tpu as pltpu
from jax.sharding import PartitionSpec as P

NSUB = 4
SUBLANES = 8
LANES = 128
BLOCK = 256
STEP_ROWS = 24
VMEM_BYTES = 56 * 1024 * 1024


def chunk_sizes(comp_count, shares):
    if comp_count % 16:
        return [comp_count]
    units, total = comp_count // 16, sum(shares)
    bounds = [units * sum(shares[:j]) // total for j in range(len(shares) + 1)]
    return [16 * (high - low) for low, high in zip(bounds, bounds[1:]) if high > low]


def wave_speeds(freq_index, sub_steps):
    group_speed = 1.4 * jnp.power(0.93, freq_index.astype(jnp.float32))
    return group_speed / sub_steps.astype(jnp.float32)


def direction_table(dir_count):
    angles = (np.arange(dir_count, dtype=np.float32) + np.float32(0.5)) * np.float32(
        2.0 * np.pi / dir_count
    )
    return [part(angles.astype(np.float64)).astype(np.float32) for part in (np.cos, np.sin)]


def freq_weights(freq_count, dir_count):
    raw_weight = jnp.power(1.1, jnp.arange(freq_count, dtype=jnp.float32))
    raw_weight = raw_weight / (dir_count * jnp.sum(raw_weight))
    return jnp.repeat(raw_weight, dir_count)


def propagate_kernel(
    start,
    speed_ref, steps_ref, cos_ref, sin_ref,
    spec_ref, low_ref, high_ref, mask_ref,
    *refs,
):
    out_ref, keep, even, odd = refs[-4:]
    block, rows, cols = spec_ref.shape
    halo = low_ref.shape[1]
    strips = rows // SUBLANES + 2
    parts = cols // LANES
    row_id = lax.broadcasted_iota(jnp.int32, (SUBLANES, LANES), 0)
    col_id = lax.broadcasted_iota(jnp.int32, (SUBLANES, LANES), 1)

    def strip_rows(s):
        return pl.ds(s * SUBLANES, SUBLANES)

    def run(i, ax, ay, steps, x_up, y_up):
        blank = jnp.zeros((SUBLANES - halo, cols), jnp.float32)
        for s in range(strips):
            keep[strip_rows(s), :] = (
                1.0
                - ax * mask_ref[2 if x_up else 1, strip_rows(s), :]
                - ay * mask_ref[4 if y_up else 3, strip_rows(s), :]
            )
            if s == 0:
                value = jnp.concatenate([blank, low_ref[i]], axis=0)
            elif s == strips - 1:
                value = jnp.concatenate([high_ref[i], blank], axis=0)
            else:
                value = spec_ref[i, strip_rows(s - 1), :]
            even[strip_rows(s), :] = value * mask_ref[0, strip_rows(s), :]

        edge_row = row_id == (0 if y_up else SUBLANES - 1)
        edge_col = col_id == (0 if x_up else LANES - 1)
        nothing = jnp.zeros((SUBLANES, LANES), jnp.float32)

        def substep(source, target=None):
            before_y = [nothing] * parts
            for s in range(strips) if y_up else range(strips - 1, -1, -1):
                inner = 0 < s < strips - 1
                before_x = nothing
                for t in range(parts) if x_up else range(parts - 1, -1, -1):
                    at = (strip_rows(s), slice(t * LANES, (t + 1) * LANES))
                    value = source[at]
                    turned = pltpu.roll(value, 1 if y_up else SUBLANES - 1, 0)
                    upwind_y = jnp.where(edge_row, before_y[t], turned)
                    before_y[t] = turned
                    if target is None and not inner:
                        continue
                    turned = pltpu.roll(value, 1 if x_up else LANES - 1, 1)
                    upwind_x = jnp.where(edge_col, before_x, turned)
                    before_x = turned
                    moved = value * keep[at] + mask_ref[(0, *at)] * (
                        ax * upwind_x + ay * upwind_y
                    )
                    if target is None:
                        out_ref[(i, strip_rows(s - 1), at[1])] = moved
                    else:
                        target[at] = moved

        def pair(_, carry):
            substep(even, odd)
            substep(odd, even)
            return carry

        lax.fori_loop(0, (steps - 1) // 2, pair, 0)

        @pl.when(lax.rem(steps, 2) == 0)
        def _():
            substep(even, odd)
            substep(odd)

        @pl.when(lax.rem(steps, 2) == 1)
        def _():
            substep(even)

    def component(i, carry):
        at = start + pl.program_id(0) * block + i
        freq = at // cos_ref.shape[0]
        toward = at - freq * cos_ref.shape[0]
        cx, cy = speed_ref[freq] * cos_ref[toward], speed_ref[freq] * sin_ref[toward]
        steps = steps_ref[freq]
        for x_up in (True, False):
            for y_up in (True, False):

                @pl.when(((cx >= 0.0) == x_up) & ((cy >= 0.0) == y_up))
                def _():
                    run(i, cx if x_up else -cx, cy if y_up else -cy, steps, x_up, y_up)

        return carry

    lax.fori_loop(0, block, component, 0)


def propagate(scalars, spectrum, low, high, masks, start, size, low_start, chain):
    comp_count, rows, cols = spectrum.shape
    halo = low.shape[1]
    block = next(
        n for n in range(min(16, size), 0, -1)
        if size % n == 0 and start % n == 0 and low_start % n == 0
    )
    ext = masks.shape[1]
    cells = size * rows * cols
    return pl.pallas_call(
        functools.partial(propagate_kernel, start),
        grid_spec=pltpu.PrefetchScalarGridSpec(
            num_scalar_prefetch=4,
            grid=(size // block,),
            in_specs=[
                pl.BlockSpec((block, rows, cols), lambda g, *_: (start // block + g, 0, 0)),
                pl.BlockSpec((block, halo, cols), lambda g, *_: (low_start // block + g, 0, 0)),
                pl.BlockSpec((block, halo, cols), lambda g, *_: (low_start // block + g, 0, 0)),
                pl.BlockSpec(masks.shape, lambda g, *_: (0, 0, 0)),
            ]
            + [pl.BlockSpec(memory_space=pl.ANY) for _ in chain],
            out_specs=pl.BlockSpec((block, rows, cols), lambda g, *_: (start // block + g, 0, 0)),
            scratch_shapes=[pltpu.VMEM((ext, cols), jnp.float32) for _ in range(3)],
        ),
        out_shape=jax.ShapeDtypeStruct((comp_count, rows, cols), jnp.float32),
        input_output_aliases={8: 0} if chain else {},
        compiler_params=pltpu.CompilerParams(vmem_limit_bytes=VMEM_BYTES),
        cost_estimate=pl.CostEstimate(
            flops=cells * 30, bytes_accessed=cells * 8, transcendentals=0
        ),
        name="propagate",
    )(*scalars, spectrum, low, high, masks, *chain)


def selection(dest_row):
    slot = lax.broadcasted_iota(jnp.int32, (BLOCK, BLOCK), 0)
    slot = slot.astype(jnp.float32).astype(jnp.bfloat16)
    one, zero = jnp.ones((), jnp.bfloat16), jnp.zeros((), jnp.bfloat16)
    return jnp.where(slot == dest_row.astype(jnp.float32).astype(jnp.bfloat16), one, zero)


def tile_of(offset):
    return lax.shift_right_logical(offset, BLOCK.bit_length() - 1)


def lane_of(offset):
    return jnp.bitwise_and(offset, BLOCK - 1)


def tile_place(tile, per_group):
    lane = lax.rem(tile, per_group) * BLOCK
    return tile // per_group, slice(None), pl.ds(pl.multiple_of(lane, BLOCK), BLOCK)


def gather_kernel(offset_ref, field_ref, dest_ref, *refs):
    outs, (packed, rows_of, open_tile) = refs[:-3], refs[-3:]
    size, rows, cols = field_ref.shape
    blocks = cols // BLOCK
    per_group = packed.shape[2] // BLOCK
    step = pl.program_id(0)
    first_block = step * rows * blocks

    @pl.when(step == 0)
    def _():
        packed[...] = jnp.zeros_like(packed)
        open_tile[...] = jnp.zeros_like(open_tile)

    for t in range(cols // LANES):
        rows_of[t] = field_ref[:, :, t * LANES:(t + 1) * LANES].reshape(size * rows, LANES)

    lane_id = lax.broadcasted_iota(jnp.int32, (size, BLOCK), 1)
    begun = open_tile[...]
    for b in range(rows * blocks):
        r, t = b // blocks, b % blocks * (BLOCK // LANES)
        values = jnp.concatenate(
            [rows_of[t + i, pl.ds(r, size, stride=rows), :] for i in range(BLOCK // LANES)], axis=1
        ).astype(jnp.bfloat16)
        placed = lax.dot_general(
            values, selection(dest_ref[pl.ds(b, 1), :]), (((1,), (1,)), ((), ())),
            preferred_element_type=jnp.float32,
        )
        offset, following = offset_ref[first_block + b], offset_ref[first_block + b + 1]
        full = jnp.where(lane_id >= lane_of(offset), placed, begun)
        packed[tile_place(tile_of(offset), per_group)] = full.astype(jnp.bfloat16)
        begun = jnp.where(tile_of(following) > tile_of(offset), placed, full)
    open_tile[...] = begun

    @pl.when(step == pl.num_programs(0) - 1)
    def _():
        tile = tile_of(offset_ref[first_block + rows * blocks])
        packed[tile_place(tile, per_group)] = begun.astype(jnp.bfloat16)
        groups, _, width = outs[0].shape
        for h, out in enumerate(outs):
            out[...] = packed[:groups, :, h * width:(h + 1) * width]


def gather_points(offsets, dest, field, start, size, groups, per_group, pieces):
    rows, cols = field.shape[1:]
    parts = cols // LANES
    width = per_group // pieces
    return pl.pallas_call(
        gather_kernel,
        grid_spec=pltpu.PrefetchScalarGridSpec(
            num_scalar_prefetch=1,
            grid=(rows // STEP_ROWS,),
            in_specs=[
                pl.BlockSpec(
                    (pl.Element(size), pl.Element(STEP_ROWS), pl.Element(cols)),
                    lambda g, *_: (start, g * STEP_ROWS, 0),
                ),
                pl.BlockSpec((STEP_ROWS * cols // BLOCK, BLOCK), lambda g, *_: (g, 0)),
            ],
            out_specs=[
                pl.BlockSpec((groups, size, width), lambda g, *_: (0, 0, 0))
                for _ in range(pieces)
            ],
            scratch_shapes=[
                pltpu.VMEM((groups + 1, size, per_group), jnp.bfloat16),
                pltpu.VMEM((parts, size * STEP_ROWS, LANES), jnp.float32),
                pltpu.VMEM((size, BLOCK), jnp.float32),
            ],
        ),
        out_shape=[
            jax.ShapeDtypeStruct((groups, size, width), jnp.bfloat16) for _ in range(pieces)
        ],
        compiler_params=pltpu.CompilerParams(vmem_limit_bytes=VMEM_BYTES),
        cost_estimate=pl.CostEstimate(
            flops=size * rows * cols * 2 * BLOCK,
            bytes_accessed=size * rows * cols * 6,
            transcendentals=0,
        ),
        name="gather_points",
    )(offsets, field, dest)


def scatter_kernel(offset_ref, field_ref, dest_ref, first_ref, second_ref, *refs):
    out_ref, packed, rows_of = refs[-3:]
    size, rows, cols = field_ref.shape
    blocks = cols // BLOCK
    width = first_ref.shape[2]
    per_group = packed.shape[2] // BLOCK
    last_tile = packed.shape[0] * per_group - 1
    first_block = pl.program_id(0) * rows * blocks

    @pl.when(pl.program_id(0) == 0)
    def _():
        packed[:, :, :width] = first_ref[...]
        packed[:, :, width:] = second_ref[...]

    lane_id = lax.broadcasted_iota(jnp.int32, (size, BLOCK), 1)
    lane_id = lane_id.astype(jnp.float32).astype(jnp.bfloat16)
    for b in range(rows * blocks):
        r, t = b // blocks, b % blocks * (BLOCK // LANES)
        offset = offset_ref[first_block + b]
        tile = jnp.minimum(tile_of(offset), last_tile)
        following = jnp.minimum(tile + 1, last_tile)
        values = jnp.where(
            lane_id >= lane_of(offset).astype(jnp.float32).astype(jnp.bfloat16),
            packed[tile_place(tile, per_group)],
            packed[tile_place(following, per_group)],
        )
        found = jnp.dot(
            values, selection(dest_ref[pl.ds(b, 1), :]), preferred_element_type=jnp.float32
        )
        for i in range(BLOCK // LANES):
            rows_of[t + i, pl.ds(r, size, stride=rows), :] = found[:, i * LANES:(i + 1) * LANES]
    for t in range(cols // LANES):
        at = (slice(None), slice(None), slice(t * LANES, (t + 1) * LANES))
        out_ref[at] = field_ref[at] + rows_of[t].reshape(size, rows, LANES)


def scatter_points(offsets, dest, field, first, second, start):
    groups, size, width = second.shape
    rows, cols = field.shape[1:]
    parts = cols // LANES
    field_spec = pl.BlockSpec(
        (pl.Element(size), pl.Element(STEP_ROWS), pl.Element(cols)),
        lambda g, *_: (start, g * STEP_ROWS, 0),
    )
    return pl.pallas_call(
        scatter_kernel,
        grid_spec=pltpu.PrefetchScalarGridSpec(
            num_scalar_prefetch=1,
            grid=(rows // STEP_ROWS,),
            in_specs=[
                field_spec,
                pl.BlockSpec((STEP_ROWS * cols // BLOCK, BLOCK), lambda g, *_: (g, 0)),
                pl.BlockSpec(
                    (pl.Element(groups), pl.Element(size), pl.Element(width)),
                    lambda g, *_: (0, start, 0),
                    pipeline_mode=pl.Buffered(1),
                ),
                pl.BlockSpec(
                    (groups, size, width), lambda g, *_: (0, 0, 0), pipeline_mode=pl.Buffered(1)
                ),
            ],
            out_specs=field_spec,
            scratch_shapes=[
                pltpu.VMEM((groups, size, 2 * width), jnp.bfloat16),
                pltpu.VMEM((parts, size * STEP_ROWS, LANES), jnp.float32),
            ],
        ),
        out_shape=jax.ShapeDtypeStruct(field.shape, jnp.float32),
        input_output_aliases={1: 0},
        compiler_params=pltpu.CompilerParams(vmem_limit_bytes=VMEM_BYTES),
        cost_estimate=pl.CostEstimate(
            flops=size * rows * cols * 2 * BLOCK,
            bytes_accessed=size * rows * cols * 10,
            transcendentals=0,
        ),
        name="scatter_points",
    )(offsets, field, dest, first, second)


def source_kernel(counts, out_counts, groups, mix_in, mix_out, growth, damping, weight, *refs):
    ins, outs, points = refs[:len(counts)], refs[len(counts):-1], refs[-1]
    total = sum(counts)
    for g in range(groups):
        at = g * total
        for ref, count in zip(ins, counts):
            points[at:at + count, :] = ref[g * count:(g + 1) * count, :]
            at += count
    rounded = points[...]
    hidden = jnp.dot(mix_in[...], rounded, preferred_element_type=jnp.float32)
    square = (hidden * hidden).astype(jnp.bfloat16)
    transfer = jnp.dot(mix_out[...], square, preferred_element_type=jnp.float32)
    energy = rounded.astype(jnp.float32)
    mean_energy = jnp.sum(weight[...] * energy, axis=0, keepdims=True)
    increment = 0.5 * (
        growth[...] * energy
        + 0.25 * transfer
        - damping[...] * energy * (mean_energy / (1.0 + mean_energy))
    )
    increment = increment.astype(jnp.bfloat16)
    for g in range(groups):
        at = g * total
        for ref, count in zip(outs, out_counts):
            ref[g * count:(g + 1) * count, :] = increment[at:at + count, :]
            at += count


def source_terms(pieces, counts, out_counts, slots, starts, groups, mix_in, mix_out, columns):
    comp_count = mix_in.shape[0]
    width = min(512, slots)
    fixed = lambda g: (0, 0)
    if len(counts) == 1:
        counts, out_counts, groups = [comp_count], [comp_count], 1

    def moving(start):
        return lambda g: (0, start // width + g)

    return pl.pallas_call(
        functools.partial(source_kernel, counts, out_counts, groups),
        grid=(slots // width,),
        in_specs=[pl.BlockSpec(mix_in.shape, fixed)] * 2
        + [pl.BlockSpec((comp_count, 1), fixed)] * 3
        + [
            pl.BlockSpec((groups * count, width), moving(start))
            for count, start in zip(counts, starts)
        ],
        out_specs=[pl.BlockSpec((groups * count, width), moving(0)) for count in out_counts],
        out_shape=[
            jax.ShapeDtypeStruct((groups * count, slots), jnp.bfloat16) for count in out_counts
        ],
        scratch_shapes=[pltpu.VMEM((comp_count, width), jnp.bfloat16)],
        compiler_params=pltpu.CompilerParams(vmem_limit_bytes=VMEM_BYTES),
        cost_estimate=pl.CostEstimate(
            flops=4 * comp_count * comp_count * slots,
            bytes_accessed=4 * comp_count * (comp_count + slots),
            transcendentals=0,
        ),
        name="source_terms",
    )(mix_in, mix_out, *columns, *pieces)


def edge_rows(make, axis):
    count = lax.axis_size(axis)
    forward = [(i, i + 1) for i in range(count - 1)]
    backward = [(target, source) for source, target in forward]
    return lax.ppermute(make(True), axis, forward), lax.ppermute(make(False), axis, backward)


def mask_planes(sea_mask, low, high, strip):
    blank = jnp.zeros((strip - low.shape[0], sea_mask.shape[1]), jnp.float32)
    inner = sea_mask.astype(jnp.float32)
    mask = jnp.concatenate([blank, low, inner, high, blank], axis=0)
    row = jnp.zeros_like(mask[:1])
    col = jnp.zeros_like(mask[:, :1])
    left = jnp.concatenate([col, mask[:, :-1]], axis=1)
    right = jnp.concatenate([mask[:, 1:], col], axis=1)
    above = jnp.concatenate([row, mask[:-1]], axis=0)
    below = jnp.concatenate([mask[1:], row], axis=0)
    return jnp.stack([mask, left, right, above, below])


def slot_table(sea_mask):
    cells = sea_mask.reshape(-1, BLOCK).astype(jnp.float32)
    upto = jnp.triu(jnp.ones((BLOCK, BLOCK), jnp.float32))
    rank = jnp.dot(cells, upto, precision=lax.Precision.HIGHEST)
    count = rank[:, -1]
    blocks = cells.shape[0]
    before = jnp.tril(jnp.ones((blocks, blocks), jnp.float32), -1)
    offset = jnp.dot(before, count, precision=lax.Precision.HIGHEST)
    offset = jnp.append(offset, offset[-1] + count[-1]).astype(jnp.int32)
    place = lane_of(rank.astype(jnp.int32) - 1 + offset[:-1, None])
    return offset, jnp.where(cells > 0.0, place, -1)


def local(
    spectrum, sea_mask, point_index, band_counts, sub_counts, mix_in, mix_out, growth, damping
):
    freq_count, dir_count, row_count, lon_count = spectrum.shape
    comp_count = freq_count * dir_count
    all_count = growth.shape[0] * growth.shape[1]
    groups = lax.axis_size("comp")
    per_group = point_index.shape[1] // groups
    half = per_group // 2
    sizes = chunk_sizes(comp_count, (1, 1, 1))
    starts = [sum(sizes[:j]) for j in range(len(sizes))]
    out_sizes = chunk_sizes(comp_count, (7, 2))
    out_starts = [sum(out_sizes[:j]) for j in range(len(out_sizes))]

    field = spectrum.reshape(comp_count, row_count, lon_count)

    def first_edge(last):
        at = slice(row_count - NSUB, row_count) if last else slice(0, NSUB)
        mask_rows = sea_mask[at].astype(jnp.float32)
        return jnp.concatenate([field[:sizes[0], at], mask_rows[None]], axis=0)

    def later_edge(last):
        at = slice(row_count - NSUB, row_count) if last else slice(0, NSUB)
        return field[sizes[0]:, at]

    edges = [edge_rows(first_edge, "lat")]
    if len(sizes) > 1:
        edges.append(edge_rows(later_edge, "lat"))
    mask_low, mask_high = edges[0][0][sizes[0]], edges[0][1][sizes[0]]

    freq_index = lax.axis_index("comp") * freq_count + jnp.arange(freq_count, dtype=jnp.int32)
    scalars = (wave_speeds(freq_index, sub_counts), sub_counts, *direction_table(dir_count))
    offsets, dest = slot_table(sea_mask)
    masks = mask_planes(sea_mask, mask_low, mask_high, SUBLANES)

    done = []

    def exchange(piece):
        if done:
            piece, done[-1] = lax.optimization_barrier((piece, done[-1]))
        done.append(lax.all_to_all(piece, "comp", split_axis=0, concat_axis=0, tiled=True))
        return len(done) - 1

    def as_rows(piece):
        return piece.reshape(groups * piece.shape[1], piece.shape[2])

    chain, arrived = [], [[], []]
    for j, (start, size) in enumerate(zip(starts, sizes)):
        low, high = edges[min(j, 1)]
        low_start = 0 if j == 0 else start - sizes[0]
        moved = propagate(scalars, field, low, high, masks, start, size, low_start, chain)
        pieces = 2 if j == len(sizes) - 1 else 1
        packed = gather_points(offsets, dest, moved, start, size, groups, per_group, pieces)
        chain = [moved, packed[0]]
        packed = [exchange(piece) for piece in packed]
        for h in range(2):
            arrived[h].append((packed[h % pieces], h * half if pieces == 1 else 0))

    columns = [
        column.reshape(all_count, 1)
        for column in (growth, damping, freq_weights(*growth.shape))
    ]
    back = []
    for h in range(2):
        parts_out = [comp_count] if h == 0 else out_sizes
        increments = source_terms(
            [as_rows(done[at]) for at, _ in arrived[h]], sizes, parts_out, half,
            [lane for _, lane in arrived[h]], groups, mix_in, mix_out, columns,
        )
        for rows, size in zip(increments, parts_out):
            back.append(exchange(rows.reshape(groups, size, half)))

    for start, at in zip(out_starts, back[1:]):
        moved = scatter_points(offsets, dest, moved, done[back[0]], done[at], start)
    return moved.reshape(spectrum.shape)


def solution(mesh):
    return jax.shard_map(
        local,
        mesh=mesh,
        in_specs=(
            P("comp", None, "lat", None),
            P("lat", None),
            P("lat", None),
            P("lat"),
            P("comp"),
            P(),
            P(),
            P(),
            P(),
        ),
        out_specs=P("comp", None, "lat", None),
        check_vma=False,
    )
```

```python
import functools

import jax
import jax.numpy as jnp
import numpy as np
from jax import lax
from jax.experimental import pallas as pl
from jax.experimental.pallas import tpu as pltpu
from jax.sharding import PartitionSpec as P

NSUB = 4
SUBLANES = 8
LANES = 128
BLOCK = 256
STEP_ROWS = 24
VMEM_BYTES = 56 * 1024 * 1024


def chunk_sizes(comp_count, shares):
    if comp_count % 16:
        return [comp_count]
    units, total = comp_count // 16, sum(shares)
    bounds = [units * sum(shares[:j]) // total for j in range(len(shares) + 1)]
    return [16 * (high - low) for low, high in zip(bounds, bounds[1:]) if high > low]


def wave_speeds(freq_index, sub_steps):
    group_speed = 1.4 * jnp.power(0.93, freq_index.astype(jnp.float32))
    return group_speed / sub_steps.astype(jnp.float32)


def direction_table(dir_count):
    angles = (np.arange(dir_count, dtype=np.float32) + np.float32(0.5)) * np.float32(
        2.0 * np.pi / dir_count
    )
    return [part(angles.astype(np.float64)).astype(np.float32) for part in (np.cos, np.sin)]


def freq_weights(freq_count, dir_count):
    raw_weight = jnp.power(1.1, jnp.arange(freq_count, dtype=jnp.float32))
    raw_weight = raw_weight / (dir_count * jnp.sum(raw_weight))
    return jnp.repeat(raw_weight, dir_count)


def propagate_kernel(
    start,
    speed_ref, steps_ref, cos_ref, sin_ref,
    spec_ref, low_ref, high_ref, mask_ref,
    *refs,
):
    out_ref, keep, even, odd = refs[-4:]
    block, rows, cols = spec_ref.shape
    halo = low_ref.shape[1]
    strips = rows // SUBLANES + 2
    parts = cols // LANES
    row_id = lax.broadcasted_iota(jnp.int32, (SUBLANES, LANES), 0)
    col_id = lax.broadcasted_iota(jnp.int32, (SUBLANES, LANES), 1)

    def strip_rows(s):
        return pl.ds(s * SUBLANES, SUBLANES)

    def run(i, ax, ay, steps, x_up, y_up):
        blank = jnp.zeros((SUBLANES - halo, cols), jnp.float32)
        for s in range(strips):
            keep[strip_rows(s), :] = (
                1.0
                - ax * mask_ref[2 if x_up else 1, strip_rows(s), :]
                - ay * mask_ref[4 if y_up else 3, strip_rows(s), :]
            )
            if s == 0:
                value = jnp.concatenate([blank, low_ref[i]], axis=0)
            elif s == strips - 1:
                value = jnp.concatenate([high_ref[i], blank], axis=0)
            else:
                value = spec_ref[i, strip_rows(s - 1), :]
            even[strip_rows(s), :] = value * mask_ref[0, strip_rows(s), :]

        edge_row = row_id == (0 if y_up else SUBLANES - 1)
        edge_col = col_id == (0 if x_up else LANES - 1)
        nothing = jnp.zeros((SUBLANES, LANES), jnp.float32)

        def substep(source, target=None):
            before_y = [nothing] * parts
            for s in range(strips) if y_up else range(strips - 1, -1, -1):
                inner = 0 < s < strips - 1
                before_x = nothing
                for t in range(parts) if x_up else range(parts - 1, -1, -1):
                    at = (strip_rows(s), slice(t * LANES, (t + 1) * LANES))
                    value = source[at]
                    turned = pltpu.roll(value, 1 if y_up else SUBLANES - 1, 0)
                    upwind_y = jnp.where(edge_row, before_y[t], turned)
                    before_y[t] = turned
                    if target is None and not inner:
                        continue
                    turned = pltpu.roll(value, 1 if x_up else LANES - 1, 1)
                    upwind_x = jnp.where(edge_col, before_x, turned)
                    before_x = turned
                    moved = value * keep[at] + mask_ref[(0, *at)] * (
                        ax * upwind_x + ay * upwind_y
                    )
                    if target is None:
                        out_ref[(i, strip_rows(s - 1), at[1])] = moved
                    else:
                        target[at] = moved

        def pair(_, carry):
            substep(even, odd)
            substep(odd, even)
            return carry

        lax.fori_loop(0, (steps - 1) // 2, pair, 0)

        @pl.when(lax.rem(steps, 2) == 0)
        def _():
            substep(even, odd)
            substep(odd)

        @pl.when(lax.rem(steps, 2) == 1)
        def _():
            substep(even)

    def component(i, carry):
        at = start + pl.program_id(0) * block + i
        freq = at // cos_ref.shape[0]
        toward = at - freq * cos_ref.shape[0]
        cx, cy = speed_ref[freq] * cos_ref[toward], speed_ref[freq] * sin_ref[toward]
        steps = steps_ref[freq]
        for x_up in (True, False):
            for y_up in (True, False):

                @pl.when(((cx >= 0.0) == x_up) & ((cy >= 0.0) == y_up))
                def _():
                    run(i, cx if x_up else -cx, cy if y_up else -cy, steps, x_up, y_up)

        return carry

    lax.fori_loop(0, block, component, 0)


def propagate(scalars, spectrum, low, high, masks, start, size, into, count, chain):
    rows, cols = spectrum.shape[1:]
    halo = low.shape[1]
    block = next(
        n for n in range(min(16, size), 0, -1)
        if size % n == 0 and start % n == 0 and into % n == 0
    )
    ext = masks.shape[1]
    cells = size * rows * cols
    return pl.pallas_call(
        functools.partial(propagate_kernel, start),
        grid_spec=pltpu.PrefetchScalarGridSpec(
            num_scalar_prefetch=4,
            grid=(size // block,),
            in_specs=[
                pl.BlockSpec((block, rows, cols), lambda g, *_: (start // block + g, 0, 0)),
                pl.BlockSpec((block, halo, cols), lambda g, *_: (into // block + g, 0, 0)),
                pl.BlockSpec((block, halo, cols), lambda g, *_: (into // block + g, 0, 0)),
                pl.BlockSpec(masks.shape, lambda g, *_: (0, 0, 0)),
            ]
            + [pl.BlockSpec(memory_space=pl.ANY) for _ in chain],
            out_specs=pl.BlockSpec((block, rows, cols), lambda g, *_: (into // block + g, 0, 0)),
            scratch_shapes=[pltpu.VMEM((ext, cols), jnp.float32) for _ in range(3)],
        ),
        out_shape=jax.ShapeDtypeStruct((count, rows, cols), jnp.float32),
        input_output_aliases={8: 0} if len(chain) == 2 else {},
        compiler_params=pltpu.CompilerParams(vmem_limit_bytes=VMEM_BYTES),
        cost_estimate=pl.CostEstimate(
            flops=cells * 30, bytes_accessed=cells * 8, transcendentals=0
        ),
        name="propagate",
    )(*scalars, spectrum, low, high, masks, *chain)


def selection(dest_row):
    slot = lax.broadcasted_iota(jnp.int32, (BLOCK, BLOCK), 0)
    slot = slot.astype(jnp.float32).astype(jnp.bfloat16)
    one, zero = jnp.ones((), jnp.bfloat16), jnp.zeros((), jnp.bfloat16)
    return jnp.where(slot == dest_row.astype(jnp.float32).astype(jnp.bfloat16), one, zero)


def tile_of(offset):
    return lax.shift_right_logical(offset, BLOCK.bit_length() - 1)


def lane_of(offset):
    return jnp.bitwise_and(offset, BLOCK - 1)


def place_of(tile, total, level, tail):
    used = tile_of(total + BLOCK - 1)
    return jnp.where(tile < level, tile, jnp.minimum(level + tail, tile - used + level + tail))


def tile_slices(groups, per_group):
    return [
        (g * per_group + i, g, slice(i * BLOCK, (i + 1) * BLOCK))
        for g in range(groups)
        for i in range(per_group)
    ]


def gather_kernel(groups, level, tail, offset_ref, field_ref, dest_ref, *refs):
    outs, (packed, rows_of, open_tile) = refs[:-3], refs[-3:]
    size, rows, cols = field_ref.shape
    blocks = cols // BLOCK
    step = pl.program_id(0)
    first_block = step * rows * blocks
    total = offset_ref[pl.num_programs(0) * rows * blocks]

    @pl.when(step == 0)
    def _():
        packed[...] = jnp.zeros_like(packed)
        open_tile[...] = jnp.zeros_like(open_tile)

    for t in range(cols // LANES):
        rows_of[t] = field_ref[:, :, t * LANES:(t + 1) * LANES].reshape(size * rows, LANES)

    lane_id = lax.broadcasted_iota(jnp.int32, (size, BLOCK), 1)
    begun = open_tile[...]
    for b in range(rows * blocks):
        r, t = b // blocks, b % blocks * (BLOCK // LANES)
        values = jnp.concatenate(
            [rows_of[t + i, pl.ds(r, size, stride=rows), :] for i in range(BLOCK // LANES)], axis=1
        ).astype(jnp.bfloat16)
        placed = lax.dot_general(
            values, selection(dest_ref[pl.ds(b, 1), :]), (((1,), (1,)), ((), ())),
            preferred_element_type=jnp.float32,
        )
        offset, following = offset_ref[first_block + b], offset_ref[first_block + b + 1]
        full = jnp.where(lane_id >= lane_of(offset), placed, begun)
        packed[place_of(tile_of(offset), total, level, tail)] = full.astype(jnp.bfloat16)
        begun = jnp.where(tile_of(following) > tile_of(offset), placed, full)
    open_tile[...] = begun

    @pl.when(step == pl.num_programs(0) - 1)
    def _():
        packed[place_of(tile_of(total), total, level, tail)] = begun.astype(jnp.bfloat16)
        main = level - tail
        for out, first, count in zip(outs, (0, main, level), (main, tail, tail)):
            for i, g, lanes in tile_slices(groups, count // groups):
                out[g, :, lanes] = packed[first + i]


def gather_points(offsets, dest, field, start, size, groups, full, level, tail):
    rows, cols = field.shape[1:]
    parts = cols // LANES
    widths = [(level - tail) // groups * BLOCK] + [tail // groups * BLOCK] * (2 - (level == full))
    return pl.pallas_call(
        functools.partial(gather_kernel, groups, level, tail),
        grid_spec=pltpu.PrefetchScalarGridSpec(
            num_scalar_prefetch=1,
            grid=(rows // STEP_ROWS,),
            in_specs=[
                pl.BlockSpec(
                    (pl.Element(size), pl.Element(STEP_ROWS), pl.Element(cols)),
                    lambda g, *_: (start, g * STEP_ROWS, 0),
                ),
                pl.BlockSpec((STEP_ROWS * cols // BLOCK, BLOCK), lambda g, *_: (g, 0)),
            ],
            out_specs=[
                pl.BlockSpec((groups, size, width), lambda g, *_: (0, 0, 0)) for width in widths
            ],
            scratch_shapes=[
                pltpu.VMEM((level + tail + 1, size, BLOCK), jnp.bfloat16),
                pltpu.VMEM((parts, size * STEP_ROWS, LANES), jnp.float32),
                pltpu.VMEM((size, BLOCK), jnp.float32),
            ],
        ),
        out_shape=[
            jax.ShapeDtypeStruct((groups, size, width), jnp.bfloat16) for width in widths
        ],
        compiler_params=pltpu.CompilerParams(vmem_limit_bytes=VMEM_BYTES),
        cost_estimate=pl.CostEstimate(
            flops=size * rows * cols * 2 * BLOCK,
            bytes_accessed=size * rows * cols * 6,
            transcendentals=0,
        ),
        name="gather_points",
    )(offsets, field, dest)


def scatter_kernel(level, tail, count, offset_ref, field_ref, dest_ref, *refs):
    sources, (out_ref, packed, rows_of) = refs[:count], refs[-3:]
    size, rows, cols = field_ref.shape
    blocks = cols // BLOCK
    first_block = pl.program_id(0) * rows * blocks
    total = offset_ref[pl.num_programs(0) * rows * blocks]
    last = packed.shape[0] - 1

    @pl.when(pl.program_id(0) == 0)
    def _():
        for source, first in zip(sources, (0, level - tail, level)):
            for i, g, lanes in tile_slices(source.shape[0], source.shape[2] // BLOCK):
                packed[first + i] = source[g, :, lanes]

    lane_id = lax.broadcasted_iota(jnp.int32, (size, BLOCK), 1)
    lane_id = lane_id.astype(jnp.float32).astype(jnp.bfloat16)
    for b in range(rows * blocks):
        r, t = b // blocks, b % blocks * (BLOCK // LANES)
        offset = offset_ref[first_block + b]
        tile = tile_of(offset)
        values = jnp.where(
            lane_id >= lane_of(offset).astype(jnp.float32).astype(jnp.bfloat16),
            packed[jnp.minimum(place_of(tile, total, level, tail), last)],
            packed[jnp.minimum(place_of(tile + 1, total, level, tail), last)],
        )
        found = jnp.dot(
            values, selection(dest_ref[pl.ds(b, 1), :]), preferred_element_type=jnp.float32
        )
        for i in range(BLOCK // LANES):
            rows_of[t + i, pl.ds(r, size, stride=rows), :] = found[:, i * LANES:(i + 1) * LANES]
    for t in range(cols // LANES):
        at = (slice(None), slice(None), slice(t * LANES, (t + 1) * LANES))
        out_ref[at] = field_ref[at] + rows_of[t].reshape(size, rows, LANES)


def scatter_points(offsets, dest, field, main, tails, whole, comp_count, start, level, tail):
    size, rows, cols = field.shape
    groups, width = main.shape[0], main.shape[2]
    parts = cols // LANES
    aliased = [] if whole is None else [whole]
    sources = 1 + len(tails)
    return pl.pallas_call(
        functools.partial(scatter_kernel, level, tail, sources),
        grid_spec=pltpu.PrefetchScalarGridSpec(
            num_scalar_prefetch=1,
            grid=(rows // STEP_ROWS,),
            in_specs=[
                pl.BlockSpec((size, STEP_ROWS, cols), lambda g, *_: (0, g, 0)),
                pl.BlockSpec((STEP_ROWS * cols // BLOCK, BLOCK), lambda g, *_: (g, 0)),
                pl.BlockSpec(
                    (groups, size, width), lambda g, *_: (0, 0, 0), pipeline_mode=pl.Buffered(1)
                ),
            ]
            + [
                pl.BlockSpec(
                    (pl.Element(groups), pl.Element(size), pl.Element(tail // groups * BLOCK)),
                    lambda g, *_: (0, start, 0),
                    pipeline_mode=pl.Buffered(1),
                )
                for _ in tails
            ]
            + [pl.BlockSpec(memory_space=pl.ANY) for _ in aliased],
            out_specs=pl.BlockSpec(
                (pl.Element(size), pl.Element(STEP_ROWS), pl.Element(cols)),
                lambda g, *_: (start, g * STEP_ROWS, 0),
            ),
            scratch_shapes=[
                pltpu.VMEM((level + tail * (len(tails) - 1), size, BLOCK), jnp.bfloat16),
                pltpu.VMEM((parts, size * STEP_ROWS, LANES), jnp.float32),
            ],
        ),
        out_shape=jax.ShapeDtypeStruct((comp_count, rows, cols), jnp.float32),
        input_output_aliases={3 + sources: 0} if aliased else {},
        compiler_params=pltpu.CompilerParams(vmem_limit_bytes=VMEM_BYTES),
        cost_estimate=pl.CostEstimate(
            flops=size * rows * cols * 2 * BLOCK,
            bytes_accessed=size * rows * cols * 10,
            transcendentals=0,
        ),
        name="scatter_points",
    )(offsets, field, dest, main, *tails, *aliased)


def source_kernel(counts, out_counts, groups, mix_in, mix_out, growth, damping, weight, *refs):
    ins, outs, points = refs[:len(counts)], refs[len(counts):-1], refs[-1]
    total = sum(counts)
    for g in range(groups):
        at = g * total
        for ref, count in zip(ins, counts):
            points[at:at + count, :] = ref[g * count:(g + 1) * count, :]
            at += count
    rounded = points[...]
    hidden = jnp.dot(mix_in[...], rounded, preferred_element_type=jnp.float32)
    square = (hidden * hidden).astype(jnp.bfloat16)
    transfer = jnp.dot(mix_out[...], square, preferred_element_type=jnp.float32)
    energy = rounded.astype(jnp.float32)
    mean_energy = jnp.sum(weight[...] * energy, axis=0, keepdims=True)
    increment = 0.5 * (
        growth[...] * energy
        + 0.25 * transfer
        - damping[...] * energy * (mean_energy / (1.0 + mean_energy))
    )
    increment = increment.astype(jnp.bfloat16)
    for g in range(groups):
        at = g * total
        for ref, count in zip(outs, out_counts):
            ref[g * count:(g + 1) * count, :] = increment[at:at + count, :]
            at += count


def source_terms(pieces, out_counts, mix_in, mix_out, columns):
    comp_count = mix_in.shape[0]
    groups, _, slots = pieces[0].shape
    counts = [piece.shape[1] for piece in pieces]
    width = 512 if slots % 512 == 0 else BLOCK
    fixed = lambda g: (0, 0)
    moving = lambda g: (0, g)
    shapes = [(groups, count, slots) for count in out_counts]
    pieces = [piece.reshape(-1, slots) for piece in pieces]
    if len(counts) == 1 and len(out_counts) == 1:
        counts, out_counts, groups = [comp_count], [comp_count], 1
    increments = pl.pallas_call(
        functools.partial(source_kernel, counts, out_counts, groups),
        grid=(slots // width,),
        in_specs=[pl.BlockSpec(mix_in.shape, fixed)] * 2
        + [pl.BlockSpec((comp_count, 1), fixed)] * 3
        + [pl.BlockSpec((groups * count, width), moving) for count in counts],
        out_specs=[pl.BlockSpec((groups * count, width), moving) for count in out_counts],
        out_shape=[
            jax.ShapeDtypeStruct((groups * count, slots), jnp.bfloat16) for count in out_counts
        ],
        scratch_shapes=[pltpu.VMEM((comp_count, width), jnp.bfloat16)],
        compiler_params=pltpu.CompilerParams(vmem_limit_bytes=VMEM_BYTES),
        cost_estimate=pl.CostEstimate(
            flops=4 * comp_count * comp_count * slots,
            bytes_accessed=4 * comp_count * (comp_count + slots),
            transcendentals=0,
        ),
        name="source_terms",
    )(mix_in, mix_out, *columns, *pieces)
    return [rows.reshape(shape) for rows, shape in zip(increments, shapes)]


def edge_rows(make, axis):
    count = lax.axis_size(axis)
    forward = [(i, i + 1) for i in range(count - 1)]
    backward = [(target, source) for source, target in forward]
    return lax.ppermute(make(True), axis, forward), lax.ppermute(make(False), axis, backward)


def mask_planes(sea_mask, low, high, strip):
    blank = jnp.zeros((strip - low.shape[0], sea_mask.shape[1]), jnp.float32)
    inner = sea_mask.astype(jnp.float32)
    mask = jnp.concatenate([blank, low, inner, high, blank], axis=0)
    row = jnp.zeros_like(mask[:1])
    col = jnp.zeros_like(mask[:, :1])
    left = jnp.concatenate([col, mask[:, :-1]], axis=1)
    right = jnp.concatenate([mask[:, 1:], col], axis=1)
    above = jnp.concatenate([row, mask[:-1]], axis=0)
    below = jnp.concatenate([mask[1:], row], axis=0)
    return jnp.stack([mask, left, right, above, below])


def slot_table(sea_mask):
    cells = sea_mask.reshape(-1, BLOCK).astype(jnp.float32)
    upto = jnp.triu(jnp.ones((BLOCK, BLOCK), jnp.float32))
    rank = jnp.dot(cells, upto, precision=lax.Precision.HIGHEST)
    count = rank[:, -1]
    blocks = cells.shape[0]
    before = jnp.tril(jnp.ones((blocks, blocks), jnp.float32), -1)
    offset = jnp.dot(before, count, precision=lax.Precision.HIGHEST)
    offset = jnp.append(offset, offset[-1] + count[-1]).astype(jnp.int32)
    place = lane_of(rank.astype(jnp.int32) - 1 + offset[:-1, None])
    return offset, jnp.where(cells > 0.0, place, -1)


def local(
    spectrum, sea_mask, point_index, band_counts, sub_counts, mix_in, mix_out, growth, damping
):
    freq_count, dir_count, row_count, lon_count = spectrum.shape
    comp_count = freq_count * dir_count
    all_count = growth.shape[0] * growth.shape[1]
    groups = lax.axis_size("comp")
    bands = lax.axis_size("lat")
    group_tiles = point_index.shape[1] // (groups * BLOCK)
    full = group_tiles * groups
    tail = max(1, group_tiles * 3 // 16) * groups
    levels = list(range(full - tail, full + 1, groups)) if bands % 2 == 0 else [full]
    sizes = chunk_sizes(comp_count, (2, 3, 4))
    starts = [sum(sizes[:j]) for j in range(len(sizes))]
    head = sizes[0]

    field = spectrum.reshape(comp_count, row_count, lon_count)

    def edge_slice(last):
        return slice(row_count - NSUB, row_count) if last else slice(0, NSUB)

    def first_edge(last):
        mask_rows = sea_mask[edge_slice(last)].astype(jnp.float32)
        return jnp.concatenate([field[:head, edge_slice(last)], mask_rows[None]], axis=0)

    def later_edge(last):
        return field[head:, edge_slice(last)]

    edges = [edge_rows(first_edge, "lat")]
    if len(sizes) > 1:
        edges.append(edge_rows(later_edge, "lat"))
    mask_low, mask_high = edges[0][0][head], edges[0][1][head]

    freq_index = lax.axis_index("comp") * freq_count + jnp.arange(freq_count, dtype=jnp.int32)
    scalars = (wave_speeds(freq_index, sub_counts), sub_counts, *direction_table(dir_count))
    offsets, dest = slot_table(sea_mask)
    masks = mask_planes(sea_mask, mask_low, mask_high, SUBLANES)
    first_field = propagate(scalars, field, *edges[0], masks, 0, head, 0, head, [])
    columns = [
        column.reshape(all_count, 1)
        for column in (growth, damping, freq_weights(*growth.shape))
    ]

    def used_tiles(count):
        return (count + BLOCK - 1) // BLOCK

    def rest(level, first_field, field, later_low, later_high, masks, scalars, offsets, dest,
             partner_count, mix_in, mix_out, columns):
        done = []

        def exchange(piece):
            if done:
                piece, done[-1] = lax.optimization_barrier((piece, done[-1]))
            done.append(lax.all_to_all(piece, "comp", split_axis=0, concat_axis=0, tiled=True))
            return len(done) - 1

        def partners(array):
            return lax.ppermute(array, "lat", [(i, i ^ 1) for i in range(bands)])

        tail_tile = lax.broadcasted_iota(jnp.int32, (groups, 1, tail // groups * BLOCK), 0)
        tail_tile = tail_tile * (tail // groups) + (
            lax.broadcasted_iota(jnp.int32, tail_tile.shape, 2) // BLOCK
        )
        lent = tail_tile >= tail + level - used_tiles(partner_count)

        moved, chain, arrived, tails = first_field, [], [], []
        for j, (start, size) in enumerate(zip(starts, sizes)):
            if j > 0:
                moved = propagate(
                    scalars, field, later_low, later_high, masks, start, size, start - head,
                    comp_count - head, chain,
                )
            packed = gather_points(
                offsets, dest, moved, start - head if j > 0 else 0, size, groups, full, level, tail
            )
            chain = [moved, packed[0]] if j > 0 else [packed[0]]
            arrived.append(exchange(packed[0]))
            own = packed[1]
            if level < full:
                own = jnp.where(lent, partners(packed[2]), own)
            tails.append(own)
        tail_at = exchange(jnp.concatenate(tails, axis=1))

        out_sizes = [head] + [comp_count - head] * (len(sizes) > 1)
        increments = source_terms([done[at] for at in arrived], out_sizes, mix_in, mix_out, columns)
        main_at = [exchange(increments[-1])]
        tail_back, = source_terms([done[tail_at]], [comp_count], mix_in, mix_out, columns)
        tail_at = exchange(tail_back)
        if len(sizes) > 1:
            main_at.append(exchange(increments[0]))
        tails = [done[tail_at]]
        if level < full:
            tails.append(partners(tails[0]))
        whole = None
        if len(sizes) > 1:
            whole = scatter_points(
                offsets, dest, moved, done[main_at[0]], tails, None, comp_count, head, level, tail
            )
        return scatter_points(
            offsets, dest, first_field, done[main_at[-1]], tails, whole, comp_count, 0, level, tail
        )

    counts = lax.all_gather(band_counts, "lat", tiled=True)
    partner_count = lax.dynamic_index_in_dim(
        counts, jnp.bitwise_xor(lax.axis_index("lat"), 1 if bands > 1 else 0), keepdims=False
    )
    later_low, later_high = edges[-1]
    operands = (first_field, field, later_low, later_high, masks, scalars, offsets, dest,
                partner_count, mix_in, mix_out, columns)
    if len(levels) == 1:
        whole = rest(full, *operands)
    else:
        need = jnp.max(jnp.sum(used_tiles(counts).reshape(-1, 2), axis=1))
        pick = sum((need > 2 * level).astype(jnp.int32) for level in levels[:-1])
        whole = lax.switch(pick, [functools.partial(rest, level) for level in levels], *operands)
    return whole.reshape(spectrum.shape)


def solution(mesh):
    return jax.shard_map(
        local,
        mesh=mesh,
        in_specs=(
            P("comp", None, "lat", None),
            P("lat", None),
            P("lat", None),
            P("lat"),
            P("comp"),
            P(),
            P(),
            P(),
            P(),
        ),
        out_specs=P("comp", None, "lat", None),
        check_vma=False,
    )
```

```python
import functools

import jax
import jax.numpy as jnp
import numpy as np
from jax import lax
from jax.experimental import pallas as pl
from jax.experimental.pallas import tpu as pltpu
from jax.sharding import PartitionSpec as P

NSUB = 4
SUBLANES = 8
LANES = 128
BLOCK = 256
STEP_ROWS = 24
SPREAD = 16
VMEM_BYTES = 56 * 1024 * 1024


def chunk_sizes(comp_count, shares):
    if comp_count % 16:
        return [comp_count]
    units, total = comp_count // 16, sum(shares)
    bounds = [units * sum(shares[:j]) // total for j in range(len(shares) + 1)]
    return [16 * (high - low) for low, high in zip(bounds, bounds[1:]) if high > low]


def wave_speeds(freq_index, sub_steps):
    group_speed = 1.4 * jnp.power(0.93, freq_index.astype(jnp.float32))
    return group_speed / sub_steps.astype(jnp.float32)


def direction_table(dir_count):
    angles = (np.arange(dir_count, dtype=np.float32) + np.float32(0.5)) * np.float32(
        2.0 * np.pi / dir_count
    )
    return [part(angles.astype(np.float64)).astype(np.float32) for part in (np.cos, np.sin)]


def freq_weights(freq_count, dir_count):
    raw_weight = jnp.power(1.1, jnp.arange(freq_count, dtype=jnp.float32))
    raw_weight = raw_weight / (dir_count * jnp.sum(raw_weight))
    return jnp.repeat(raw_weight, dir_count)


def propagate_kernel(
    start,
    speed_ref, steps_ref, cos_ref, sin_ref,
    spec_ref, low_ref, high_ref, mask_ref,
    *refs,
):
    out_ref, keep, even, odd = refs[-4:]
    block, rows, cols = spec_ref.shape
    halo = low_ref.shape[1]
    strips = rows // SUBLANES + 2
    parts = cols // LANES
    row_id = lax.broadcasted_iota(jnp.int32, (SUBLANES, LANES), 0)
    col_id = lax.broadcasted_iota(jnp.int32, (SUBLANES, LANES), 1)

    def strip_rows(s):
        return pl.ds(s * SUBLANES, SUBLANES)

    def run(i, ax, ay, steps, x_up, y_up):
        blank = jnp.zeros((SUBLANES - halo, cols), jnp.float32)
        for s in range(strips):
            keep[strip_rows(s), :] = (
                1.0
                - ax * mask_ref[2 if x_up else 1, strip_rows(s), :]
                - ay * mask_ref[4 if y_up else 3, strip_rows(s), :]
            )
            if s == 0:
                value = jnp.concatenate([blank, low_ref[i]], axis=0)
            elif s == strips - 1:
                value = jnp.concatenate([high_ref[i], blank], axis=0)
            else:
                value = spec_ref[i, strip_rows(s - 1), :]
            even[strip_rows(s), :] = value * mask_ref[0, strip_rows(s), :]

        edge_row = row_id == (0 if y_up else SUBLANES - 1)
        edge_col = col_id == (0 if x_up else LANES - 1)
        nothing = jnp.zeros((SUBLANES, LANES), jnp.float32)

        def substep(source, target=None):
            before_y = [nothing] * parts
            for s in range(strips) if y_up else range(strips - 1, -1, -1):
                inner = 0 < s < strips - 1
                before_x = nothing
                for t in range(parts) if x_up else range(parts - 1, -1, -1):
                    at = (strip_rows(s), slice(t * LANES, (t + 1) * LANES))
                    value = source[at]
                    turned = pltpu.roll(value, 1 if y_up else SUBLANES - 1, 0)
                    upwind_y = jnp.where(edge_row, before_y[t], turned)
                    before_y[t] = turned
                    if target is None and not inner:
                        continue
                    turned = pltpu.roll(value, 1 if x_up else LANES - 1, 1)
                    upwind_x = jnp.where(edge_col, before_x, turned)
                    before_x = turned
                    moved = value * keep[at] + mask_ref[(0, *at)] * (
                        ax * upwind_x + ay * upwind_y
                    )
                    if target is None:
                        out_ref[(i, strip_rows(s - 1), at[1])] = moved
                    else:
                        target[at] = moved

        def pair(_, carry):
            substep(even, odd)
            substep(odd, even)
            return carry

        lax.fori_loop(0, (steps - 1) // 2, pair, 0)

        @pl.when(lax.rem(steps, 2) == 0)
        def _():
            substep(even, odd)
            substep(odd)

        @pl.when(lax.rem(steps, 2) == 1)
        def _():
            substep(even)

    def component(i, carry):
        at = start + pl.program_id(0) * block + i
        freq = at // cos_ref.shape[0]
        toward = at - freq * cos_ref.shape[0]
        cx, cy = speed_ref[freq] * cos_ref[toward], speed_ref[freq] * sin_ref[toward]
        steps = steps_ref[freq]
        for x_up in (True, False):
            for y_up in (True, False):

                @pl.when(((cx >= 0.0) == x_up) & ((cy >= 0.0) == y_up))
                def _():
                    run(i, cx if x_up else -cx, cy if y_up else -cy, steps, x_up, y_up)

        return carry

    lax.fori_loop(0, block, component, 0)


def propagate(scalars, spectrum, low, high, masks, start, size, chain):
    comp_count, rows, cols = spectrum.shape
    halo = low.shape[1]
    block = next(
        n for n in range(min(16, size), 0, -1)
        if size % n == 0 and start % n == 0
    )
    ext = masks.shape[1]
    cells = size * rows * cols
    return pl.pallas_call(
        functools.partial(propagate_kernel, start),
        grid_spec=pltpu.PrefetchScalarGridSpec(
            num_scalar_prefetch=4,
            grid=(size // block,),
            in_specs=[
                pl.BlockSpec((block, rows, cols), lambda g, *_: (start // block + g, 0, 0)),
                pl.BlockSpec((block, halo, cols), lambda g, *_: (g, 0, 0)),
                pl.BlockSpec((block, halo, cols), lambda g, *_: (g, 0, 0)),
                pl.BlockSpec(masks.shape, lambda g, *_: (0, 0, 0)),
            ]
            + [pl.BlockSpec(memory_space=pl.ANY) for _ in chain],
            out_specs=pl.BlockSpec((block, rows, cols), lambda g, *_: (start // block + g, 0, 0)),
            scratch_shapes=[pltpu.VMEM((ext, cols), jnp.float32) for _ in range(3)],
        ),
        out_shape=jax.ShapeDtypeStruct((comp_count, rows, cols), jnp.float32),
        input_output_aliases={8: 0} if chain else {},
        compiler_params=pltpu.CompilerParams(vmem_limit_bytes=VMEM_BYTES),
        cost_estimate=pl.CostEstimate(
            flops=cells * 30, bytes_accessed=cells * 8, transcendentals=0
        ),
        name="propagate",
    )(*scalars, spectrum, low, high, masks, *chain)


def selection(dest):
    spread = dest.shape[0]
    slot = lax.broadcasted_iota(jnp.int32, (BLOCK, BLOCK), 0)
    slot = slot.astype(jnp.float32).astype(jnp.bfloat16).reshape(BLOCK // spread, spread, BLOCK)
    one, zero = jnp.ones((), jnp.bfloat16), jnp.zeros((), jnp.bfloat16)
    return jnp.where(slot == dest[None], one, zero).reshape(BLOCK, BLOCK)


def tile_of(offset):
    return lax.shift_right_logical(offset, BLOCK.bit_length() - 1)


def lane_of(offset):
    return jnp.bitwise_and(offset, BLOCK - 1)


def tile_place(tile, per_group):
    lane = lax.rem(tile, per_group) * BLOCK
    return tile // per_group, slice(None), pl.ds(pl.multiple_of(lane, BLOCK), BLOCK)


def gather_kernel(offset_ref, field_ref, dest_ref, *refs):
    outs, (packed, rows_of, open_tile) = refs[:-3], refs[-3:]
    size, rows, cols = field_ref.shape
    blocks = cols // BLOCK
    per_group = packed.shape[2] // BLOCK
    step = pl.program_id(0)
    first_block = step * rows * blocks

    @pl.when(step == 0)
    def _():
        packed[...] = jnp.zeros_like(packed)
        open_tile[...] = jnp.zeros_like(open_tile)

    for t in range(cols // LANES):
        rows_of[t] = field_ref[:, :, t * LANES:(t + 1) * LANES].reshape(size * rows, LANES)

    lane_id = lax.broadcasted_iota(jnp.int32, (size, BLOCK), 1)
    begun = open_tile[...]
    for b in range(rows * blocks):
        r, t = b // blocks, b % blocks * (BLOCK // LANES)
        values = jnp.concatenate(
            [rows_of[t + i, pl.ds(r, size, stride=rows), :] for i in range(BLOCK // LANES)], axis=1
        ).astype(jnp.bfloat16)
        placed = lax.dot_general(
            values, selection(dest_ref[b]), (((1,), (1,)), ((), ())),
            preferred_element_type=jnp.float32,
        )
        offset, following = offset_ref[first_block + b], offset_ref[first_block + b + 1]
        full = jnp.where(lane_id >= lane_of(offset), placed, begun)
        packed[tile_place(tile_of(offset), per_group)] = full.astype(jnp.bfloat16)
        begun = jnp.where(tile_of(following) > tile_of(offset), placed, full)
    open_tile[...] = begun

    @pl.when(step == pl.num_programs(0) - 1)
    def _():
        tile = tile_of(offset_ref[first_block + rows * blocks])
        packed[tile_place(tile, per_group)] = begun.astype(jnp.bfloat16)
        groups, _, width = outs[0].shape
        for h, out in enumerate(outs):
            out[...] = packed[:groups, :, h * width:(h + 1) * width]


def gather_points(offsets, dest, field, start, size, groups, per_group, pieces):
    rows, cols = field.shape[1:]
    parts = cols // LANES
    width = per_group // pieces
    return pl.pallas_call(
        gather_kernel,
        grid_spec=pltpu.PrefetchScalarGridSpec(
            num_scalar_prefetch=1,
            grid=(rows // STEP_ROWS,),
            in_specs=[
                pl.BlockSpec(
                    (pl.Element(size), pl.Element(STEP_ROWS), pl.Element(cols)),
                    lambda g, *_: (start, g * STEP_ROWS, 0),
                ),
                pl.BlockSpec((STEP_ROWS * cols // BLOCK, *dest.shape[1:]), lambda g, *_: (g, 0, 0)),
            ],
            out_specs=[
                pl.BlockSpec((groups, size, width), lambda g, *_: (0, 0, 0))
                for _ in range(pieces)
            ],
            scratch_shapes=[
                pltpu.VMEM((groups + 1, size, per_group), jnp.bfloat16),
                pltpu.VMEM((parts, size * STEP_ROWS, LANES), jnp.float32),
                pltpu.VMEM((size, BLOCK), jnp.float32),
            ],
        ),
        out_shape=[
            jax.ShapeDtypeStruct((groups, size, width), jnp.bfloat16) for _ in range(pieces)
        ],
        compiler_params=pltpu.CompilerParams(vmem_limit_bytes=VMEM_BYTES),
        cost_estimate=pl.CostEstimate(
            flops=size * rows * cols * 2 * BLOCK,
            bytes_accessed=size * rows * cols * 6,
            transcendentals=0,
        ),
        name="gather_points",
    )(offsets, field, dest)


def scatter_kernel(offset_ref, field_ref, dest_ref, first_ref, second_ref, *refs):
    out_ref, packed, rows_of = refs[-3:]
    size, rows, cols = field_ref.shape
    blocks = cols // BLOCK
    width = first_ref.shape[2]
    per_group = packed.shape[2] // BLOCK
    last_tile = packed.shape[0] * per_group - 1
    first_block = pl.program_id(0) * rows * blocks

    @pl.when(pl.program_id(0) == 0)
    def _():
        packed[:, :, :width] = first_ref[...]
        packed[:, :, width:] = second_ref[...]

    lane_id = lax.broadcasted_iota(jnp.int32, (size, BLOCK), 1)
    lane_id = lane_id.astype(jnp.float32).astype(jnp.bfloat16)
    for b in range(rows * blocks):
        r, t = b // blocks, b % blocks * (BLOCK // LANES)
        offset = offset_ref[first_block + b]
        tile = jnp.minimum(tile_of(offset), last_tile)
        following = jnp.minimum(tile + 1, last_tile)
        values = jnp.where(
            lane_id >= lane_of(offset).astype(jnp.float32).astype(jnp.bfloat16),
            packed[tile_place(tile, per_group)],
            packed[tile_place(following, per_group)],
        )
        found = jnp.dot(
            values, selection(dest_ref[b]), preferred_element_type=jnp.float32
        )
        for i in range(BLOCK // LANES):
            rows_of[t + i, pl.ds(r, size, stride=rows), :] = found[:, i * LANES:(i + 1) * LANES]
    for t in range(cols // LANES):
        at = (slice(None), slice(None), slice(t * LANES, (t + 1) * LANES))
        out_ref[at] = field_ref[at] + rows_of[t].reshape(size, rows, LANES)


def scatter_points(offsets, dest, field, first, second, start):
    groups, size, width = second.shape
    rows, cols = field.shape[1:]
    parts = cols // LANES
    field_spec = pl.BlockSpec(
        (pl.Element(size), pl.Element(STEP_ROWS), pl.Element(cols)),
        lambda g, *_: (start, g * STEP_ROWS, 0),
    )
    return pl.pallas_call(
        scatter_kernel,
        grid_spec=pltpu.PrefetchScalarGridSpec(
            num_scalar_prefetch=1,
            grid=(rows // STEP_ROWS,),
            in_specs=[
                field_spec,
                pl.BlockSpec((STEP_ROWS * cols // BLOCK, *dest.shape[1:]), lambda g, *_: (g, 0, 0)),
                pl.BlockSpec(
                    (pl.Element(groups), pl.Element(size), pl.Element(width)),
                    lambda g, *_: (0, start, 0),
                    pipeline_mode=pl.Buffered(1),
                ),
                pl.BlockSpec(
                    (groups, size, width), lambda g, *_: (0, 0, 0), pipeline_mode=pl.Buffered(1)
                ),
            ],
            out_specs=field_spec,
            scratch_shapes=[
                pltpu.VMEM((groups, size, 2 * width), jnp.bfloat16),
                pltpu.VMEM((parts, size * STEP_ROWS, LANES), jnp.float32),
            ],
        ),
        out_shape=jax.ShapeDtypeStruct(field.shape, jnp.float32),
        input_output_aliases={1: 0},
        compiler_params=pltpu.CompilerParams(vmem_limit_bytes=VMEM_BYTES),
        cost_estimate=pl.CostEstimate(
            flops=size * rows * cols * 2 * BLOCK,
            bytes_accessed=size * rows * cols * 10,
            transcendentals=0,
        ),
        name="scatter_points",
    )(offsets, field, dest, first, second)


def source_kernel(counts, out_counts, groups, mix_in, mix_out, growth, damping, weight, *refs):
    ins, outs, points = refs[:len(counts)], refs[len(counts):-1], refs[-1]
    total = sum(counts)
    for g in range(groups):
        at = g * total
        for ref, count in zip(ins, counts):
            points[at:at + count, :] = ref[g * count:(g + 1) * count, :]
            at += count
    rounded = points[...]
    hidden = jnp.dot(mix_in[...], rounded, preferred_element_type=jnp.float32)
    square = (hidden * hidden).astype(jnp.bfloat16)
    transfer = jnp.dot(mix_out[...], square, preferred_element_type=jnp.float32)
    energy = rounded.astype(jnp.float32)
    mean_energy = jnp.sum(weight[...] * energy, axis=0, keepdims=True)
    increment = 0.5 * (
        growth[...] * energy
        + 0.25 * transfer
        - damping[...] * energy * (mean_energy / (1.0 + mean_energy))
    )
    increment = increment.astype(jnp.bfloat16)
    for g in range(groups):
        at = g * total
        for ref, count in zip(outs, out_counts):
            ref[g * count:(g + 1) * count, :] = increment[at:at + count, :]
            at += count


def source_terms(pieces, counts, out_counts, slots, starts, groups, mix_in, mix_out, columns):
    comp_count = mix_in.shape[0]
    width = min(512, slots)
    fixed = lambda g: (0, 0)
    if len(counts) == 1:
        counts, out_counts, groups = [comp_count], [comp_count], 1

    def moving(start):
        return lambda g: (0, start // width + g)

    return pl.pallas_call(
        functools.partial(source_kernel, counts, out_counts, groups),
        grid=(slots // width,),
        in_specs=[pl.BlockSpec(mix_in.shape, fixed)] * 2
        + [pl.BlockSpec((comp_count, 1), fixed)] * 3
        + [
            pl.BlockSpec((groups * count, width), moving(start))
            for count, start in zip(counts, starts)
        ],
        out_specs=[pl.BlockSpec((groups * count, width), moving(0)) for count in out_counts],
        out_shape=[
            jax.ShapeDtypeStruct((groups * count, slots), jnp.bfloat16) for count in out_counts
        ],
        scratch_shapes=[pltpu.VMEM((comp_count, width), jnp.bfloat16)],
        compiler_params=pltpu.CompilerParams(vmem_limit_bytes=VMEM_BYTES),
        cost_estimate=pl.CostEstimate(
            flops=4 * comp_count * comp_count * slots,
            bytes_accessed=4 * comp_count * (comp_count + slots),
            transcendentals=0,
        ),
        name="source_terms",
    )(mix_in, mix_out, *columns, *pieces)


def edge_rows(make, axis):
    count = lax.axis_size(axis)
    forward = [(i, i + 1) for i in range(count - 1)]
    backward = [(target, source) for source, target in forward]
    return lax.ppermute(make(True), axis, forward), lax.ppermute(make(False), axis, backward)


def mask_planes(sea_mask, low, high, strip):
    blank = jnp.zeros((strip - low.shape[0], sea_mask.shape[1]), jnp.float32)
    inner = sea_mask.astype(jnp.float32)
    mask = jnp.concatenate([blank, low, inner, high, blank], axis=0)
    row = jnp.zeros_like(mask[:1])
    col = jnp.zeros_like(mask[:, :1])
    left = jnp.concatenate([col, mask[:, :-1]], axis=1)
    right = jnp.concatenate([mask[:, 1:], col], axis=1)
    above = jnp.concatenate([row, mask[:-1]], axis=0)
    below = jnp.concatenate([mask[1:], row], axis=0)
    return jnp.stack([mask, left, right, above, below])


def slot_table(sea_mask):
    cells = sea_mask.reshape(-1, BLOCK).astype(jnp.float32)
    upto = jnp.triu(jnp.ones((BLOCK, BLOCK), jnp.float32))
    rank = jnp.dot(cells, upto, precision=lax.Precision.HIGHEST)
    count = rank[:, -1]
    blocks = cells.shape[0]
    before = jnp.tril(jnp.ones((blocks, blocks), jnp.float32), -1)
    offset = jnp.dot(before, count, precision=lax.Precision.HIGHEST)
    offset = jnp.append(offset, offset[-1] + count[-1]).astype(jnp.int32)
    place = lane_of(rank.astype(jnp.int32) - 1 + offset[:-1, None])
    place = jnp.where(cells > 0.0, place, -1).astype(jnp.float32).astype(jnp.bfloat16)
    return offset, jnp.broadcast_to(place[:, None, :], (blocks, SPREAD, BLOCK))


def local(
    spectrum, sea_mask, point_index, band_counts, sub_counts, mix_in, mix_out, growth, damping
):
    freq_count, dir_count, row_count, lon_count = spectrum.shape
    comp_count = freq_count * dir_count
    all_count = growth.shape[0] * growth.shape[1]
    groups = lax.axis_size("comp")
    per_group = point_index.shape[1] // groups
    half = per_group // 2
    sizes = chunk_sizes(comp_count, (2, 3, 4))
    starts = [sum(sizes[:j]) for j in range(len(sizes))]
    out_sizes = chunk_sizes(comp_count, (7, 2))
    out_starts = [sum(out_sizes[:j]) for j in range(len(out_sizes))]

    field = spectrum.reshape(comp_count, row_count, lon_count)

    def first_edge(last):
        at = slice(row_count - NSUB, row_count) if last else slice(0, NSUB)
        mask_rows = sea_mask[at].astype(jnp.float32)
        return jnp.concatenate([field[:sizes[0], at], mask_rows[None]], axis=0)

    def later_edges(start, size, after):
        def later_edge(last):
            at = slice(row_count - NSUB, row_count) if last else slice(0, NSUB)
            return lax.optimization_barrier((field[start:start + size, at], after))[0]

        return edge_rows(later_edge, "lat")

    first_edges = edge_rows(first_edge, "lat")
    mask_low, mask_high = first_edges[0][sizes[0]], first_edges[1][sizes[0]]

    freq_index = lax.axis_index("comp") * freq_count + jnp.arange(freq_count, dtype=jnp.int32)
    scalars = (wave_speeds(freq_index, sub_counts), sub_counts, *direction_table(dir_count))
    offsets, dest = slot_table(sea_mask)
    masks = mask_planes(sea_mask, mask_low, mask_high, SUBLANES)

    done = []

    def exchange(piece):
        if done:
            piece, done[-1] = lax.optimization_barrier((piece, done[-1]))
        done.append(lax.all_to_all(piece, "comp", split_axis=0, concat_axis=0, tiled=True))
        return len(done) - 1

    def as_rows(piece):
        return piece.reshape(groups * piece.shape[1], piece.shape[2])

    chain, arrived = [], [[], []]
    for j, (start, size) in enumerate(zip(starts, sizes)):
        low, high = later_edges(start, size, chain[1]) if j > 0 else first_edges
        moved = propagate(scalars, field, low, high, masks, start, size, chain)
        pieces = 2 if j == len(sizes) - 1 else 1
        packed = gather_points(offsets, dest, moved, start, size, groups, per_group, pieces)
        chain = [moved, packed[0]]
        packed = [exchange(piece) for piece in packed]
        for h in range(2):
            arrived[h].append((packed[h % pieces], h * half if pieces == 1 else 0))

    columns = [
        column.reshape(all_count, 1)
        for column in (growth, damping, freq_weights(*growth.shape))
    ]
    back = []
    for h in range(2):
        parts_out = [comp_count] if h == 0 else out_sizes
        increments = source_terms(
            [as_rows(done[at]) for at, _ in arrived[h]], sizes, parts_out, half,
            [lane for _, lane in arrived[h]], groups, mix_in, mix_out, columns,
        )
        for rows, size in zip(increments, parts_out):
            back.append(exchange(rows.reshape(groups, size, half)))

    for start, at in zip(out_starts, back[1:]):
        moved = scatter_points(offsets, dest, moved, done[back[0]], done[at], start)
    return moved.reshape(spectrum.shape)


def solution(mesh):
    return jax.shard_map(
        local,
        mesh=mesh,
        in_specs=(
            P("comp", None, "lat", None),
            P("lat", None),
            P("lat", None),
            P("lat"),
            P("comp"),
            P(),
            P(),
            P(),
            P(),
        ),
        out_specs=P("comp", None, "lat", None),
        check_vma=False,
    )
```

```python
import functools

import jax
import jax.numpy as jnp
import numpy as np
from jax import lax
from jax.experimental import pallas as pl
from jax.experimental.pallas import tpu as pltpu
from jax.sharding import PartitionSpec as P

NSUB = 4
SUBLANES = 8
LANES = 128
BLOCK = 256
STEP_ROWS = 24
SPREAD = 16
VMEM_BYTES = 56 * 1024 * 1024


def chunk_sizes(comp_count, shares):
    if comp_count % 16:
        return [comp_count]
    units, total = comp_count // 16, sum(shares)
    bounds = [units * sum(shares[:j]) // total for j in range(len(shares) + 1)]
    return [16 * (high - low) for low, high in zip(bounds, bounds[1:]) if high > low]


def wave_speeds(freq_index, sub_steps):
    group_speed = 1.4 * jnp.power(0.93, freq_index.astype(jnp.float32))
    return group_speed / sub_steps.astype(jnp.float32)


def direction_table(dir_count):
    angles = (np.arange(dir_count, dtype=np.float32) + np.float32(0.5)) * np.float32(
        2.0 * np.pi / dir_count
    )
    return [part(angles.astype(np.float64)).astype(np.float32) for part in (np.cos, np.sin)]


def freq_weights(freq_count, dir_count):
    raw_weight = jnp.power(1.1, jnp.arange(freq_count, dtype=jnp.float32))
    raw_weight = raw_weight / (dir_count * jnp.sum(raw_weight))
    return jnp.repeat(raw_weight, dir_count)


def propagate_kernel(
    start,
    speed_ref, steps_ref, cos_ref, sin_ref,
    spec_ref, low_ref, high_ref, mask_ref,
    *refs,
):
    out_ref, keep, even, odd = refs[-4:]
    block, rows, cols = spec_ref.shape
    halo = low_ref.shape[1]
    strips = rows // SUBLANES + 2
    parts = cols // LANES
    row_id = lax.broadcasted_iota(jnp.int32, (SUBLANES, LANES), 0)
    col_id = lax.broadcasted_iota(jnp.int32, (SUBLANES, LANES), 1)

    def strip_rows(s):
        return pl.ds(s * SUBLANES, SUBLANES)

    def run(i, ax, ay, steps, x_up, y_up):
        blank = jnp.zeros((SUBLANES - halo, cols), jnp.float32)
        for s in range(strips):
            keep[strip_rows(s), :] = (
                1.0
                - ax * mask_ref[2 if x_up else 1, strip_rows(s), :]
                - ay * mask_ref[4 if y_up else 3, strip_rows(s), :]
            )
            if s == 0:
                value = jnp.concatenate([blank, low_ref[i]], axis=0)
            elif s == strips - 1:
                value = jnp.concatenate([high_ref[i], blank], axis=0)
            else:
                value = spec_ref[i, strip_rows(s - 1), :]
            even[strip_rows(s), :] = value * mask_ref[0, strip_rows(s), :]

        edge_row = row_id == (0 if y_up else SUBLANES - 1)
        edge_col = col_id == (0 if x_up else LANES - 1)
        nothing = jnp.zeros((SUBLANES, LANES), jnp.float32)

        def substep(source, target=None):
            before_y = [nothing] * parts
            for s in range(strips) if y_up else range(strips - 1, -1, -1):
                inner = 0 < s < strips - 1
                before_x = nothing
                for t in range(parts) if x_up else range(parts - 1, -1, -1):
                    at = (strip_rows(s), slice(t * LANES, (t + 1) * LANES))
                    value = source[at]
                    turned = pltpu.roll(value, 1 if y_up else SUBLANES - 1, 0)
                    upwind_y = jnp.where(edge_row, before_y[t], turned)
                    before_y[t] = turned
                    if target is None and not inner:
                        continue
                    turned = pltpu.roll(value, 1 if x_up else LANES - 1, 1)
                    upwind_x = jnp.where(edge_col, before_x, turned)
                    before_x = turned
                    moved = value * keep[at] + mask_ref[(0, *at)] * (
                        ax * upwind_x + ay * upwind_y
                    )
                    if target is None:
                        out_ref[(i, strip_rows(s - 1), at[1])] = moved
                    else:
                        target[at] = moved

        def pair(_, carry):
            substep(even, odd)
            substep(odd, even)
            return carry

        lax.fori_loop(0, (steps - 1) // 2, pair, 0)

        @pl.when(lax.rem(steps, 2) == 0)
        def _():
            substep(even, odd)
            substep(odd)

        @pl.when(lax.rem(steps, 2) == 1)
        def _():
            substep(even)

    def component(i, carry):
        at = start + pl.program_id(0) * block + i
        freq = at // cos_ref.shape[0]
        toward = at - freq * cos_ref.shape[0]
        cx, cy = speed_ref[freq] * cos_ref[toward], speed_ref[freq] * sin_ref[toward]
        steps = steps_ref[freq]
        for x_up in (True, False):
            for y_up in (True, False):

                @pl.when(((cx >= 0.0) == x_up) & ((cy >= 0.0) == y_up))
                def _():
                    run(i, cx if x_up else -cx, cy if y_up else -cy, steps, x_up, y_up)

        return carry

    lax.fori_loop(0, block, component, 0)


def propagate(scalars, spectrum, low, high, masks, start, size, chain):
    comp_count, rows, cols = spectrum.shape
    halo = low.shape[1]
    block = next(
        n for n in range(min(16, size), 0, -1)
        if size % n == 0 and start % n == 0
    )
    ext = masks.shape[1]
    cells = size * rows * cols
    return pl.pallas_call(
        functools.partial(propagate_kernel, start),
        grid_spec=pltpu.PrefetchScalarGridSpec(
            num_scalar_prefetch=4,
            grid=(size // block,),
            in_specs=[
                pl.BlockSpec((block, rows, cols), lambda g, *_: (start // block + g, 0, 0)),
                pl.BlockSpec((block, halo, cols), lambda g, *_: (g, 0, 0)),
                pl.BlockSpec((block, halo, cols), lambda g, *_: (g, 0, 0)),
                pl.BlockSpec(masks.shape, lambda g, *_: (0, 0, 0)),
            ]
            + [pl.BlockSpec(memory_space=pl.ANY) for _ in chain],
            out_specs=pl.BlockSpec((block, rows, cols), lambda g, *_: (start // block + g, 0, 0)),
            scratch_shapes=[pltpu.VMEM((ext, cols), jnp.float32) for _ in range(3)],
        ),
        out_shape=jax.ShapeDtypeStruct((comp_count, rows, cols), jnp.float32),
        input_output_aliases={8: 0} if chain else {},
        compiler_params=pltpu.CompilerParams(vmem_limit_bytes=VMEM_BYTES),
        cost_estimate=pl.CostEstimate(
            flops=cells * 30, bytes_accessed=cells * 8, transcendentals=0
        ),
        name="propagate",
    )(*scalars, spectrum, low, high, masks, *chain)


def selection(dest):
    spread = dest.shape[0]
    slot = lax.broadcasted_iota(jnp.int32, (BLOCK, BLOCK), 0)
    slot = slot.astype(jnp.float32).astype(jnp.bfloat16).reshape(BLOCK // spread, spread, BLOCK)
    one, zero = jnp.ones((), jnp.bfloat16), jnp.zeros((), jnp.bfloat16)
    return jnp.where(slot == dest[None], one, zero).reshape(BLOCK, BLOCK)


def tile_of(offset):
    return lax.shift_right_logical(offset, BLOCK.bit_length() - 1)


def lane_of(offset):
    return jnp.bitwise_and(offset, BLOCK - 1)


def tile_place(tile, per_group):
    lane = lax.rem(tile, per_group) * BLOCK
    return tile // per_group, slice(None), pl.ds(pl.multiple_of(lane, BLOCK), BLOCK)


def gather_kernel(offset_ref, field_ref, dest_ref, *refs):
    outs, (packed, rows_of, open_tile) = refs[:-3], refs[-3:]
    size, rows, cols = field_ref.shape
    blocks = cols // BLOCK
    per_group = packed.shape[2] // BLOCK
    step = pl.program_id(0)
    first_block = step * rows * blocks

    @pl.when(step == 0)
    def _():
        packed[...] = jnp.zeros_like(packed)
        open_tile[...] = jnp.zeros_like(open_tile)

    for t in range(cols // LANES):
        rows_of[t] = field_ref[:, :, t * LANES:(t + 1) * LANES].reshape(size * rows, LANES)

    lane_id = lax.broadcasted_iota(jnp.int32, (size, BLOCK), 1)
    begun = open_tile[...]
    for b in range(rows * blocks):
        r, t = b // blocks, b % blocks * (BLOCK // LANES)
        values = jnp.concatenate(
            [rows_of[t + i, pl.ds(r, size, stride=rows), :] for i in range(BLOCK // LANES)], axis=1
        ).astype(jnp.bfloat16)
        placed = lax.dot_general(
            values, selection(dest_ref[b]), (((1,), (1,)), ((), ())),
            preferred_element_type=jnp.float32,
        )
        offset, following = offset_ref[first_block + b], offset_ref[first_block + b + 1]
        full = jnp.where(lane_id >= lane_of(offset), placed, begun)
        packed[tile_place(tile_of(offset), per_group)] = full.astype(jnp.bfloat16)
        begun = jnp.where(tile_of(following) > tile_of(offset), placed, full)
    open_tile[...] = begun

    @pl.when(step == pl.num_programs(0) - 1)
    def _():
        tile = tile_of(offset_ref[first_block + rows * blocks])
        packed[tile_place(tile, per_group)] = begun.astype(jnp.bfloat16)
        groups, _, width = outs[0].shape
        for h, out in enumerate(outs):
            out[...] = packed[:groups, :, h * width:(h + 1) * width]


def gather_points(offsets, dest, field, start, size, groups, per_group, pieces):
    rows, cols = field.shape[1:]
    parts = cols // LANES
    width = per_group // pieces
    return pl.pallas_call(
        gather_kernel,
        grid_spec=pltpu.PrefetchScalarGridSpec(
            num_scalar_prefetch=1,
            grid=(rows // STEP_ROWS,),
            in_specs=[
                pl.BlockSpec(
                    (pl.Element(size), pl.Element(STEP_ROWS), pl.Element(cols)),
                    lambda g, *_: (start, g * STEP_ROWS, 0),
                ),
                pl.BlockSpec((STEP_ROWS * cols // BLOCK, *dest.shape[1:]), lambda g, *_: (g, 0, 0)),
            ],
            out_specs=[
                pl.BlockSpec((groups, size, width), lambda g, *_: (0, 0, 0))
                for _ in range(pieces)
            ],
            scratch_shapes=[
                pltpu.VMEM((groups + 1, size, per_group), jnp.bfloat16),
                pltpu.VMEM((parts, size * STEP_ROWS, LANES), jnp.float32),
                pltpu.VMEM((size, BLOCK), jnp.float32),
            ],
        ),
        out_shape=[
            jax.ShapeDtypeStruct((groups, size, width), jnp.bfloat16) for _ in range(pieces)
        ],
        compiler_params=pltpu.CompilerParams(vmem_limit_bytes=VMEM_BYTES),
        cost_estimate=pl.CostEstimate(
            flops=size * rows * cols * 2 * BLOCK,
            bytes_accessed=size * rows * cols * 6,
            transcendentals=0,
        ),
        name="gather_points",
    )(offsets, field, dest)


def scatter_kernel(offset_ref, order_ref, field_ref, dest_ref, first_ref, *refs):
    seconds, (out_ref, packed, rows_of) = refs[:-3], refs[-3:]
    size, rows, cols = field_ref.shape
    blocks = cols // BLOCK
    width = first_ref.shape[2]
    per_group = packed.shape[2] // BLOCK
    last_tile = packed.shape[0] * per_group - 1
    first_block = pl.program_id(0) * rows * blocks

    @pl.when(pl.program_id(0) == 0)
    def _():
        packed[:, :, :width] = first_ref[...]
        if len(seconds) == 1:
            packed[:, :, width:] = seconds[0][...]
        else:
            for d, second in enumerate(seconds):
                packed[jnp.bitwise_xor(order_ref[0], d), :, width:] = second[...]

    lane_id = lax.broadcasted_iota(jnp.int32, (size, BLOCK), 1)
    lane_id = lane_id.astype(jnp.float32).astype(jnp.bfloat16)
    for b in range(rows * blocks):
        r, t = b // blocks, b % blocks * (BLOCK // LANES)
        offset = offset_ref[first_block + b]
        tile = jnp.minimum(tile_of(offset), last_tile)
        following = jnp.minimum(tile + 1, last_tile)
        values = jnp.where(
            lane_id >= lane_of(offset).astype(jnp.float32).astype(jnp.bfloat16),
            packed[tile_place(tile, per_group)],
            packed[tile_place(following, per_group)],
        )
        found = jnp.dot(
            values, selection(dest_ref[b]), preferred_element_type=jnp.float32
        )
        for i in range(BLOCK // LANES):
            rows_of[t + i, pl.ds(r, size, stride=rows), :] = found[:, i * LANES:(i + 1) * LANES]
    for t in range(cols // LANES):
        at = (slice(None), slice(None), slice(t * LANES, (t + 1) * LANES))
        out_ref[at] = field_ref[at] + rows_of[t].reshape(size, rows, LANES)


def scatter_points(offsets, order, dest, field, first, second, start):
    groups, width = first.shape[0], first.shape[2]
    seconds = second if isinstance(second, list) else [second]
    size = seconds[0].shape[-2]
    rows, cols = field.shape[1:]
    parts = cols // LANES
    field_spec = pl.BlockSpec(
        (pl.Element(size), pl.Element(STEP_ROWS), pl.Element(cols)),
        lambda g, *_: (start, g * STEP_ROWS, 0),
    )
    return pl.pallas_call(
        scatter_kernel,
        grid_spec=pltpu.PrefetchScalarGridSpec(
            num_scalar_prefetch=2,
            grid=(rows // STEP_ROWS,),
            in_specs=[
                field_spec,
                pl.BlockSpec((STEP_ROWS * cols // BLOCK, *dest.shape[1:]), lambda g, *_: (g, 0, 0)),
                pl.BlockSpec(
                    (pl.Element(groups), pl.Element(size), pl.Element(width)),
                    lambda g, *_: (0, start, 0),
                    pipeline_mode=pl.Buffered(1),
                ),
            ]
            + [
                pl.BlockSpec(
                    array.shape, lambda g, *_, zeros=(0,) * array.ndim: zeros,
                    pipeline_mode=pl.Buffered(1),
                )
                for array in seconds
            ],
            out_specs=field_spec,
            scratch_shapes=[
                pltpu.VMEM((groups, size, 2 * width), jnp.bfloat16),
                pltpu.VMEM((parts, size * STEP_ROWS, LANES), jnp.float32),
            ],
        ),
        out_shape=jax.ShapeDtypeStruct(field.shape, jnp.float32),
        input_output_aliases={2: 0},
        compiler_params=pltpu.CompilerParams(vmem_limit_bytes=VMEM_BYTES),
        cost_estimate=pl.CostEstimate(
            flops=size * rows * cols * 2 * BLOCK,
            bytes_accessed=size * rows * cols * 10,
            transcendentals=0,
        ),
        name="scatter_points",
    )(offsets, order, field, dest, first, *seconds)


def source_kernel(
    counts, out_counts, split, groups, order_ref, mix_in, mix_out, growth, damping, weight, *refs
):
    ins, outs, (points, result) = refs[:len(counts)], refs[len(counts):-2], refs[-2:]
    total = sum(counts)
    for g in range(groups):
        at = g * total
        for ref, count in zip(ins, counts):
            points[at:at + count, :] = ref[g * count:(g + 1) * count, :]
            at += count
    rounded = points[...]
    hidden = jnp.dot(mix_in[...], rounded, preferred_element_type=jnp.float32)
    square = (hidden * hidden).astype(jnp.bfloat16)
    transfer = jnp.dot(mix_out[...], square, preferred_element_type=jnp.float32)
    energy = rounded.astype(jnp.float32)
    mean_energy = jnp.sum(weight[...] * energy, axis=0, keepdims=True)
    increment = 0.5 * (
        growth[...] * energy
        + 0.25 * transfer
        - damping[...] * energy * (mean_energy / (1.0 + mean_energy))
    )
    increment = increment.astype(jnp.bfloat16)
    if split:
        result[...] = increment
        for d, ref in enumerate(outs[:groups]):
            at = jnp.bitwise_xor(order_ref[0], d) * total
            ref[...] = result[pl.ds(pl.multiple_of(at, 16), out_counts[0]), :]
        outs = [None, *outs[groups:]]
    for g in range(groups):
        at = g * total
        for ref, count in zip(outs, out_counts):
            if ref is not None:
                ref[g * count:(g + 1) * count, :] = increment[at:at + count, :]
            at += count


def source_terms(
    order, pieces, counts, out_counts, split, slots, starts, groups, mix_in, mix_out, columns
):
    comp_count = mix_in.shape[0]
    width = min(512, slots)
    fixed = lambda g, *_: (0, 0)
    if len(counts) == 1:
        counts, out_counts, groups = [comp_count], [comp_count], 1

    def moving(start):
        return lambda g, *_: (0, start // width + g)

    shapes = [groups * count for count in out_counts]
    if split:
        shapes[:1] = [out_counts[0]] * groups
    return pl.pallas_call(
        functools.partial(source_kernel, counts, out_counts, split, groups),
        grid_spec=pltpu.PrefetchScalarGridSpec(
            num_scalar_prefetch=1,
            grid=(slots // width,),
            in_specs=[pl.BlockSpec(mix_in.shape, fixed)] * 2
            + [pl.BlockSpec((comp_count, 1), fixed)] * 3
            + [
                pl.BlockSpec((groups * count, width), moving(start))
                for count, start in zip(counts, starts)
            ],
            out_specs=[pl.BlockSpec((rows, width), moving(0)) for rows in shapes],
            scratch_shapes=[pltpu.VMEM((comp_count, width), jnp.bfloat16)] * 2,
        ),
        out_shape=[jax.ShapeDtypeStruct((rows, slots), jnp.bfloat16) for rows in shapes],
        compiler_params=pltpu.CompilerParams(vmem_limit_bytes=VMEM_BYTES),
        cost_estimate=pl.CostEstimate(
            flops=4 * comp_count * comp_count * slots,
            bytes_accessed=4 * comp_count * (comp_count + slots),
            transcendentals=0,
        ),
        name="source_terms",
    )(order, mix_in, mix_out, *columns, *pieces)


def edge_rows(make, axis):
    count = lax.axis_size(axis)
    forward = [(i, i + 1) for i in range(count - 1)]
    backward = [(target, source) for source, target in forward]
    return lax.ppermute(make(True), axis, forward), lax.ppermute(make(False), axis, backward)


def mask_planes(sea_mask, low, high, strip):
    blank = jnp.zeros((strip - low.shape[0], sea_mask.shape[1]), jnp.float32)
    inner = sea_mask.astype(jnp.float32)
    mask = jnp.concatenate([blank, low, inner, high, blank], axis=0)
    row = jnp.zeros_like(mask[:1])
    col = jnp.zeros_like(mask[:, :1])
    left = jnp.concatenate([col, mask[:, :-1]], axis=1)
    right = jnp.concatenate([mask[:, 1:], col], axis=1)
    above = jnp.concatenate([row, mask[:-1]], axis=0)
    below = jnp.concatenate([mask[1:], row], axis=0)
    return jnp.stack([mask, left, right, above, below])


def slot_table(sea_mask):
    cells = sea_mask.reshape(-1, BLOCK).astype(jnp.float32)
    upto = jnp.triu(jnp.ones((BLOCK, BLOCK), jnp.float32))
    rank = jnp.dot(cells, upto, precision=lax.Precision.HIGHEST)
    count = rank[:, -1]
    blocks = cells.shape[0]
    before = jnp.tril(jnp.ones((blocks, blocks), jnp.float32), -1)
    offset = jnp.dot(before, count, precision=lax.Precision.HIGHEST)
    offset = jnp.append(offset, offset[-1] + count[-1]).astype(jnp.int32)
    place = lane_of(rank.astype(jnp.int32) - 1 + offset[:-1, None])
    place = jnp.where(cells > 0.0, place, -1).astype(jnp.float32).astype(jnp.bfloat16)
    return offset, jnp.broadcast_to(place[:, None, :], (blocks, SPREAD, BLOCK))


def local(
    spectrum, sea_mask, point_index, band_counts, sub_counts, mix_in, mix_out, growth, damping
):
    freq_count, dir_count, row_count, lon_count = spectrum.shape
    comp_count = freq_count * dir_count
    all_count = growth.shape[0] * growth.shape[1]
    groups = lax.axis_size("comp")
    per_group = point_index.shape[1] // groups
    half = per_group // 2
    sizes = chunk_sizes(comp_count, (2, 3, 4))
    starts = [sum(sizes[:j]) for j in range(len(sizes))]
    out_sizes = chunk_sizes(comp_count, (7, 2))
    out_starts = [sum(out_sizes[:j]) for j in range(len(out_sizes))]

    field = spectrum.reshape(comp_count, row_count, lon_count)

    def first_edge(last):
        at = slice(row_count - NSUB, row_count) if last else slice(0, NSUB)
        mask_rows = sea_mask[at].astype(jnp.float32)
        return jnp.concatenate([field[:sizes[0], at], mask_rows[None]], axis=0)

    def later_edges(start, size, after):
        def later_edge(last):
            at = slice(row_count - NSUB, row_count) if last else slice(0, NSUB)
            return lax.optimization_barrier((field[start:start + size, at], after))[0]

        return edge_rows(later_edge, "lat")

    first_edges = edge_rows(first_edge, "lat")
    mask_low, mask_high = first_edges[0][sizes[0]], first_edges[1][sizes[0]]

    freq_index = lax.axis_index("comp") * freq_count + jnp.arange(freq_count, dtype=jnp.int32)
    scalars = (wave_speeds(freq_index, sub_counts), sub_counts, *direction_table(dir_count))
    offsets, dest = slot_table(sea_mask)
    masks = mask_planes(sea_mask, mask_low, mask_high, SUBLANES)

    done = []

    def exchange(piece):
        if done:
            piece, done[-1] = lax.optimization_barrier((piece, done[-1]))
        done.append(lax.all_to_all(piece, "comp", split_axis=0, concat_axis=0, tiled=True))
        return len(done) - 1

    def as_rows(piece):
        return piece.reshape(groups * piece.shape[1], piece.shape[2])

    chain, arrived = [], [[], []]
    for j, (start, size) in enumerate(zip(starts, sizes)):
        low, high = later_edges(start, size, chain[1]) if j > 0 else first_edges
        moved = propagate(scalars, field, low, high, masks, start, size, chain)
        pieces = 2 if j == len(sizes) - 1 else 1
        packed = gather_points(offsets, dest, moved, start, size, groups, per_group, pieces)
        chain = [moved, packed[0]]
        packed = [exchange(piece) for piece in packed]
        for h in range(2):
            arrived[h].append((packed[h % pieces], h * half if pieces == 1 else 0))

    columns = [
        column.reshape(all_count, 1)
        for column in (growth, damping, freq_weights(*growth.shape))
    ]
    order = lax.axis_index("comp").reshape(1)
    split = len(out_sizes) > 1 and groups & (groups - 1) == 0
    back = []
    for h in range(2):
        parts_out = [comp_count] if h == 0 else out_sizes
        increments = source_terms(
            order, [as_rows(done[at]) for at, _ in arrived[h]], sizes, parts_out, split and h == 1,
            half, [lane for _, lane in arrived[h]], groups, mix_in, mix_out, columns,
        )
        if split and h == 1:
            back.append([
                rows if d == 0
                else lax.ppermute(rows, "comp", [(i, i ^ d) for i in range(groups)])
                for d, rows in enumerate(increments[:groups])
            ])
            increments, parts_out = increments[groups:], parts_out[1:]
        for rows, size in zip(increments, parts_out):
            back.append(exchange(rows.reshape(groups, size, half)))

    for start, at in zip(out_starts, back[1:]):
        second = at if isinstance(at, list) else done[at]
        moved = scatter_points(offsets, order, dest, moved, done[back[0]], second, start)
    return moved.reshape(spectrum.shape)


def solution(mesh):
    return jax.shard_map(
        local,
        mesh=mesh,
        in_specs=(
            P("comp", None, "lat", None),
            P("lat", None),
            P("lat", None),
            P("lat"),
            P("comp"),
            P(),
            P(),
            P(),
            P(),
        ),
        out_specs=P("comp", None, "lat", None),
        check_vma=False,
    )
```

```python
import functools

import jax
import jax.numpy as jnp
import numpy as np
from jax import lax
from jax.experimental import pallas as pl
from jax.experimental.pallas import tpu as pltpu
from jax.sharding import PartitionSpec as P

NSUB = 4
SUBLANES = 8
LANES = 128
BLOCK = 256
STEP_ROWS = 24
VMEM_BYTES = 56 * 1024 * 1024


def chunk_sizes(comp_count, shares):
    if comp_count % 16:
        return [comp_count]
    units, total = comp_count // 16, sum(shares)
    bounds = [units * sum(shares[:j]) // total for j in range(len(shares) + 1)]
    return [16 * (high - low) for low, high in zip(bounds, bounds[1:]) if high > low]


def wave_speeds(freq_index, sub_steps):
    group_speed = 1.4 * jnp.power(0.93, freq_index.astype(jnp.float32))
    return group_speed / sub_steps.astype(jnp.float32)


def direction_table(dir_count):
    angles = (np.arange(dir_count, dtype=np.float32) + np.float32(0.5)) * np.float32(
        2.0 * np.pi / dir_count
    )
    return [part(angles.astype(np.float64)).astype(np.float32) for part in (np.cos, np.sin)]


def freq_weights(freq_count, dir_count):
    raw_weight = jnp.power(1.1, jnp.arange(freq_count, dtype=jnp.float32))
    raw_weight = raw_weight / (dir_count * jnp.sum(raw_weight))
    return jnp.repeat(raw_weight, dir_count)


def propagate_kernel(
    start,
    speed_ref, steps_ref, cos_ref, sin_ref,
    spec_ref, low_ref, high_ref, mask_ref,
    *refs,
):
    out_ref, keep, even, odd = refs[-4:]
    block, rows, cols = spec_ref.shape
    halo = low_ref.shape[1]
    strips = rows // SUBLANES + 2
    parts = cols // LANES
    row_id = lax.broadcasted_iota(jnp.int32, (SUBLANES, LANES), 0)
    col_id = lax.broadcasted_iota(jnp.int32, (SUBLANES, LANES), 1)

    def strip_rows(s):
        return pl.ds(s * SUBLANES, SUBLANES)

    def run(i, ax, ay, steps, x_up, y_up):
        blank = jnp.zeros((SUBLANES - halo, cols), jnp.float32)
        for s in range(strips):
            keep[strip_rows(s), :] = (
                1.0
                - ax * mask_ref[2 if x_up else 1, strip_rows(s), :]
                - ay * mask_ref[4 if y_up else 3, strip_rows(s), :]
            )
            if s == 0:
                value = jnp.concatenate([blank, low_ref[i]], axis=0)
            elif s == strips - 1:
                value = jnp.concatenate([high_ref[i], blank], axis=0)
            else:
                value = spec_ref[i, strip_rows(s - 1), :]
            even[strip_rows(s), :] = value * mask_ref[0, strip_rows(s), :]

        edge_row = row_id == (0 if y_up else SUBLANES - 1)
        edge_col = col_id == (0 if x_up else LANES - 1)
        nothing = jnp.zeros((SUBLANES, LANES), jnp.float32)

        def substep(source, target=None):
            before_y = [nothing] * parts
            for s in range(strips) if y_up else range(strips - 1, -1, -1):
                inner = 0 < s < strips - 1
                before_x = nothing
                for t in range(parts) if x_up else range(parts - 1, -1, -1):
                    at = (strip_rows(s), slice(t * LANES, (t + 1) * LANES))
                    value = source[at]
                    turned = pltpu.roll(value, 1 if y_up else SUBLANES - 1, 0)
                    upwind_y = jnp.where(edge_row, before_y[t], turned)
                    before_y[t] = turned
                    if target is None and not inner:
                        continue
                    turned = pltpu.roll(value, 1 if x_up else LANES - 1, 1)
                    upwind_x = jnp.where(edge_col, before_x, turned)
                    before_x = turned
                    moved = value * keep[at] + mask_ref[(0, *at)] * (
                        ax * upwind_x + ay * upwind_y
                    )
                    if target is None:
                        out_ref[(i, strip_rows(s - 1), at[1])] = moved
                    else:
                        target[at] = moved

        def pair(_, carry):
            substep(even, odd)
            substep(odd, even)
            return carry

        lax.fori_loop(0, (steps - 1) // 2, pair, 0)

        @pl.when(lax.rem(steps, 2) == 0)
        def _():
            substep(even, odd)
            substep(odd)

        @pl.when(lax.rem(steps, 2) == 1)
        def _():
            substep(even)

    def component(i, carry):
        at = start + pl.program_id(0) * block + i
        freq = at // cos_ref.shape[0]
        toward = at - freq * cos_ref.shape[0]
        cx, cy = speed_ref[freq] * cos_ref[toward], speed_ref[freq] * sin_ref[toward]
        steps = steps_ref[freq]
        for x_up in (True, False):
            for y_up in (True, False):

                @pl.when(((cx >= 0.0) == x_up) & ((cy >= 0.0) == y_up))
                def _():
                    run(i, cx if x_up else -cx, cy if y_up else -cy, steps, x_up, y_up)

        return carry

    lax.fori_loop(0, block, component, 0)


def propagate(scalars, spectrum, low, high, masks, start, size, low_start, chain):
    comp_count, rows, cols = spectrum.shape
    halo = low.shape[1]
    block = next(
        n for n in range(min(16, size), 0, -1)
        if size % n == 0 and start % n == 0 and low_start % n == 0
    )
    ext = masks.shape[1]
    cells = size * rows * cols
    return pl.pallas_call(
        functools.partial(propagate_kernel, start),
        grid_spec=pltpu.PrefetchScalarGridSpec(
            num_scalar_prefetch=4,
            grid=(size // block,),
            in_specs=[
                pl.BlockSpec((block, rows, cols), lambda g, *_: (start // block + g, 0, 0)),
                pl.BlockSpec((block, halo, cols), lambda g, *_: (low_start // block + g, 0, 0)),
                pl.BlockSpec((block, halo, cols), lambda g, *_: (low_start // block + g, 0, 0)),
                pl.BlockSpec(masks.shape, lambda g, *_: (0, 0, 0)),
            ]
            + [pl.BlockSpec(memory_space=pl.ANY) for _ in chain],
            out_specs=pl.BlockSpec((block, rows, cols), lambda g, *_: (start // block + g, 0, 0)),
            scratch_shapes=[pltpu.VMEM((ext, cols), jnp.float32) for _ in range(3)],
        ),
        out_shape=jax.ShapeDtypeStruct((comp_count, rows, cols), jnp.float32),
        input_output_aliases={8: 0} if chain else {},
        compiler_params=pltpu.CompilerParams(vmem_limit_bytes=VMEM_BYTES),
        cost_estimate=pl.CostEstimate(
            flops=cells * 30, bytes_accessed=cells * 8, transcendentals=0
        ),
        name="propagate",
    )(*scalars, spectrum, low, high, masks, *chain)


def selection(dest_row):
    slot = lax.broadcasted_iota(jnp.int32, (BLOCK, BLOCK), 0)
    slot = slot.astype(jnp.float32).astype(jnp.bfloat16)
    one, zero = jnp.ones((), jnp.bfloat16), jnp.zeros((), jnp.bfloat16)
    return jnp.where(slot == dest_row.astype(jnp.float32).astype(jnp.bfloat16), one, zero)


def tile_of(offset):
    return lax.shift_right_logical(offset, BLOCK.bit_length() - 1)


def lane_of(offset):
    return jnp.bitwise_and(offset, BLOCK - 1)


def tile_place(tile, per_group):
    lane = lax.rem(tile, per_group) * BLOCK
    return tile // per_group, slice(None), pl.ds(pl.multiple_of(lane, BLOCK), BLOCK)


def gather_kernel(offset_ref, field_ref, dest_ref, *refs):
    outs, (packed, rows_of, open_tile) = refs[:-3], refs[-3:]
    size, rows, cols = field_ref.shape
    blocks = cols // BLOCK
    per_group = packed.shape[2] // BLOCK
    step = pl.program_id(0)
    first_block = step * rows * blocks

    @pl.when(step == 0)
    def _():
        packed[...] = jnp.zeros_like(packed)
        open_tile[...] = jnp.zeros_like(open_tile)

    for t in range(cols // LANES):
        rows_of[t] = field_ref[:, :, t * LANES:(t + 1) * LANES].reshape(size * rows, LANES)

    lane_id = lax.broadcasted_iota(jnp.int32, (size, BLOCK), 1)
    begun = open_tile[...]
    for b in range(rows * blocks):
        r, t = b // blocks, b % blocks * (BLOCK // LANES)
        values = jnp.concatenate(
            [rows_of[t + i, pl.ds(r, size, stride=rows), :] for i in range(BLOCK // LANES)], axis=1
        ).astype(jnp.bfloat16)
        placed = lax.dot_general(
            values, selection(dest_ref[pl.ds(b, 1), :]), (((1,), (1,)), ((), ())),
            preferred_element_type=jnp.float32,
        )
        offset, following = offset_ref[first_block + b], offset_ref[first_block + b + 1]
        full = jnp.where(lane_id >= lane_of(offset), placed, begun)
        packed[tile_place(tile_of(offset), per_group)] = full.astype(jnp.bfloat16)
        begun = jnp.where(tile_of(following) > tile_of(offset), placed, full)
    open_tile[...] = begun

    @pl.when(step == pl.num_programs(0) - 1)
    def _():
        tile = tile_of(offset_ref[first_block + rows * blocks])
        packed[tile_place(tile, per_group)] = begun.astype(jnp.bfloat16)
        groups, _, width = outs[0].shape
        for h, out in enumerate(outs):
            out[...] = packed[:groups, :, h * width:(h + 1) * width]


def gather_points(offsets, dest, field, start, size, groups, per_group, pieces):
    rows, cols = field.shape[1:]
    parts = cols // LANES
    width = per_group // pieces
    return pl.pallas_call(
        gather_kernel,
        grid_spec=pltpu.PrefetchScalarGridSpec(
            num_scalar_prefetch=1,
            grid=(rows // STEP_ROWS,),
            in_specs=[
                pl.BlockSpec(
                    (pl.Element(size), pl.Element(STEP_ROWS), pl.Element(cols)),
                    lambda g, *_: (start, g * STEP_ROWS, 0),
                ),
                pl.BlockSpec((STEP_ROWS * cols // BLOCK, BLOCK), lambda g, *_: (g, 0)),
            ],
            out_specs=[
                pl.BlockSpec((groups, size, width), lambda g, *_: (0, 0, 0))
                for _ in range(pieces)
            ],
            scratch_shapes=[
                pltpu.VMEM((groups + 1, size, per_group), jnp.bfloat16),
                pltpu.VMEM((parts, size * STEP_ROWS, LANES), jnp.float32),
                pltpu.VMEM((size, BLOCK), jnp.float32),
            ],
        ),
        out_shape=[
            jax.ShapeDtypeStruct((groups, size, width), jnp.bfloat16) for _ in range(pieces)
        ],
        compiler_params=pltpu.CompilerParams(vmem_limit_bytes=VMEM_BYTES),
        cost_estimate=pl.CostEstimate(
            flops=size * rows * cols * 2 * BLOCK,
            bytes_accessed=size * rows * cols * 6,
            transcendentals=0,
        ),
        name="gather_points",
    )(offsets, field, dest)


def scatter_kernel(offset_ref, field_ref, dest_ref, first_ref, second_ref, *refs):
    out_ref, packed, rows_of = refs[-3:]
    size, rows, cols = field_ref.shape
    blocks = cols // BLOCK
    width = first_ref.shape[2]
    per_group = packed.shape[2] // BLOCK
    last_tile = packed.shape[0] * per_group - 1
    first_block = pl.program_id(0) * rows * blocks

    @pl.when(pl.program_id(0) == 0)
    def _():
        packed[:, :, :width] = first_ref[...]
        packed[:, :, width:] = second_ref[...]

    lane_id = lax.broadcasted_iota(jnp.int32, (size, BLOCK), 1)
    lane_id = lane_id.astype(jnp.float32).astype(jnp.bfloat16)
    for b in range(rows * blocks):
        r, t = b // blocks, b % blocks * (BLOCK // LANES)
        offset = offset_ref[first_block + b]
        tile = jnp.minimum(tile_of(offset), last_tile)
        following = jnp.minimum(tile + 1, last_tile)
        values = jnp.where(
            lane_id >= lane_of(offset).astype(jnp.float32).astype(jnp.bfloat16),
            packed[tile_place(tile, per_group)],
            packed[tile_place(following, per_group)],
        )
        found = jnp.dot(
            values, selection(dest_ref[pl.ds(b, 1), :]), preferred_element_type=jnp.float32
        )
        for i in range(BLOCK // LANES):
            rows_of[t + i, pl.ds(r, size, stride=rows), :] = found[:, i * LANES:(i + 1) * LANES]
    for t in range(cols // LANES):
        at = (slice(None), slice(None), slice(t * LANES, (t + 1) * LANES))
        out_ref[at] = field_ref[at] + rows_of[t].reshape(size, rows, LANES)


def scatter_points(offsets, dest, field, first, second, start):
    groups, size, width = second.shape
    rows, cols = field.shape[1:]
    parts = cols // LANES
    field_spec = pl.BlockSpec(
        (pl.Element(size), pl.Element(STEP_ROWS), pl.Element(cols)),
        lambda g, *_: (start, g * STEP_ROWS, 0),
    )
    return pl.pallas_call(
        scatter_kernel,
        grid_spec=pltpu.PrefetchScalarGridSpec(
            num_scalar_prefetch=1,
            grid=(rows // STEP_ROWS,),
            in_specs=[
                field_spec,
                pl.BlockSpec((STEP_ROWS * cols // BLOCK, BLOCK), lambda g, *_: (g, 0)),
                pl.BlockSpec(
                    (pl.Element(groups), pl.Element(size), pl.Element(width)),
                    lambda g, *_: (0, start, 0),
                    pipeline_mode=pl.Buffered(1),
                ),
                pl.BlockSpec(
                    (groups, size, width), lambda g, *_: (0, 0, 0), pipeline_mode=pl.Buffered(1)
                ),
            ],
            out_specs=field_spec,
            scratch_shapes=[
                pltpu.VMEM((groups, size, 2 * width), jnp.bfloat16),
                pltpu.VMEM((parts, size * STEP_ROWS, LANES), jnp.float32),
            ],
        ),
        out_shape=jax.ShapeDtypeStruct(field.shape, jnp.float32),
        input_output_aliases={1: 0},
        compiler_params=pltpu.CompilerParams(vmem_limit_bytes=VMEM_BYTES),
        cost_estimate=pl.CostEstimate(
            flops=size * rows * cols * 2 * BLOCK,
            bytes_accessed=size * rows * cols * 10,
            transcendentals=0,
        ),
        name="scatter_points",
    )(offsets, field, dest, first, second)


def source_kernel(counts, out_counts, groups, mix_in, mix_out, growth, damping, weight, *refs):
    ins, outs, points = refs[:len(counts)], refs[len(counts):-1], refs[-1]
    total = sum(counts)
    for g in range(groups):
        at = g * total
        for ref, count in zip(ins, counts):
            points[at:at + count, :] = ref[g * count:(g + 1) * count, :]
            at += count
    rounded = points[...]
    hidden = jnp.dot(mix_in[...], rounded, preferred_element_type=jnp.float32)
    square = (hidden * hidden).astype(jnp.bfloat16)
    transfer = jnp.dot(mix_out[...], square, preferred_element_type=jnp.float32)
    energy = rounded.astype(jnp.float32)
    mean_energy = jnp.sum(weight[...] * energy, axis=0, keepdims=True)
    increment = 0.5 * (
        growth[...] * energy
        + 0.25 * transfer
        - damping[...] * energy * (mean_energy / (1.0 + mean_energy))
    )
    increment = increment.astype(jnp.bfloat16)
    for g in range(groups):
        at = g * total
        for ref, count in zip(outs, out_counts):
            ref[g * count:(g + 1) * count, :] = increment[at:at + count, :]
            at += count


def source_terms(pieces, counts, out_counts, slots, starts, groups, mix_in, mix_out, columns):
    comp_count = mix_in.shape[0]
    width = min(512, slots)
    fixed = lambda g: (0, 0)
    if len(counts) == 1:
        counts, out_counts, groups = [comp_count], [comp_count], 1

    def moving(start):
        return lambda g: (0, start // width + g)

    return pl.pallas_call(
        functools.partial(source_kernel, counts, out_counts, groups),
        grid=(slots // width,),
        in_specs=[pl.BlockSpec(mix_in.shape, fixed)] * 2
        + [pl.BlockSpec((comp_count, 1), fixed)] * 3
        + [
            pl.BlockSpec((groups * count, width), moving(start))
            for count, start in zip(counts, starts)
        ],
        out_specs=[pl.BlockSpec((groups * count, width), moving(0)) for count in out_counts],
        out_shape=[
            jax.ShapeDtypeStruct((groups * count, slots), jnp.bfloat16) for count in out_counts
        ],
        scratch_shapes=[pltpu.VMEM((comp_count, width), jnp.bfloat16)],
        compiler_params=pltpu.CompilerParams(vmem_limit_bytes=VMEM_BYTES),
        cost_estimate=pl.CostEstimate(
            flops=4 * comp_count * comp_count * slots,
            bytes_accessed=4 * comp_count * (comp_count + slots),
            transcendentals=0,
        ),
        name="source_terms",
    )(mix_in, mix_out, *columns, *pieces)


def edge_rows(make, axis):
    count = lax.axis_size(axis)
    forward = [(i, i + 1) for i in range(count - 1)]
    backward = [(target, source) for source, target in forward]
    return lax.ppermute(make(True), axis, forward), lax.ppermute(make(False), axis, backward)


def mask_planes(sea_mask, low, high, strip):
    blank = jnp.zeros((strip - low.shape[0], sea_mask.shape[1]), jnp.float32)
    inner = sea_mask.astype(jnp.float32)
    mask = jnp.concatenate([blank, low, inner, high, blank], axis=0)
    row = jnp.zeros_like(mask[:1])
    col = jnp.zeros_like(mask[:, :1])
    left = jnp.concatenate([col, mask[:, :-1]], axis=1)
    right = jnp.concatenate([mask[:, 1:], col], axis=1)
    above = jnp.concatenate([row, mask[:-1]], axis=0)
    below = jnp.concatenate([mask[1:], row], axis=0)
    return jnp.stack([mask, left, right, above, below])


def slot_table(sea_mask):
    cells = sea_mask.reshape(-1, BLOCK).astype(jnp.float32)
    upto = jnp.triu(jnp.ones((BLOCK, BLOCK), jnp.float32))
    rank = jnp.dot(cells, upto, precision=lax.Precision.HIGHEST)
    count = rank[:, -1]
    blocks = cells.shape[0]
    before = jnp.tril(jnp.ones((blocks, blocks), jnp.float32), -1)
    offset = jnp.dot(before, count, precision=lax.Precision.HIGHEST)
    offset = jnp.append(offset, offset[-1] + count[-1]).astype(jnp.int32)
    place = lane_of(rank.astype(jnp.int32) - 1 + offset[:-1, None])
    return offset, jnp.where(cells > 0.0, place, -1)


def local(
    spectrum, sea_mask, point_index, band_counts, sub_counts, mix_in, mix_out, growth, damping
):
    freq_count, dir_count, row_count, lon_count = spectrum.shape
    comp_count = freq_count * dir_count
    all_count = growth.shape[0] * growth.shape[1]
    groups = lax.axis_size("comp")
    per_group = point_index.shape[1] // groups
    half = per_group // 2
    sizes = chunk_sizes(comp_count, (2, 3, 4))
    starts = [sum(sizes[:j]) for j in range(len(sizes))]
    out_sizes = chunk_sizes(comp_count, (7, 2))
    out_starts = [sum(out_sizes[:j]) for j in range(len(out_sizes))]

    field = spectrum.reshape(comp_count, row_count, lon_count)

    ahead = sum(sizes[:2])

    def first_edge(last):
        at = slice(row_count - NSUB, row_count) if last else slice(0, NSUB)
        mask_rows = sea_mask[at].astype(jnp.float32)
        return jnp.concatenate([field[:ahead, at], mask_rows[None]], axis=0)

    def later_edges(start, size, after):
        def later_edge(last):
            at = slice(row_count - NSUB, row_count) if last else slice(0, NSUB)
            return lax.optimization_barrier((field[start:start + size, at], after))[0]

        return edge_rows(later_edge, "lat")

    first_edges = edge_rows(first_edge, "lat")
    mask_low, mask_high = first_edges[0][ahead], first_edges[1][ahead]

    freq_index = lax.axis_index("comp") * freq_count + jnp.arange(freq_count, dtype=jnp.int32)
    scalars = (wave_speeds(freq_index, sub_counts), sub_counts, *direction_table(dir_count))
    offsets, dest = slot_table(sea_mask)
    masks = mask_planes(sea_mask, mask_low, mask_high, SUBLANES)

    done = []

    def exchange(piece):
        if done:
            piece, done[-1] = lax.optimization_barrier((piece, done[-1]))
        done.append(lax.all_to_all(piece, "comp", split_axis=0, concat_axis=0, tiled=True))
        return len(done) - 1

    def as_rows(piece):
        return piece.reshape(groups * piece.shape[1], piece.shape[2])

    chain, arrived = [], [[], []]
    for j, (start, size) in enumerate(zip(starts, sizes)):
        low, high = later_edges(start, size, chain[1]) if start >= ahead else first_edges
        low_start = 0 if start >= ahead else start
        moved = propagate(scalars, field, low, high, masks, start, size, low_start, chain)
        pieces = 2 if j == len(sizes) - 1 else 1
        packed = gather_points(offsets, dest, moved, start, size, groups, per_group, pieces)
        chain = [moved, packed[0]]
        packed = [exchange(piece) for piece in packed]
        for h in range(2):
            arrived[h].append((packed[h % pieces], h * half if pieces == 1 else 0))

    columns = [
        column.reshape(all_count, 1)
        for column in (growth, damping, freq_weights(*growth.shape))
    ]
    back = []
    for h in range(2):
        parts_out = [comp_count] if h == 0 else out_sizes
        increments = source_terms(
            [as_rows(done[at]) for at, _ in arrived[h]], sizes, parts_out, half,
            [lane for _, lane in arrived[h]], groups, mix_in, mix_out, columns,
        )
        for rows, size in zip(increments, parts_out):
            back.append(exchange(rows.reshape(groups, size, half)))

    for start, at in zip(out_starts, back[1:]):
        moved = scatter_points(offsets, dest, moved, done[back[0]], done[at], start)
    return moved.reshape(spectrum.shape)


def solution(mesh):
    return jax.shard_map(
        local,
        mesh=mesh,
        in_specs=(
            P("comp", None, "lat", None),
            P("lat", None),
            P("lat", None),
            P("lat"),
            P("comp"),
            P(),
            P(),
            P(),
            P(),
        ),
        out_specs=P("comp", None, "lat", None),
        check_vma=False,
    )
```
